32 devices in a mesh: band: 4 (over y, core), sub: 8 (over z, x).
Axes of the slice: x: 2, y: 2, z: 4, core: 2. Of those that a mesh axis runs over, the one named last changes fastest.
Arguments:
- background: float32 [8, 4, 768, 1536], P('band', None, 'sub'), may hold values from -18 to 18
- obs_columns: float32 [8, 4, 32768], P('band', None, 'sub'), may hold values from -18 to 18
- obs_owner: int32 [32768, 1], P('sub'), may hold values from 0 to 7; in each aligned block of 4096 rows (0 to 4095, 4096 to 8191, ...) at most 1024 rows name the same one
- obs_cell: int32 [32768], P('sub'), may hold values from 0 to 147455
- lat_length: float32 [8, 4, 768], P('band'), may hold values from 1 to 2200
- lon_length: float32 [8, 4], P('band'), may hold values from 2 to 48
- vert_length: float32 [8, 4], P('band'), may hold values from 1 to 720
Outputs:
- filtered: float32 [8, 4, 768, 1536], P('band', None, 'sub')
The draws below stay inside these ranges and needn't reach their ends.
Inputs may be any that keep to these rules, and one draw needn't show every extreme that they name: `obs_owner`: among the 4096 observations of one device no subdomain is named more than 1024 times, and in every draw some device names some subdomain exactly 1024 times.
All inputs are finite; a program needn't handle non-finite values.
Results may differ from the reference program's by a relative error of at most 0.0003.
Values sent between devices are 32-bit elements; how exact they have to be, the bound alone decides.
No kernel may reach another device: no remote copies, remote signals or barrier semaphores. Data moves between devices by JAX's collectives and lax.ppermute only.
A program may use at most 128 MiB of HBM per device.

```python
import math
import jax
import jax.numpy as jnp
import numpy as np
from jax import lax

VARIABLE_TOTAL = 4
LATITUDE_ROWS = 768
NLON = 1536
OBS_DEV = 4096
LEVEL_TOTAL = 8
NOBS = 32768
CAP = 1024
N_SUB = 8


def draw_background(key, part):
    jagged_key = jax.random.fold_in(jax.random.fold_in(key, 17), 0)
    return 3.0 * jax.random.truncated_normal(jagged_key, -6.0, 6.0, (LEVEL_TOTAL, VARIABLE_TOTAL, LATITUDE_ROWS, NLON), jnp.float32)


def draw_lat_length(key, part):
    root_key, jagged_key, spike_key = jax.random.split(jax.random.fold_in(key, 11), 3)
    log_base = jax.random.uniform(root_key, (LEVEL_TOTAL, VARIABLE_TOTAL, 1), jnp.float32, math.log(6.0), math.log(1536.0))
    rough = jax.random.uniform(jagged_key, (LEVEL_TOTAL, VARIABLE_TOTAL, LATITUDE_ROWS), jnp.float32, math.log(0.7), math.log(1.4))
    spike_sample = jax.random.uniform(spike_key, (2, LEVEL_TOTAL, VARIABLE_TOTAL, LATITUDE_ROWS), jnp.float32)
    spike_length = 1.5 + 1.5 * spike_sample[1]
    scale_length = jnp.exp(log_base + rough)
    return jnp.where(spike_sample[0] < 2.0 / LATITUDE_ROWS, spike_length, scale_length)


def draw_vert_length(key, part):
    sequence_key, location_key, jagged_key, spike_key = jax.random.split(jax.random.fold_in(key, 13), 4)
    ladder = jax.random.permutation(sequence_key, VARIABLE_TOTAL).astype(jnp.float32)
    spot = jax.random.uniform(location_key, (VARIABLE_TOTAL,), jnp.float32)
    share = (ladder + spot) / VARIABLE_TOTAL
    log_base = (math.log(2.0) + share * (math.log(512.0) - math.log(2.0)))[None, :]
    rough = jax.random.uniform(jagged_key, (LEVEL_TOTAL, VARIABLE_TOTAL), jnp.float32, math.log(0.7), math.log(1.4))
    spike_sample = jax.random.uniform(spike_key, (2, LEVEL_TOTAL, VARIABLE_TOTAL), jnp.float32)
    spike_length = 1.5 + 1.5 * spike_sample[1]
    scale_length = jnp.exp(log_base + rough)
    return jnp.where(spike_sample[0] < 2.0 / LEVEL_TOTAL, spike_length, scale_length)


def set_ends(entries, rng, least, top_value):
    place = [jax.random.randint(jax.random.fold_in(rng, axis), (), 0, length) for axis, length in enumerate(entries.shape)]
    main_axis = entries.shape.index(max(entries.shape))
    neighbour = place[:main_axis] + [(place[main_axis] + 1) % entries.shape[main_axis]] + place[main_axis + 1:]
    return entries.at[tuple(place)].set(least).at[tuple(neighbour)].set(top_value)


def level_of(key, shape, cuts, least, top_value):
    level, own = 1.0, jax.random.fold_in(key, 6)
    for axis_at, shards_of in cuts:
        steps = jnp.exp(jax.random.uniform(jax.random.fold_in(own, axis_at), (shards_of,), jnp.float32, least / len(cuts), top_value / len(cuts)))
        level = level * jnp.repeat(steps, shape[axis_at] // shards_of).reshape([-1 if axis == axis_at else 1 for axis in range(len(shape))])
    return level


def assign_block(stream_key, own, number, rows, count, top, limit, slope):
    ranking = jax.random.permutation(stream_key, count)
    heavy_load, common = load_shares(count, rows * top, limit, slope, True), load_shares(count, rows * top, limit, slope, False)
    places = jnp.arange(count)

    def named(lengths, offset_by):
        used = int((lengths > 0).sum())
        fixed = max(1, used // 4)
        passed = fixed + (places - fixed + offset_by * (used - fixed)) % max(1, count - fixed)
        return jnp.zeros((count,), jnp.int32).at[ranking[jnp.where(places < fixed, places, passed)]].set(jnp.asarray(lengths, jnp.int32))

    lengths = jnp.where(number % 4 == 0, named(heavy_load, number // 4), named(common, number - number // 4 - 1))
    mixed = jax.random.permutation(jax.random.fold_in(own, 3), count)
    source_of, receiver = mixed[0:count // 2 * 2:2], mixed[1:count // 2 * 2:2]
    room = jnp.minimum(lengths[source_of] - 1, limit - lengths[receiver]) // 2
    room = jnp.where((source_of == ranking[0]) | (receiver == ranking[0]) | (lengths[receiver] == 0), 0, jnp.maximum(room, 0))
    passed = jax.random.randint(jax.random.fold_in(own, 4), (count // 2,), 0, 1 << 20) % (room + 1)
    lengths = lengths.at[source_of].add(-passed).at[receiver].add(passed)
    items = jnp.searchsorted(jnp.cumsum(lengths), jnp.arange(rows * top), side="right").astype(jnp.int32)
    grid = items.reshape(top, rows).T
    grid = grid[jax.random.permutation(jax.random.fold_in(own, 1), rows)]
    offset_by = jax.random.randint(jax.random.fold_in(own, 2), (rows, 1), 0, top)
    return jnp.take_along_axis(grid, (jnp.arange(top)[None, :] + offset_by) % top, axis=1)


def load_shares(count, total, reach, skew, full):
    loads = [(1 << 20) // math.isqrt(standing ** skew) + 1 for standing in range(1, count + 1)]
    largest = reach if full else min(reach, max(-(-total // count), total * loads[0] // sum(loads)))
    least = 1 if total - largest >= count - 1 else 0
    given, spare = [largest] + [least] * (count - 1), total - largest - least * (count - 1)
    while spare > 0:
        movable = [i for i in range(1, count) if given[i] < largest] or [i for i in range(1, count) if given[i] < reach]
        mass, budget = sum([loads[i] for i in movable]), spare
        for i in movable:
            more = min(reach - given[i], max(1, budget * loads[i] // mass), spare)
            given[i] = given[i] + more
            spare = spare - more
    return np.array(given)


def noise(own_key, extent, deviation, reach, cuts=(), kind=jnp.bfloat16):
    values = jax.random.normal(own_key, extent, jnp.float32) * deviation
    if len(cuts) > 0:
        values = level_of(own_key, extent, cuts, -0.22, 0.18) * values
    return jnp.clip(values, min=-reach, max=reach).astype(kind)


def setup_inputs(seed: int = 0) -> dict:
    streams_of = jax.random.split(jax.random.key(seed), 8)
    background = draw_background(jax.random.fold_in(streams_of[7], 71), 0)
    obs_columns = noise(streams_of[1], (LEVEL_TOTAL, VARIABLE_TOTAL, NOBS), 3.0, 18.0, ((0, 4), (2, 8)), jnp.float32)
    obs_owner_keys = jax.random.split(jax.random.fold_in(streams_of[2], 1), NOBS // OBS_DEV)
    obs_owner_turns = jax.random.permutation(jax.random.fold_in(streams_of[2], 3), NOBS // OBS_DEV)
    obs_owner = jax.vmap(lambda own, number: assign_block(jax.random.fold_in(streams_of[2], 2), own, number, OBS_DEV, N_SUB, 1, CAP, 2))(obs_owner_keys, obs_owner_turns).reshape((NOBS, 1))
    obs_cell = set_ends(jax.random.randint(streams_of[3], (NOBS,), 0, LATITUDE_ROWS // N_SUB * NLON), jax.random.fold_in(streams_of[3], 1), 0, (LATITUDE_ROWS // N_SUB * NLON) - 1).astype(jnp.int32)
    lat_length = draw_lat_length(jax.random.fold_in(streams_of[7], 71), 0)
    lon_length = jnp.clip(jnp.exp(math.log(48.0) - 3.1780538 * jax.random.uniform(streams_of[5], (LEVEL_TOTAL, VARIABLE_TOTAL), jnp.float32) ** level_of(streams_of[5], (LEVEL_TOTAL, VARIABLE_TOTAL), ((0, 4),), -0.2, 0.2)), 2.0, 48.0)
    vert_length = draw_vert_length(jax.random.fold_in(streams_of[7], 71), 0)
    return {"background": background, "obs_columns": obs_columns, "obs_owner": obs_owner, "obs_cell": obs_cell, "lat_length": lat_length, "lon_length": lon_length, "vert_length": vert_length}


def decay_of(scale_length):
    return jnp.exp(-1.0 / scale_length)


def sweep(values, decays, reverse):
    def advance(carry_state, inputs):
        column, factor = inputs
        output = factor * carry_state + (1.0 - factor) * column
        return output, output

    _, result = lax.scan(advance, jnp.zeros_like(values[0]), (values, decays), reverse=reverse)
    return result


def cycle_sweep(values, decay_row, reverse):
    scale_length = values.shape[0]
    factors = jnp.broadcast_to(decay_row, (scale_length,) + decay_row.shape)
    zero_start = sweep(values, factors, reverse)
    log_decay = jnp.log(decay_row)
    powers = jnp.exp(jnp.arange(1, scale_length + 1, dtype=jnp.float32).reshape(scale_length, 1, 1) * log_decay[None])
    full_turn = 1.0 - jnp.exp(scale_length * log_decay)
    if reverse:
        wrapped = zero_start[0] / full_turn
        return zero_start + jnp.flip(powers, 0) * wrapped[None]
    wrapped = zero_start[scale_length - 1] / full_turn
    return zero_start + powers * wrapped[None]


def horizontal(level_field, lat_decay, lon_decay):
    moved = jnp.transpose(level_field, (1, 0, 2))
    lat_factors = jnp.transpose(lat_decay, (1, 0))[:, :, None]
    for reverse in (False, True, False, True):
        moved = sweep(moved, lat_factors, reverse)
    moved = jnp.transpose(moved, (2, 1, 0))
    lon_factor = lon_decay[:, None]
    for reverse in (False, True, False, True):
        moved = cycle_sweep(moved, lon_factor, reverse)
    return jnp.transpose(moved, (1, 2, 0))


def reference(background, obs_columns, obs_owner, obs_cell, lat_length, lon_length, vert_length):
    strip_cells = (LATITUDE_ROWS // N_SUB) * NLON
    grid_cell = (obs_owner[:, 0] * strip_cells + obs_cell).astype(jnp.int32)
    flat = background.reshape(LEVEL_TOTAL, VARIABLE_TOTAL, LATITUDE_ROWS * NLON)
    flat = flat.at[:, :, grid_cell].add(obs_columns)
    forced = flat.reshape(LEVEL_TOTAL, VARIABLE_TOTAL, LATITUDE_ROWS, NLON)
    lat_decay = decay_of(lat_length)
    lon_decay = decay_of(lon_length)
    vert_decay = decay_of(vert_length)

    def one_level(inputs):
        return horizontal(inputs[0], inputs[1], inputs[2])

    smoothed = lax.map(one_level, (forced, lat_decay, lon_decay))
    vert_factors = vert_decay[:, :, None, None]
    smoothed = sweep(smoothed, vert_factors, False)
    smoothed = sweep(smoothed, vert_factors, True)
    return smoothed
```

```python
import functools

import jax
import jax.numpy as jnp
from jax import lax
from jax.experimental import pallas as pl
from jax.experimental.pallas import tpu as pltpu
from jax.sharding import PartitionSpec as P

f32 = jnp.float32
i32 = jnp.int32
bf16 = jnp.bfloat16
highest = lax.Precision.HIGHEST

LANES = 128
SUBLANES = 8
BLOCK = 256
CHAINS = 4

VMEM = pl.BlockSpec(memory_space=pltpu.VMEM)
SMEM = pl.BlockSpec(memory_space=pltpu.SMEM)
ANY = pl.BlockSpec(memory_space=pl.ANY)


def params(mib):
    return pltpu.CompilerParams(vmem_limit_bytes=mib << 20)


def cost(flops, read):
    return pl.CostEstimate(flops=flops, bytes_accessed=read, transcendentals=0)


def dot(a, b, dims=(((1,), (0,)), ((), ()))):
    return lax.dot_general(a, b, dims, preferred_element_type=f32)


def split(x):
    high = x.astype(bf16)
    return high, (x - high.astype(f32)).astype(bf16)


def split_outside(x):
    high = lax.reduce_precision(x, 8, 7)
    return high.astype(bf16), (x - high).astype(bf16)


def pack_kernel(group_count, chunk_count, strip, starts, places, cells, values, packed):
    sub_count = packed.shape[0]
    lane = lax.broadcasted_iota(i32, (1, LANES), 1)
    word_row = chunk_count * group_count

    def unaligned(ref, base):
        row = lax.shift_right_logical(base, 7)
        offset = base & 127
        turn = (LANES - offset) & 127
        first = pltpu.roll(ref[pl.ds(row, 1), :], turn, 1)
        second = pltpu.roll(ref[pl.ds(row + 1, 1), :], turn, 1)
        return jnp.where(lane < LANES - offset, first, second)

    def one_owner(owner, carry):
        start = starts[owner]
        count = starts[owner + 1] - start
        word_rows = packed.shape[1] - word_row
        packed[owner, word_row:, :] = jnp.full((word_rows, LANES), float(strip), f32)

        def one_chunk(chunk, carry):
            base = start + chunk * LANES
            place = jnp.broadcast_to(unaligned(places, base), (SUBLANES, LANES))
            source = lax.shift_right_logical(place, 7)
            within = place & 127
            for tile in range(group_count // SUBLANES):
                rows = slice(tile * SUBLANES, (tile + 1) * SUBLANES)
                total = jnp.zeros((SUBLANES, LANES), f32)
                for column in range(values.shape[1] // LANES):
                    block = values[rows, column * LANES : (column + 1) * LANES]
                    total = jnp.where(
                        source == column, jnp.take_along_axis(block, within, axis=1), total
                    )
                at = pl.multiple_of(chunk * group_count + tile * SUBLANES, SUBLANES)
                packed[owner, pl.ds(at, SUBLANES), :] = total
            cell = unaligned(cells, base)
            word = (cell - (cell & 127)) + ((cell - lane) & 127)
            word = jnp.where(lane + chunk * LANES < count, word, strip)
            packed[owner, pl.ds(word_row + chunk, 1), :] = word.astype(f32)
            return carry

        lax.fori_loop(0, (count + LANES - 1) // LANES, one_chunk, 0)
        return carry

    lax.fori_loop(0, sub_count, one_owner, 0)


def pack_observations(obs_values, owners, cells, sub_count, strip, capacity):
    group_count, obs_count = obs_values.shape
    chunk_count = capacity // LANES
    rows = chunk_count * group_count + SUBLANES * (-(-chunk_count // SUBLANES))
    keys, places = lax.sort(
        (owners * strip + cells, lax.iota(i32, obs_count)), num_keys=1, is_stable=False
    )
    bounds = jnp.arange(sub_count + 1, dtype=i32)
    starts = jnp.sum((owners[:, None] < bounds[None, :]).astype(i32), axis=0)
    pad = (0, SUBLANES * LANES)
    places = jnp.pad(places, pad).reshape(-1, LANES)
    cells = jnp.pad(keys % strip, pad).reshape(-1, LANES)
    return pl.pallas_call(
        functools.partial(pack_kernel, group_count, chunk_count, strip),
        out_shape=jax.ShapeDtypeStruct((sub_count, rows, LANES), f32),
        in_specs=[SMEM, VMEM, VMEM, VMEM],
        out_specs=VMEM,
        compiler_params=params(16),
        cost_estimate=cost(10**6, 10**6),
    )(starts, places, cells, obs_values)


def deposit_kernel(sizes, words, got, field, decay, swept, exits, loaded, *rest):
    sub_count, group_count, row_count, column_count, chunk_count, strip = sizes
    totals, sems = rest[:CHAINS], rest[CHAINS]
    tiles = group_count // SUBLANES
    span = (chunk_count + 1) * LANES

    def load(column):
        return pltpu.make_async_copy(
            field.at[:, pl.ds(column * LANES, LANES)], loaded.at[column], sems.at[column]
        )

    for column in range(column_count):
        load(column).start()

    def clear(at, carry):
        for total in totals:
            for tile in range(tiles):
                for k in range(8):
                    total[tile, at * 8 + k] = jnp.zeros((SUBLANES, LANES), f32)
        return carry

    lax.fori_loop(0, row_count * column_count // 8, clear, 0)
    lane = lax.broadcasted_iota(i32, (SUBLANES, LANES), 1)

    def one_source(source, carry):
        first = source * span

        def more(chunk):
            return words[first + chunk * LANES] < strip

        def one_chunk(chunk):
            start = first + chunk * LANES
            blocks = [
                got[
                    source,
                    pl.ds(pl.multiple_of(chunk * group_count + tile * SUBLANES, 8), SUBLANES),
                    :,
                ]
                for tile in range(tiles)
            ]
            for slot in range(LANES):
                word = words[start + slot]
                target = lax.shift_right_logical(word, 7)
                turn = word & 127
                for tile in range(tiles):
                    value = pltpu.roll(jnp.where(lane == slot, blocks[tile], 0.0), turn, 1)
                    total = totals[slot % CHAINS]
                    total[tile, target] = total[tile, target] + value
            return chunk + 1

        lax.while_loop(more, one_chunk, jnp.int32(0))
        return carry

    lax.fori_loop(0, sub_count, one_source, 0)
    for column in range(column_count):
        load(column).wait()

    for tile in range(tiles):
        held = totals[0]
        spot = tile * SUBLANES * row_count

        def read_first(row, column):
            at = row * column_count + column
            value = loaded[column, pl.ds(spot + row, SUBLANES, stride=row_count), :]
            for total in totals:
                value = value + total[tile, at]
            return value

        def read_held(row, column):
            return held[tile, row * column_count + column]

        def write_held(row, column, value):
            held[tile, row * column_count + column] = value

        def write_last(row, column, value):
            swept[column, pl.ds(spot + row, SUBLANES, stride=row_count), :] = value

        for turn in range(4):
            read = read_first if turn == 0 else read_held
            write = write_last if turn == 3 else write_held

            def one_row(step, state, turn=turn, read=read, write=write):
                row = row_count - 1 - step if turn % 2 else step
                keep = decay[row, tile * SUBLANES : (tile + 1) * SUBLANES, :]
                take = 1.0 - keep
                following = []
                for column in range(column_count):
                    value = keep * state[column] + take * read(row, column)
                    write(row, column, value)
                    following.append(value)
                return tuple(following)

            nothing = tuple(jnp.zeros((SUBLANES, LANES), f32) for _ in range(column_count))
            state = lax.fori_loop(0, row_count, one_row, nothing, unroll=4)
            message_rows = 4 * column_count
            for column in range(column_count):
                at = tile * SUBLANES * message_rows + turn * column_count + column
                exits[pl.ds(at, SUBLANES, stride=message_rows), :] = state[column]


def deposit_and_sweep(field, got, words, decay, sizes):
    sub_count, group_count, row_count, column_count, chunk_count, strip = sizes
    tiles = group_count // SUBLANES
    cells = row_count * column_count
    return pl.pallas_call(
        functools.partial(deposit_kernel, sizes),
        out_shape=[
            jax.ShapeDtypeStruct((column_count, group_count * row_count, LANES), f32),
            jax.ShapeDtypeStruct((group_count * 4 * column_count, LANES), f32),
        ],
        in_specs=[SMEM, VMEM, ANY, VMEM],
        out_specs=[VMEM, VMEM],
        scratch_shapes=[pltpu.VMEM((column_count, group_count * row_count, LANES), f32)]
        + [pltpu.VMEM((tiles, cells + 8, SUBLANES, LANES), f32)] * CHAINS
        + [pltpu.SemaphoreType.DMA((column_count,))],
        compiler_params=params(40),
        cost_estimate=cost(10**7, 10**7),
    )(words, got, field, decay)


def unit_kernel(decay, inside, leaving, held):
    row_count = decay.shape[0]
    state_of = lax.broadcasted_iota(i32, (1, LANES), 1) & 3
    held[...] = jnp.zeros(held.shape, f32)
    for turn in range(4):

        def one_row(step, state, turn=turn):
            row = row_count - 1 - step if turn % 2 else step
            keep = decay[pl.ds(row, 1), :]
            value = keep * state + (1.0 - keep) * held[pl.ds(row, 1), :]
            held[pl.ds(row, 1), :] = value
            return value

        enter = jnp.where(state_of == turn, 1.0, 0.0)
        leaving[turn : turn + 1, :] = lax.fori_loop(0, row_count, one_row, enter, unroll=8)
    inside[...] = jnp.transpose(held[...], (1, 0))


def unit_responses(decay):
    return pl.pallas_call(
        unit_kernel,
        out_shape=[
            jax.ShapeDtypeStruct((LANES, LANES), f32),
            jax.ShapeDtypeStruct((4, LANES), f32),
        ],
        in_specs=[VMEM],
        out_specs=[VMEM, VMEM],
        scratch_shapes=[pltpu.VMEM((LANES, LANES), f32)],
        compiler_params=params(8),
        cost_estimate=cost(10**6, 10**6),
    )(decay)


def circle_weights(lon_length, column_total):
    block_count = column_total // BLOCK
    rate = -1.0 / lon_length[:, None, None]
    decay = jnp.exp(rate)
    gain = jnp.square(-jnp.expm1(rate) / (1.0 + decay))
    centre = (1.0 + decay * decay) / -jnp.expm1(2.0 * rate)
    spot = jnp.arange(BLOCK, dtype=f32)
    gap = jnp.abs(spot[:, None] - spot[None, :])[None]
    near = gain * jnp.exp(rate * gap) * (gap + centre)
    lane = jnp.arange(LANES)
    kind = (lane % 4)[None, None, :]
    forth = (BLOCK - spot)[None, :, None]
    back = spot[None, :, None]
    far = jnp.where(kind < 2, forth, back)
    moment = jnp.exp(rate * far) * jnp.where(kind % 2 == 1, far, 1.0)
    row = jnp.arange(LANES)
    row_kind = (row % 4)[:, None]
    row_block = ((row // 4) % 8)[:, None]
    column = jnp.arange(column_total)[None, :]
    column_block = column // BLOCK
    column_spot = (column % BLOCK).astype(f32)
    ahead = jnp.where(row_kind < 2, column_block - row_block, row_block - column_block)
    steps = ((ahead - 1) % block_count).astype(f32)[None]
    reach = jnp.where(row_kind < 2, column_spot, BLOCK - column_spot)[None]
    turn = jnp.exp(rate * column_total)
    open_turn = -jnp.expm1(rate * column_total)
    weight = gain * jnp.exp(rate * (reach + BLOCK * steps)) / open_turn
    lead = reach + centre + BLOCK * (steps + block_count * turn / open_turn)
    spread = jnp.where(row_kind[None] % 2 == 1, weight, weight * lead)
    spread = jnp.where(row_block[None] < block_count, spread, 0.0)
    near_high, near_low = split_outside(near)
    moment_high, moment_low = split_outside(moment)
    spread_high, spread_low = split_outside(spread)
    use_high = (row // 32 < 2)[None, :, None]
    return (
        near_high,
        near_low,
        jnp.concatenate([moment_high, moment_low], axis=2),
        jnp.where(use_high, spread_high, spread_low),
    )


def circle(pieces, near_high, near_low, moment, spread):
    row_count = pieces[0].shape[0]
    whole = jnp.concatenate(pieces, axis=0)
    high, low = split(whole)
    near = dot(high, near_high) + dot(low, near_high) + dot(high, near_low)
    sums = dot(high, moment)
    sums = sums[:, :LANES] + sums[:, LANES:] + dot(low, moment[:, :LANES])
    lane = lax.broadcasted_iota(i32, (row_count, LANES), 1)
    slot = lax.shift_right_logical(lane, 2) & 7
    moments = jnp.zeros((row_count, LANES), f32)
    for at in range(len(pieces)):
        part = sums[at * row_count : (at + 1) * row_count]
        moments = jnp.where(slot == at, part, moments)
    rest = moments - moments.astype(bf16).astype(f32)
    moments = jnp.where((lax.shift_right_logical(lane, 5) & 1) == 1, rest, moments).astype(bf16)
    far = dot(moments, spread)
    return [
        near[at * row_count : (at + 1) * row_count] + far[:, at * BLOCK : (at + 1) * BLOCK]
        for at in range(len(pieces))
    ]


def longitude_kernel(send_base, swept, near_high, near_low, moment, spread, *rest):
    if send_base is None:
        (out,) = rest
    else:
        weights, out, sent = rest
    column_count = swept.shape[0]
    pieces = [
        jnp.concatenate([swept[2 * at, 0], swept[2 * at + 1, 0]], axis=1)
        for at in range(column_count // 2)
    ]
    pieces = circle(pieces, near_high[0], near_low[0], moment[0], spread[0])
    level = pl.program_id(0)
    for at, piece in enumerate(pieces):
        out[0, :, at * BLOCK : (at + 1) * BLOCK] = piece
    if send_base is None:
        return
    weight = weights[send_base + level * 4]

    @pl.when(level == 0)
    def _():
        for at, piece in enumerate(pieces):
            sent[:, at * BLOCK : (at + 1) * BLOCK] = weight * piece

    @pl.when(level > 0)
    def _():
        for at, piece in enumerate(pieces):
            spot = slice(at * BLOCK, (at + 1) * BLOCK)
            sent[:, spot] = sent[:, spot] + weight * piece


def longitude(swept, weights, count, first, stride, send=None):
    column_count, _, row_count, _ = swept.shape
    column_total = column_count * LANES

    def of(i):
        return first + stride * i

    in_specs = [
        pl.BlockSpec((column_count, 1, row_count, LANES), lambda i: (0, of(i), 0, 0)),
        pl.BlockSpec((1, BLOCK, BLOCK), lambda i: (of(i), 0, 0)),
        pl.BlockSpec((1, BLOCK, BLOCK), lambda i: (of(i), 0, 0)),
        pl.BlockSpec((1, BLOCK, BLOCK), lambda i: (of(i), 0, 0)),
        pl.BlockSpec((1, LANES, column_total), lambda i: (of(i), 0, 0)),
    ]
    out_specs = [pl.BlockSpec((1, row_count, column_total), lambda i: (i, 0, 0))]
    out_shape = [jax.ShapeDtypeStruct((count, row_count, column_total), f32)]
    operands = [swept, *weights]
    if send is not None:
        in_specs.append(SMEM)
        operands.append(send)
        out_specs.append(pl.BlockSpec((row_count, column_total), lambda i: (0, 0)))
        out_shape.append(jax.ShapeDtypeStruct((row_count, column_total), f32))
    return pl.pallas_call(
        functools.partial(longitude_kernel, None if send is None else first),
        grid=(count,),
        in_specs=in_specs,
        out_specs=out_specs,
        out_shape=out_shape,
        compiler_params=params(24),
        cost_estimate=cost(count * 10**9, count * 2 * 10**6),
    )(*operands)


def chain_kernel(index, exits, leaving, inside, near_high, near_low, moment, spread, out, held):
    sub_count, _, _ = exits.shape
    column_count = exits.shape[1] // 4
    shape = (column_count, LANES)
    entering = {}
    for turn in range(4):
        order = list(range(sub_count))
        if turn % 2:
            order.reverse()
        state = jnp.zeros(shape, f32)
        for block in order:
            entering[turn, block] = state
            at = (turn * sub_count + block) * column_count
            held[at : at + column_count, :] = state
            state = exits[block, turn * column_count : (turn + 1) * column_count, :]
            for other in range(turn + 1):
                state = state + leaving[turn, block * 4 + other] * entering[other, block]
    pieces = []
    for at in range(column_count // 2):
        pair = [
            held[pl.ds(2 * at + k, 4 * sub_count, stride=column_count), :] for k in range(2)
        ]
        pieces.append(jnp.concatenate(pair, axis=1))
    pieces = circle(pieces, near_high[0], near_low[0], moment[0], spread[0])
    message_rows = out.shape[0] // sub_count
    for at, piece in enumerate(pieces):
        for k in range(2):
            for turn in range(4):
                place = turn * column_count + 2 * at + k
                out[pl.ds(place, sub_count, stride=message_rows), :] = piece[
                    turn * sub_count : (turn + 1) * sub_count, k * LANES : (k + 1) * LANES
                ]
    for block in range(sub_count):
        at = block * message_rows + 4 * column_count
        out[at : at + 4, :] = inside[block * 4 : (block + 1) * 4, :]
        out[at + 4 : (block + 1) * message_rows, :] = jnp.zeros(
            (message_rows - 4 * column_count - 4, LANES), f32
        )


def chain_states(index, exits, leaving, inside, weights):
    sub_count, rows, _ = exits.shape
    column_total = rows // 4 * LANES
    message_rows = rows + 8

    def whole(*shape):
        return pl.BlockSpec(shape, lambda i, at: (0,) * len(shape))

    def own(*shape):
        return pl.BlockSpec((1,) + shape, lambda i, at: (at[0], 0, 0))

    return pl.pallas_call(
        chain_kernel,
        grid_spec=pltpu.PrefetchScalarGridSpec(
            num_scalar_prefetch=1,
            grid=(1,),
            in_specs=[
                whole(*exits.shape),
                SMEM,
                whole(LANES, LANES),
                own(BLOCK, BLOCK),
                own(BLOCK, BLOCK),
                own(BLOCK, BLOCK),
                own(LANES, column_total),
            ],
            out_specs=whole(sub_count * message_rows, LANES),
            scratch_shapes=[pltpu.VMEM((sub_count * rows, LANES), f32)],
        ),
        out_shape=jax.ShapeDtypeStruct((sub_count * message_rows, LANES), f32),
        compiler_params=params(24),
        cost_estimate=cost(10**9, 2 * 10**6),
    )(index, exits, leaving, inside, *weights)


def level_operator(vert_length):
    rate = (-1.0 / vert_length).T
    count = rate.shape[1]
    lower = jnp.arange(count)[:, None] >= jnp.arange(count)[None, :]
    until = jnp.sum(jnp.where(lower[None], rate[:, None, :], 0.0), axis=2)
    before = until - rate
    take = -jnp.expm1(rate)
    forward = jnp.where(
        lower[None], jnp.exp(jnp.minimum(until[:, :, None] - until[:, None, :], 0.0)), 0.0
    ) * take[:, None, :]
    backward = jnp.where(
        lower.T[None], jnp.exp(jnp.minimum(before[:, None, :] - before[:, :, None], 0.0)), 0.0
    ) * take[:, None, :]
    return jnp.sum(backward[:, :, :, None] * forward[:, None, :, :], axis=2)


def pair_factors(decay):
    top, low = decay[:, 0], decay[:, 1]
    top_take, low_take = 1.0 - top, 1.0 - low
    through = top * low
    sends = (low * top_take, low_take)
    low_out = (low_take * through, low, low_take * low * top_take, low_take * low_take)
    top_out = (
        top * low_out[0] + top_take * top,
        top * low_out[1],
        top * low_out[2] + top_take * top_take,
        top * low_out[3],
    )
    return through, sends, top_out, low_out


def band_tables(vert_length, band):
    decay = jnp.exp(-1.0 / vert_length)
    through, sends, top_out, low_out = pair_factors(decay)
    echo = top_out[0]
    bands = jnp.arange(4)[:, None]
    even = bands % 2 == 0

    def other(x):
        return x.reshape(2, 2, -1)[:, ::-1].reshape(4, -1)

    through_n, echo_n = other(through), other(echo)
    send = [jnp.where(even, sends[i], top_out[2 + i]) for i in range(2)]
    first = [jnp.where(even, through * echo_n * sends[i] + top_out[2 + i], sends[i]) for i in range(2)]
    zeta = jnp.where(bands == 1, (through * through * echo_n + echo)[2][None], 0.0)
    final = []
    for fin, bin_, own_top, own_low in (top_out, low_out):
        for own, sent in ((own_top, sends[0]), (own_low, sends[1])):
            final.append(jnp.where(even, own + bin_ * echo_n * sent, own))
        final.append(jnp.where(even, bin_, fin))
        final.append(
            jnp.where(bands == 0, bin_ * through_n, jnp.where(bands == 3, fin * through_n, 0.0))
        )
        final.append(
            jnp.where(
                bands == 1,
                bin_,
                jnp.where(bands == 2, fin + bin_ * echo_n * through, 0.0),
            )
        )
    table = jnp.stack(send + first + [through, zeta] + final)
    table = lax.dynamic_index_in_dim(table, band, 1, False)
    return table[:2].reshape(-1), table[2:5], table[5], table[6:].reshape(-1)


def last_kernel(variable, own, near, far, kept, message, mix, weights, *rest):
    out = rest[-1]
    row_count, column_total = near.shape
    column_count = column_total // LANES
    message_rows = message.shape[0] // 32
    step = 4 * message_rows
    first = variable * message_rows
    lanes = []
    for column in range(column_count):
        lanes.append(
            jnp.concatenate(
                [
                    message[pl.ds(first + k * column_count + column, 8, stride=step), :]
                    for k in range(4)
                ],
                axis=0,
            )
        )
    states = jnp.concatenate(lanes, axis=1)
    high, low = split(states)
    states = jnp.concatenate([high, high, low, low], axis=0)
    inside = [
        message[pl.ds(first + 4 * column_count + k, 8, stride=step), :] for k in range(4)
    ]
    for level in range(2):
        mixed = jnp.concatenate([part * mix[level, 0] for part in inside], axis=0)
        high, low = split(mixed)
        mixed = jnp.concatenate([high, low, high, low], axis=0)
        total = dot(mixed, states, (((0,), (0,)), ((), ())))[:row_count]
        at = level * 20 + variable
        total = total + weights[at] * own[0] + weights[at + 4] * own[1]
        total = total + weights[at + 8] * near[...] + weights[at + 12] * far[...]
        out[level, 0] = total + weights[at + 16] * kept[...]


def last_step(variable, own, near, far, kept, message, mix, weights, so_far):
    _, row_count, column_total = own.shape

    def whole(shape):
        return pl.BlockSpec(shape, lambda i: (0,) * len(shape))

    operands = [own, near, far, kept, message, mix, weights]
    in_specs = [whole(x.shape) for x in operands[:5]]
    in_specs.append(pl.BlockSpec((2, 1, 8, LANES), lambda i: (0, variable, 0, 0)))
    in_specs.append(SMEM)
    aliases = {}
    if so_far is not None:
        operands.append(so_far)
        in_specs.append(ANY)
        aliases = {7: 0}
    return pl.pallas_call(
        functools.partial(last_kernel, variable),
        grid=(1,),
        in_specs=in_specs,
        out_specs=pl.BlockSpec(
            (2, 1, row_count, column_total), lambda i: (0, variable, 0, 0)
        ),
        out_shape=jax.ShapeDtypeStruct((2, 4, row_count, column_total), f32),
        input_output_aliases=aliases,
        compiler_params=params(24),
        cost_estimate=cost(10**8, 5 * 10**6),
    )(*operands)


def four_bands(swept, lon_weights, messages, vert_length):
    band = lax.axis_index("band")
    lengths = lax.all_gather(vert_length, "band")
    send, first, zeta, final = band_tables(lengths, band)
    operator = level_operator(lengths.reshape(8, 4))
    order = jnp.stack([band, band ^ 2, band ^ 1, band ^ 3])
    columns = (order[:, None] * 2 + jnp.arange(2)[None, :]).reshape(-1)
    mix = lax.dynamic_slice_in_dim(operator, 2 * band, 2, 1)
    mix = jnp.take(mix, columns, axis=2)
    mix = jnp.broadcast_to(jnp.transpose(mix, (1, 0, 2))[..., None], (2, 4, 8, LANES))

    swap = [(0, 1), (1, 0), (2, 3), (3, 2)]
    cross = [(0, 2), (2, 0), (1, 3), (3, 1)]
    fields = []
    for variable in range(4):
        own, sent = longitude(swept, lon_weights, 2, variable, 4, send)
        near = lax.ppermute(sent, "band", swap)
        total = (
            first[0, variable] * own[0] + first[1, variable] * own[1] + first[2, variable] * near
        )
        met = lax.ppermute(total, "band", [(1, 2), (2, 1)])
        kept = met + zeta[variable] * total
        far = lax.ppermute(kept, "band", [(1, 0), (2, 3)])
        fields.append((own, near, far, kept))
    opposite = lax.ppermute(messages, "band", cross)
    pair = jnp.concatenate([messages, opposite], axis=0)
    pair = jnp.concatenate([pair, lax.ppermute(pair, "band", swap)], axis=0)
    result = None
    for variable in range(4):
        result = last_step(variable, *fields[variable], pair, mix, final, result)
    return result


def prefix(part, axis, combine, identity, reverse):
    count = lax.axis_size(axis)
    place = lax.axis_index(axis)
    ahead = count - 1 - place if reverse else place
    gathered = jax.tree.map(lambda a: lax.all_gather(a, axis), part)
    state = jax.tree.map(lambda a, e: jnp.zeros_like(a) + jnp.asarray(e, a.dtype), part, identity)

    def one(turn, state):
        source = count - 1 - turn if reverse else turn
        return combine(
            state, jax.tree.map(lambda a: lax.dynamic_index_in_dim(a, source, 0, False), gathered)
        )

    return lax.fori_loop(0, ahead, one, state)


def combine(earlier, later):
    return (earlier[0] * later[0], later[0] * earlier[1] + later[1])


def level_chain(values, decays, reverse):
    level_count = values.shape[0]
    visit_order = range(level_count - 1, -1, -1) if reverse else range(level_count)
    carry_state = jnp.zeros_like(values[0])
    level_gain = jnp.ones((values.shape[1],), f32)
    outputs = [None] * level_count
    carried = [None] * level_count
    for level_index in visit_order:
        factor = decays[level_index][:, None, None]
        carry_state = factor * carry_state + (1.0 - factor) * values[level_index]
        level_gain = level_gain * decays[level_index]
        outputs[level_index] = carry_state
        carried[level_index] = level_gain
    total_decay = level_gain[:, None, None]
    identity = (jnp.ones_like(total_decay), jnp.zeros_like(carry_state))
    incoming = prefix((total_decay, carry_state), "band", combine, identity, reverse)[1]
    return jnp.stack(
        [
            outputs[level_index] + carried[level_index][:, None, None] * incoming
            for level_index in range(level_count)
        ]
    )


def any_bands(swept, lon_weights, messages, vert_length):
    column_count, group_count, row_count, _ = swept.shape
    (values,) = longitude(swept, lon_weights, group_count, 0, 1)
    messages = messages.reshape(group_count, -1, LANES)
    states = messages[:, : 4 * column_count].reshape(group_count, 4, -1)
    inside = messages[:, 4 * column_count : 4 * column_count + 4, :row_count]
    values = values + jnp.einsum("gkr,gkc->grc", inside, states, precision=highest)
    decay = jnp.exp(-1.0 / vert_length)
    values = values.reshape(decay.shape + values.shape[1:])
    return level_chain(level_chain(values, decay, False), decay, True)


def per_device(background, obs_columns, obs_owner, obs_cell, lat_length, lon_length, vert_length):
    level_count, var_count, row_count, lon_count = background.shape
    sub_count = lax.axis_size("sub")
    sub_index = lax.axis_index("sub")
    group_count = level_count * var_count
    strip = row_count * lon_count
    column_count = lon_count // LANES
    owners = obs_owner[:, 0]
    capacity = 2 * owners.shape[0] // sub_count
    chunk_count = capacity // LANES

    packed = pack_observations(
        obs_columns.reshape(group_count, -1), owners, obs_cell, sub_count, strip, capacity
    )
    got = lax.all_to_all(packed, "sub", split_axis=0, concat_axis=0, tiled=True)
    words = got[:, chunk_count * group_count :, :].reshape(sub_count, -1)[:, :capacity]
    words = jnp.pad(words.astype(i32), ((0, 0), (0, LANES)), constant_values=strip).reshape(-1)

    lengths = lat_length.reshape(group_count, sub_count, row_count)
    own_rows = lax.dynamic_index_in_dim(lengths, sub_index, 1, False)
    decay = jnp.exp(-1.0 / own_rows).T
    decay = jnp.broadcast_to(decay[:, :, None], (row_count, group_count, LANES))
    own_group = lax.dynamic_index_in_dim(lengths, sub_index, 0, False)
    unit_decay = jnp.repeat(jnp.exp(-1.0 / own_group).T, 4, axis=1)
    unit_decay = jnp.pad(unit_decay, ((0, 0), (0, LANES - 4 * sub_count)))
    inside, leaving = unit_responses(unit_decay)
    lon_weights = circle_weights(lon_length.reshape(-1), lon_count)

    sizes = (sub_count, group_count, row_count, column_count, chunk_count, strip)
    swept, exits = deposit_and_sweep(
        background.reshape(group_count * row_count, lon_count), got, words, decay, sizes
    )
    swept = swept.reshape(column_count, group_count, row_count, LANES)
    exits = exits.reshape(group_count, 4 * column_count, LANES)
    exits = lax.all_to_all(exits, "sub", split_axis=0, concat_axis=0, tiled=True)
    index = sub_index.astype(i32).reshape(1)
    messages = chain_states(index, exits, leaving, inside, lon_weights)
    messages = lax.all_to_all(messages, "sub", split_axis=0, concat_axis=0, tiled=True)
    if lax.axis_size("band") == 4 and level_count == 2:
        return four_bands(swept, lon_weights, messages, vert_length)
    return any_bands(swept, lon_weights, messages, vert_length)


def solution(mesh):
    placed = (
        P("band", None, "sub", None),
        P("band", None, "sub"),
        P("sub", None),
        P("sub"),
        P("band", None, None),
        P("band", None),
        P("band", None),
    )
    return jax.shard_map(
        per_device,
        mesh=mesh,
        in_specs=placed,
        out_specs=P("band", None, "sub", None),
        check_vma=False,
    )
```

```python
import functools

import jax
import jax.numpy as jnp
from jax import lax
from jax.experimental import pallas as pl
from jax.experimental.pallas import tpu as pltpu
from jax.sharding import PartitionSpec as P

f32 = jnp.float32
i32 = jnp.int32
bf16 = jnp.bfloat16
highest = lax.Precision.HIGHEST

LANES = 128
SUBLANES = 8
BLOCK = 256
CHAINS = 4

VMEM = pl.BlockSpec(memory_space=pltpu.VMEM)
SMEM = pl.BlockSpec(memory_space=pltpu.SMEM)
HBM = pl.BlockSpec(memory_space=pltpu.HBM)


def params(mib):
    return pltpu.CompilerParams(vmem_limit_bytes=mib << 20)


def cost(flops, read):
    return pl.CostEstimate(flops=flops, bytes_accessed=read, transcendentals=0)


def dot(a, b, dims=(((1,), (0,)), ((), ()))):
    return lax.dot_general(a, b, dims, preferred_element_type=f32)


def split(x):
    high = x.astype(bf16)
    return high, (x - high.astype(f32)).astype(bf16)


def pack_kernel(sizes, owners, cells, values, packed, places, tally, joined, counts, sem):
    sub_count, group_count, chunk_count, strip = sizes
    block_count = owners.shape[0]
    tiles = group_count // SUBLANES
    lane = lax.broadcasted_iota(i32, (SUBLANES, LANES), 1)
    square = lambda axis: lax.broadcasted_iota(i32, (LANES, LANES), axis)
    owner = owners[...]
    picked = [jnp.where(owner == sub, 1.0, 0.0) for sub in range(sub_count)]
    upto = jnp.where(square(0) <= square(1), 1.0, 0.0).astype(bf16)
    ranks = dot(jnp.concatenate(picked, axis=0).astype(bf16), upto)
    wide = lax.broadcasted_iota(i32, (block_count, LANES), 1)
    place = jnp.zeros((block_count, LANES), f32)
    base = jnp.zeros((block_count, LANES), f32)
    totals = jnp.zeros((block_count, LANES), f32)
    for sub in range(sub_count):
        rank = ranks[sub * block_count : (sub + 1) * block_count]
        total = jnp.broadcast_to(rank[:, LANES - 1 :], rank.shape)
        place = jnp.where(owner == sub, rank - 1.0 + base, place)
        totals = jnp.where(wide == sub, total, totals)
        base = base + total
    places[...] = place.astype(i32)
    tally[...] = totals.astype(i32)
    copy = pltpu.make_async_copy(tally, counts, sem)
    copy.start()
    copy.wait()
    extra = -(group_count + SUBLANES) % 16
    row = square(0)

    def one_block(block, ends):
        at = pl.multiple_of(block * LANES, LANES)
        parts = [
            values[:, pl.ds(at, LANES)],
            jnp.broadcast_to(cells[pl.ds(block, 1), :], (SUBLANES, LANES)).astype(f32),
        ]
        if extra:
            parts.append(jnp.zeros((extra, LANES), f32))
        whole = jnp.concatenate(parts, axis=0)
        rows = whole.shape[0]
        high, rest = whole.astype(bf16), whole
        rest = rest - high.astype(f32)
        middle = rest.astype(bf16)
        low = (rest - middle.astype(f32)).astype(bf16)
        move = jnp.where(row == places[pl.ds(block, 1), :], 1.0, 0.0).astype(bf16)
        moved = dot(
            jnp.concatenate([high, middle, low], axis=0), move, (((1,), (1,)), ((), ()))
        )
        moved = moved[:rows] + moved[rows : 2 * rows] + moved[2 * rows :]
        start = jnp.int32(0)
        writes, following = [], []
        for sub in range(sub_count):
            end = ends[sub]
            chunk, offset = lax.shift_right_logical(end, 7), end & 127
            for tile in range(tiles + 1):
                turned = pltpu.roll(
                    moved[tile * SUBLANES : (tile + 1) * SUBLANES], (end - start) & 127, 1
                )
                kept = jnp.where(lane >= offset, turned, joined[sub, chunk, tile])
                writes.append((sub, chunk, tile, kept, turned))
            start = start + counts[block, sub]
            following.append(end + counts[block, sub])
        for sub, chunk, tile, kept, turned in writes:
            joined[sub, chunk, tile] = kept
            joined[sub, chunk + 1, tile] = turned
        return tuple(following)

    ends = lax.fori_loop(0, block_count, one_block, (jnp.int32(0),) * sub_count)
    word_row = chunk_count * group_count
    word_rows = packed.shape[1] - word_row
    for sub in range(sub_count):
        packed[sub, word_row:, :] = jnp.full((word_rows, LANES), float(strip), f32)
        for chunk in range(chunk_count):
            for tile in range(tiles):
                at = chunk * group_count + tile * SUBLANES
                packed[sub, at : at + SUBLANES, :] = joined[sub, chunk, tile]
            filled = lane + chunk * LANES < ends[sub]
            cell = jnp.where(filled, joined[sub, chunk, tiles], 0.0).astype(i32)
            word = (cell - (cell & 127)) + ((cell - lane) & 127)
            word = jnp.where(filled, word, strip).astype(f32)
            packed[sub, word_row + chunk : word_row + chunk + 1, :] = word[:1]


def pack_observations(obs_values, owners, cells, sub_count, strip, capacity):
    group_count, obs_count = obs_values.shape
    chunk_count = capacity // LANES
    block_count = obs_count // LANES
    rows = chunk_count * group_count + SUBLANES * (-(-chunk_count // SUBLANES))
    tiles = group_count // SUBLANES
    return pl.pallas_call(
        functools.partial(pack_kernel, (sub_count, group_count, chunk_count, strip)),
        out_shape=jax.ShapeDtypeStruct((sub_count, rows, LANES), f32),
        in_specs=[VMEM, VMEM, VMEM],
        out_specs=VMEM,
        scratch_shapes=[
            pltpu.VMEM((block_count, LANES), i32),
            pltpu.VMEM((block_count, LANES), i32),
            pltpu.VMEM((sub_count, chunk_count + 2, tiles + 1, SUBLANES, LANES), f32),
            pltpu.SMEM((block_count, LANES), i32),
            pltpu.SemaphoreType.DMA,
        ],
        compiler_params=params(40),
        cost_estimate=cost(10**6, 10**6),
    )(owners.reshape(block_count, LANES), cells.reshape(block_count, LANES), obs_values)


def deposit_kernel(sizes, index, lengths, got, field, swept, exits, loaded, *rest):
    sub_count, group_count, row_count, column_count, chunk_count, strip = sizes
    totals, (decay, own, integers, words, word_sem, sems) = rest[:CHAINS], rest[CHAINS:]
    tiles = group_count // SUBLANES
    word_row = chunk_count * group_count
    word_rows = got.shape[1] - word_row

    def load(column):
        return pltpu.make_async_copy(
            field.at[:, pl.ds(column * LANES, LANES)], loaded.at[column], sems.at[column]
        )

    for source in range(sub_count):
        integers[source * word_rows : (source + 1) * word_rows, :] = got[
            source, word_row:, :
        ].astype(i32)
    hand_over = pltpu.make_async_copy(integers, words, word_sem)
    hand_over.start()
    for column in range(column_count):
        load(column).start()
    here = index[0]
    for group in range(group_count):
        own[group : group + 1, :] = jnp.exp(-1.0 / lengths[group, pl.ds(here, 1), :])
    for tile in range(tiles):
        keep = own[tile * SUBLANES : (tile + 1) * SUBLANES, :]
        for row in range(row_count):
            decay[row, tile] = jnp.broadcast_to(keep[:, row : row + 1], (SUBLANES, LANES))

    def clear(at, carry):
        for total in totals:
            for tile in range(tiles):
                for k in range(8):
                    total[tile, at * 8 + k] = jnp.zeros((SUBLANES, LANES), f32)
        return carry

    lax.fori_loop(0, row_count * column_count // 8, clear, 0)
    lane = lax.broadcasted_iota(i32, (SUBLANES, LANES), 1)
    hand_over.wait()

    def one_source(source, carry):
        first = source * word_rows

        def more(chunk):
            last = jnp.minimum(chunk, chunk_count - 1)
            return (chunk < chunk_count) & (words[first + last, 0] < strip)

        def one_chunk(chunk):
            blocks = [
                got[
                    source,
                    pl.ds(pl.multiple_of(chunk * group_count + tile * SUBLANES, 8), SUBLANES),
                    :,
                ]
                for tile in range(tiles)
            ]
            for slot in range(LANES):
                word = words[first + chunk, slot]
                target = lax.shift_right_logical(word, 7)
                turn = word & 127
                for tile in range(tiles):
                    value = pltpu.roll(jnp.where(lane == slot, blocks[tile], 0.0), turn, 1)
                    total = totals[slot % CHAINS]
                    total[tile, target] = total[tile, target] + value
            return chunk + 1

        lax.while_loop(more, one_chunk, jnp.int32(0))
        return carry

    lax.fori_loop(0, sub_count, one_source, 0)
    for column in range(column_count):
        load(column).wait()

    for tile in range(tiles):
        held = totals[0]
        spot = tile * SUBLANES * row_count

        def read_first(row, column):
            at = row * column_count + column
            value = loaded[column, pl.ds(spot + row, SUBLANES, stride=row_count), :]
            for total in totals:
                value = value + total[tile, at]
            return value

        def read_held(row, column):
            return held[tile, row * column_count + column]

        def write_held(row, column, value):
            held[tile, row * column_count + column] = value

        def write_last(row, column, value):
            swept[column, pl.ds(spot + row, SUBLANES, stride=row_count), :] = value

        for turn in range(4):
            read = read_first if turn == 0 else read_held
            write = write_last if turn == 3 else write_held

            def one_row(step, state, turn=turn, read=read, write=write):
                row = row_count - 1 - step if turn % 2 else step
                keep = decay[row, tile]
                take = 1.0 - keep
                following = []
                for column in range(column_count):
                    value = keep * state[column] + take * read(row, column)
                    write(row, column, value)
                    following.append(value)
                return tuple(following)

            nothing = tuple(jnp.zeros((SUBLANES, LANES), f32) for _ in range(column_count))
            state = lax.fori_loop(0, row_count, one_row, nothing, unroll=4)
            message_rows = 4 * column_count
            for column in range(column_count):
                at = tile * SUBLANES * message_rows + turn * column_count + column
                exits[pl.ds(at, SUBLANES, stride=message_rows), :] = state[column]


def deposit_and_sweep(index, lengths, got, field, sizes):
    sub_count, group_count, row_count, column_count, chunk_count, strip = sizes
    tiles = group_count // SUBLANES
    cells = row_count * column_count
    word_rows = got.shape[1] - chunk_count * group_count
    return pl.pallas_call(
        functools.partial(deposit_kernel, sizes),
        out_shape=[
            jax.ShapeDtypeStruct((column_count, group_count * row_count, LANES), f32),
            jax.ShapeDtypeStruct((group_count * 4 * column_count, LANES), f32),
        ],
        in_specs=[SMEM, VMEM, VMEM, HBM],
        out_specs=[VMEM, VMEM],
        scratch_shapes=[pltpu.VMEM((column_count, group_count * row_count, LANES), f32)]
        + [pltpu.VMEM((tiles, cells + 8, SUBLANES, LANES), f32)] * CHAINS
        + [
            pltpu.VMEM((row_count, tiles, SUBLANES, LANES), f32),
            pltpu.VMEM((group_count, LANES), f32),
            pltpu.VMEM((sub_count * word_rows, LANES), i32),
            pltpu.SMEM((sub_count * word_rows, LANES), i32),
            pltpu.SemaphoreType.DMA,
            pltpu.SemaphoreType.DMA((column_count,)),
        ],
        compiler_params=params(56),
        cost_estimate=cost(10**7, 10**7),
    )(index, lengths, got, field)


def prepare_kernel(sizes, index, lon_length, lengths, *rest):
    sub_count, row_count, block_count = sizes
    near_high, near_low, moment, spread, inside, leaving, decay, held = rest
    group = pl.program_id(0)

    @pl.when(group == 0)
    def _():
        keep = jnp.exp(-1.0 / lengths[index[0]])
        decay[...] = jnp.zeros(decay.shape, f32)
        for turn in range(4):
            decay[pl.ds(turn, sub_count, stride=4), :] = keep
        decay[...] = jnp.transpose(decay[...], (1, 0))
        held[...] = jnp.zeros(held.shape, f32)
        state_of = lax.broadcasted_iota(i32, (1, LANES), 1) & 3
        for turn in range(4):

            def one_row(step, state, turn=turn):
                row = row_count - 1 - step if turn % 2 else step
                keep = decay[pl.ds(row, 1), :]
                value = keep * state + (1.0 - keep) * held[pl.ds(row, 1), :]
                held[pl.ds(row, 1), :] = value
                return value

            enter = jnp.where(state_of == turn, 1.0, 0.0)
            state = lax.fori_loop(0, row_count, one_row, enter, unroll=8)
            leaving[turn : turn + 1, :] = state
        inside[...] = jnp.transpose(held[...], (1, 0))

    def ramp(shape, axis):
        return lax.broadcasted_iota(i32, shape, axis)

    def constant(x, shape):
        return jnp.broadcast_to(x, shape)

    one = (1, LANES)
    rate = -1.0 / jnp.full(one, lon_length[group], f32)
    decays = jnp.exp(rate)
    gain = ((1.0 - decays) / (1.0 + decays)) ** 2
    centre = (1.0 + decays * decays) / (1.0 - decays * decays)
    turn = jnp.exp(rate * float(BLOCK * block_count))
    lag = float(BLOCK * block_count) * turn / (1.0 - turn)
    full_gain = gain / (1.0 - turn)

    def twice(x):
        return jnp.concatenate([x, x], axis=1)

    shape = (BLOCK, BLOCK)
    gap = jnp.abs(ramp(shape, 0) - ramp(shape, 1)).astype(f32)
    near = twice(gain) * jnp.exp(twice(rate) * gap) * (gap + twice(centre))
    high, low = split(near)
    near_high[0] = high
    near_low[0] = low
    shape = (BLOCK, LANES)
    kind = ramp(shape, 1) & 3
    spot = ramp(shape, 0)
    far = jnp.where(kind < 2, BLOCK - spot, spot).astype(f32)
    sums = jnp.exp(rate * far) * jnp.where((kind & 1) == 1, far, 1.0)
    high, low = split(sums)
    moment[0, :, :LANES] = high
    moment[0, :, LANES:] = low
    shape = (32, BLOCK)
    kind = ramp(shape, 0) & 3
    block = lax.shift_right_logical(ramp(shape, 0), 2)
    spot = ramp(shape, 1)
    reach = jnp.where(kind < 2, spot, BLOCK - spot).astype(f32)
    for at in range(block_count):
        ahead = jnp.where(kind < 2, at - block, block - at) - 1
        steps = jnp.where(ahead < 0, ahead + block_count, ahead)
        full = reach + (steps * BLOCK).astype(f32)
        weight = twice(full_gain) * jnp.exp(twice(rate) * full)
        lead = full + twice(centre + lag)
        value = jnp.where((kind & 1) == 1, weight, weight * lead)
        value = jnp.where(block < block_count, value, 0.0)
        high, low = split(value)
        spread[0, :32, at * BLOCK : (at + 1) * BLOCK] = high
        spread[0, 32:, at * BLOCK : (at + 1) * BLOCK] = low


def prepare(index, lon_length, lengths, row_count, column_total):
    group_count, sub_count, _ = lengths.shape
    sizes = (sub_count, row_count, column_total // BLOCK)
    shapes = [
        ((BLOCK, BLOCK), bf16),
        ((BLOCK, BLOCK), bf16),
        ((BLOCK, BLOCK), bf16),
        ((64, column_total), bf16),
    ]
    return pl.pallas_call(
        functools.partial(prepare_kernel, sizes),
        grid=(group_count,),
        in_specs=[SMEM, SMEM, VMEM],
        out_specs=[pl.BlockSpec((1,) + shape, lambda i: (i, 0, 0)) for shape, _ in shapes]
        + [
            pl.BlockSpec((LANES, LANES), lambda i: (0, 0)),
            pl.BlockSpec((4, LANES), lambda i: (0, 0)),
        ],
        out_shape=[jax.ShapeDtypeStruct((group_count,) + shape, kind) for shape, kind in shapes]
        + [
            jax.ShapeDtypeStruct((LANES, LANES), f32),
            jax.ShapeDtypeStruct((4, LANES), f32),
        ],
        scratch_shapes=[pltpu.VMEM((LANES, LANES), f32)] * 2,
        compiler_params=params(56),
        cost_estimate=cost(10**7, 10**7),
    )(index, lon_length, lengths)


def circle(pieces, near_high, near_low, moment, spread):
    row_count = pieces[0].shape[0]
    whole = jnp.concatenate(pieces, axis=0)
    high, low = split(whole)
    near = dot(high, near_high) + dot(low, near_high) + dot(high, near_low)
    sums = dot(high, moment)
    sums = sums[:, :LANES] + sums[:, LANES:] + dot(low, moment[:, :LANES])
    lane = lax.broadcasted_iota(i32, (row_count, LANES), 1)
    slot = lax.shift_right_logical(lane, 2) & 7
    moments = jnp.zeros((row_count, LANES), f32)
    for at in range(len(pieces)):
        part = sums[at * row_count : (at + 1) * row_count]
        moments = jnp.where(slot == at, part, moments)
    rest = moments - moments.astype(bf16).astype(f32)
    moments = jnp.where((lax.shift_right_logical(lane, 5) & 1) == 1, rest, moments).astype(bf16)
    spread = jnp.concatenate([spread[:32], spread[:32], spread[32:], spread[32:]], axis=0)
    far = dot(moments, spread)
    return [
        near[at * row_count : (at + 1) * row_count] + far[:, at * BLOCK : (at + 1) * BLOCK]
        for at in range(len(pieces))
    ]


def longitude_kernel(swept, near_high, near_low, moment, spread, *rest):
    column_count = swept.shape[0]
    pieces = [
        jnp.concatenate([swept[2 * at, 0], swept[2 * at + 1, 0]], axis=1)
        for at in range(column_count // 2)
    ]
    pieces = circle(pieces, near_high[0], near_low[0], moment[0], spread[0])
    out = rest[0] if len(rest) == 1 else rest[1]
    for at, piece in enumerate(pieces):
        out[0, :, at * BLOCK : (at + 1) * BLOCK] = piece
    if len(rest) == 1:
        return
    table, _, sent, part = rest
    level = pl.program_id(0)
    sums = []
    for target, first in ((sent, 0), (part, 2)):
        weight = table[0, pl.ds(first + level, 1), :]
        sums.append((target, jnp.concatenate([weight, weight], axis=1)))

    @pl.when(level == 0)
    def _():
        for target, weight in sums:
            for at, piece in enumerate(pieces):
                target[:, at * BLOCK : (at + 1) * BLOCK] = weight * piece

    @pl.when(level > 0)
    def _():
        for target, weight in sums:
            for at, piece in enumerate(pieces):
                spot = slice(at * BLOCK, (at + 1) * BLOCK)
                target[:, spot] = target[:, spot] + weight * piece


def longitude(swept, weights, count, first, stride, table=None):
    column_count, _, row_count, _ = swept.shape
    column_total = column_count * LANES

    def of(i):
        return first + stride * i

    in_specs = [
        pl.BlockSpec((column_count, 1, row_count, LANES), lambda i: (0, of(i), 0, 0)),
        pl.BlockSpec((1, BLOCK, BLOCK), lambda i: (of(i), 0, 0)),
        pl.BlockSpec((1, BLOCK, BLOCK), lambda i: (of(i), 0, 0)),
        pl.BlockSpec((1, BLOCK, BLOCK), lambda i: (of(i), 0, 0)),
        pl.BlockSpec((1, 64, column_total), lambda i: (of(i), 0, 0)),
    ]
    out_specs = [pl.BlockSpec((1, row_count, column_total), lambda i: (i, 0, 0))]
    out_shape = [jax.ShapeDtypeStruct((count, row_count, column_total), f32)]
    operands = [swept, *weights]
    if table is not None:
        in_specs.append(pl.BlockSpec((1, 16, LANES), lambda i: (first, 0, 0)))
        operands.append(table)
        out_specs += [pl.BlockSpec((row_count, column_total), lambda i: (0, 0))] * 2
        out_shape += [jax.ShapeDtypeStruct((row_count, column_total), f32)] * 2
    return pl.pallas_call(
        longitude_kernel,
        grid=(count,),
        in_specs=in_specs,
        out_specs=out_specs,
        out_shape=out_shape,
        compiler_params=params(56),
        cost_estimate=cost(count * 10**9, count * 2 * 10**6),
    )(*operands)


def chain_kernel(index, exits, leaving, inside, near_high, near_low, moment, spread, out, held):
    sub_count, _, _ = exits.shape
    column_count = exits.shape[1] // 4
    shape = (column_count, LANES)
    entering = {}
    for turn in range(4):
        order = list(range(sub_count))
        if turn % 2:
            order.reverse()
        state = jnp.zeros(shape, f32)
        for block in order:
            entering[turn, block] = state
            at = (turn * sub_count + block) * column_count
            held[at : at + column_count, :] = state
            state = exits[block, turn * column_count : (turn + 1) * column_count, :]
            for other in range(turn + 1):
                state = state + leaving[turn, block * 4 + other] * entering[other, block]
    pieces = []
    for at in range(column_count // 2):
        pair = [
            held[pl.ds(2 * at + k, 4 * sub_count, stride=column_count), :] for k in range(2)
        ]
        pieces.append(jnp.concatenate(pair, axis=1))
    pieces = circle(pieces, near_high[0], near_low[0], moment[0], spread[0])
    message_rows = out.shape[0] // sub_count
    for at, piece in enumerate(pieces):
        for k in range(2):
            for turn in range(4):
                place = turn * column_count + 2 * at + k
                out[pl.ds(place, sub_count, stride=message_rows), :] = piece[
                    turn * sub_count : (turn + 1) * sub_count, k * LANES : (k + 1) * LANES
                ]
    for block in range(sub_count):
        at = block * message_rows + 4 * column_count
        out[at : at + 4, :] = inside[block * 4 : (block + 1) * 4, :]
        out[at + 4 : (block + 1) * message_rows, :] = jnp.zeros(
            (message_rows - 4 * column_count - 4, LANES), f32
        )


def chain_states(index, exits, leaving, inside, weights):
    sub_count, rows, _ = exits.shape
    column_total = rows // 4 * LANES
    message_rows = rows + 8

    def whole(*shape):
        return pl.BlockSpec(shape, lambda i, at: (0,) * len(shape))

    def own(*shape):
        return pl.BlockSpec((1,) + shape, lambda i, at: (at[0], 0, 0))

    return pl.pallas_call(
        chain_kernel,
        grid_spec=pltpu.PrefetchScalarGridSpec(
            num_scalar_prefetch=1,
            grid=(1,),
            in_specs=[
                whole(*exits.shape),
                SMEM,
                whole(LANES, LANES),
                own(BLOCK, BLOCK),
                own(BLOCK, BLOCK),
                own(BLOCK, BLOCK),
                own(64, column_total),
            ],
            out_specs=whole(sub_count * message_rows, LANES),
            scratch_shapes=[pltpu.VMEM((sub_count * rows, LANES), f32)],
        ),
        out_shape=jax.ShapeDtypeStruct((sub_count * message_rows, LANES), f32),
        compiler_params=params(56),
        cost_estimate=cost(10**9, 2 * 10**6),
    )(index, exits, leaving, inside, *weights)


def pair_factors(top, low):
    top_take, low_take = 1.0 - top, 1.0 - low
    through = top * low
    sends = (low * top_take, low_take)
    low_out = (low_take * through, low, low_take * low * top_take, low_take * low_take)
    top_out = (
        top * low_out[0] + top_take * top,
        top * low_out[1],
        top * low_out[2] + top_take * top_take,
        top * low_out[3],
    )
    return through, sends, top_out, low_out


def tables_kernel(index, decay, table, mix):
    band = index[0]

    def factors(at):
        return pair_factors(decay[at * 8 : at * 8 + 4, :], decay[at * 8 + 4 : at * 8 + 8, :])

    def by_band(*values):
        result = values[0]
        for at in range(1, 4):
            result = jnp.where(band == at, values[at], result)
        return result

    through, sends, top_out, low_out = factors(0)
    across, beside, corner = factors(1), factors(2), factors(3)
    through_n, echo_n = beside[0], beside[2][0]
    third = by_band(across[0], corner[0], across[0], across[0])
    third_echo = by_band(across[2][0], corner[2][0], across[2][0], across[2][0])
    fourth_echo = by_band(corner[2][0], across[2][0], corner[2][0], corner[2][0])
    zeta = third * third * fourth_echo + third_echo
    rows = []
    for i in range(2):
        reply = top_out[2 + i]
        rows.append(by_band(sends[i], reply + through * zeta * sends[i], sends[i], reply))
    for i in range(2):
        rows.append(
            by_band(
                sends[i], sends[i], through * echo_n * sends[i] + top_out[2 + i], sends[i]
            )
        )
    rows.append(through)
    for fin, back, *own in (top_out, low_out):
        for i in range(2):
            rows.append(
                by_band(
                    own[i] + back * (through_n * through_n * zeta + echo_n) * sends[i],
                    own[i] + back * zeta * sends[i],
                    own[i] + back * echo_n * sends[i],
                    own[i],
                )
            )
        none = jnp.zeros_like(fin)
        rows.append(by_band(back, fin + back * zeta * through, back, fin))
        rows.append(by_band(back * through_n, none, none, fin * through_n))
        rows.append(by_band(none, back, fin + back * echo_n * through, none))
    for variable in range(4):
        for at, row in enumerate(rows):
            table[variable, at : at + 1, :] = row[variable : variable + 1]
    row = lax.broadcasted_iota(i32, (SUBLANES, LANES), 0)
    for variable in range(4):
        value = jnp.zeros((SUBLANES, LANES), f32)
        downward, keeps = [], []
        for level in range(8):
            other = (level // 2) ^ band
            place = (other & 1) * 2 + lax.shift_right_logical(other, 1)
            at = place * 8 + (level % 2) * 4 + variable
            keep = jnp.broadcast_to(decay[pl.ds(at, 1), :], (SUBLANES, LANES))
            unit = jnp.where(row == place * 2 + level % 2, 1.0, 0.0)
            value = keep * value + (1.0 - keep) * unit
            downward.append(value)
            keeps.append(keep)
        value = jnp.zeros((SUBLANES, LANES), f32)
        upward = [None] * 8
        for level in reversed(range(8)):
            value = keeps[level] * value + (1.0 - keeps[level]) * downward[level]
            upward[level] = value
        for level in range(2):
            mix[level, variable] = by_band(*[upward[2 * at + level] for at in range(4)])


def tables(index, decay):
    return pl.pallas_call(
        tables_kernel,
        in_specs=[SMEM, VMEM],
        out_specs=[VMEM, VMEM],
        out_shape=[
            jax.ShapeDtypeStruct((4, 16, LANES), f32),
            jax.ShapeDtypeStruct((2, 4, SUBLANES, LANES), f32),
        ],
        compiler_params=params(56),
        cost_estimate=cost(10**5, 10**5),
    )(index, decay)


def add_kernel(part, near, table, total):
    weight = table[0, 4:5, :]
    for column in range(part.shape[1] // LANES):
        at = slice(column * LANES, (column + 1) * LANES)
        total[:, at] = part[:, at] + weight * near[:, at]


def add_near(variable, part, near, table):
    row_count, column_total = part.shape
    steps = 2 if row_count % 16 == 0 else 1
    block = pl.BlockSpec((row_count // steps, column_total), lambda i: (i, 0))
    return pl.pallas_call(
        add_kernel,
        grid=(steps,),
        in_specs=[block, block, pl.BlockSpec((1, 16, LANES), lambda i: (variable, 0, 0))],
        out_specs=block,
        out_shape=jax.ShapeDtypeStruct(part.shape, f32),
        compiler_params=params(56),
        cost_estimate=cost(10**6, 2 * 10**6),
    )(part, near, table)


def last_kernel(own, near, far, met, message, mix, table, *rest):
    out, added = rest[-2:]
    rows, column_total = near.shape
    column_count = column_total // LANES
    row_count = added.shape[1]
    step = pl.program_id(0)

    @pl.when(step == 0)
    def _():
        parts = message.reshape(SUBLANES * message.shape[2], LANES)
        stride = message.shape[2]
        lanes = []
        for column in range(column_count):
            lanes.append(
                jnp.concatenate(
                    [
                        parts[pl.ds(k * column_count + column, SUBLANES, stride=stride), :]
                        for k in range(4)
                    ],
                    axis=0,
                )
            )
        high, low = split(jnp.concatenate(lanes, axis=1))
        states = jnp.concatenate([high, high, low, low], axis=0)
        inside = [parts[pl.ds(4 * column_count + k, SUBLANES, stride=stride), :] for k in range(4)]
        for level in range(2):
            mixed = jnp.concatenate([part * mix[level, 0] for part in inside], axis=0)
            high, low = split(mixed)
            mixed = jnp.concatenate([high, low, high, low], axis=0)
            added[level] = dot(mixed, states, (((0,), (0,)), ((), ())))[:row_count]

    first = pl.multiple_of(step * rows, SUBLANES)
    for level in range(2):
        weights = [table[0, 5 + level * 5 + k : 6 + level * 5 + k, :] for k in range(5)]
        for column in range(column_count):
            at = slice(column * LANES, (column + 1) * LANES)
            total = added[level, pl.ds(first, rows), at]
            total = total + weights[0] * own[0, :, at] + weights[1] * own[1, :, at]
            total = total + weights[2] * near[:, at] + weights[3] * far[:, at]
            out[level, 0, :, at] = total + weights[4] * met[:, at]


def last_step(variable, own, near, far, met, message, mix, table, so_far):
    _, row_count, column_total = own.shape
    steps = 3 if row_count % 24 == 0 else 1
    rows = row_count // steps
    block = pl.BlockSpec((rows, column_total), lambda i: (i, 0))
    message_rows = message.shape[2]
    operands = [own, near, far, met, message, mix, table]
    in_specs = [
        pl.BlockSpec((2, rows, column_total), lambda i: (0, i, 0)),
        block,
        block,
        block,
        pl.BlockSpec((8, 1, message_rows, LANES), lambda i: (0, variable, 0, 0)),
        pl.BlockSpec((2, 1, SUBLANES, LANES), lambda i: (0, variable, 0, 0)),
        pl.BlockSpec((1, 16, LANES), lambda i: (variable, 0, 0)),
    ]
    aliases = {}
    if so_far is not None:
        operands.append(so_far)
        in_specs.append(HBM)
        aliases = {7: 0}
    return pl.pallas_call(
        last_kernel,
        grid=(steps,),
        in_specs=in_specs,
        out_specs=pl.BlockSpec((2, 1, rows, column_total), lambda i: (0, variable, i, 0)),
        out_shape=jax.ShapeDtypeStruct((2, 4, row_count, column_total), f32),
        scratch_shapes=[pltpu.VMEM((2, row_count, column_total), f32)],
        input_output_aliases=aliases,
        compiler_params=params(56),
        cost_estimate=cost(10**8, 5 * 10**6),
    )(*operands)


SWAP = [(0, 1), (1, 0), (2, 3), (3, 2)]
CROSS = [(0, 2), (2, 0), (1, 3), (3, 1)]


def of_all_bands(part):
    pair = jnp.concatenate([part, lax.ppermute(part, "band", CROSS)], axis=0)
    return jnp.concatenate([pair, lax.ppermute(pair, "band", SWAP)], axis=0)


def after(value, *earlier):
    return lax.optimization_barrier((value,) + earlier)[0]


def four_bands(swept, weights, exits, chain, table, mix):
    owns, parts, nears, totals, mets = [], [], [], [], []

    def filter_one(variable, *earlier):
        own, sent, part = longitude(after(swept, *earlier), weights, 2, variable, 4, table)
        owns.append(own)
        parts.append(part)
        nears.append(lax.ppermute(sent, "band", SWAP))
        return part

    def cross_one(variable, *earlier):
        part = after(parts[variable], *earlier)
        total = add_near(variable, part, nears[variable], table)
        totals.append(total)
        mets.append(lax.ppermute(total, "band", [(1, 2), (2, 1)]))
        return total

    mark = filter_one(0)
    mark = filter_one(1, mark)
    mark = cross_one(0, mark)
    exits = lax.all_to_all(after(exits, mark), "sub", split_axis=0, concat_axis=0, tiled=True)
    mark = cross_one(1, mark)
    mark = filter_one(2, mark)
    mark = filter_one(3, mark)
    mark = cross_one(2, mark)
    mark = cross_one(3, mark)
    messages = lax.all_to_all(
        chain(after(exits, mark)), "sub", split_axis=0, concat_axis=0, tiled=True
    )
    fars = [lax.ppermute(met, "band", [(1, 0), (2, 3)]) for met in mets]
    messages = of_all_bands(messages).reshape(8, 4, -1, LANES)
    result = None
    for v in range(4):
        result = last_step(v, owns[v], nears[v], fars[v], mets[v], messages, mix, table, result)
    return result


def prefix(part, axis, combine, identity, reverse):
    count = lax.axis_size(axis)
    place = lax.axis_index(axis)
    ahead = count - 1 - place if reverse else place
    gathered = jax.tree.map(lambda a: lax.all_gather(a, axis), part)
    state = jax.tree.map(lambda a, e: jnp.zeros_like(a) + jnp.asarray(e, a.dtype), part, identity)

    def one(turn, state):
        source = count - 1 - turn if reverse else turn
        return combine(
            state, jax.tree.map(lambda a: lax.dynamic_index_in_dim(a, source, 0, False), gathered)
        )

    return lax.fori_loop(0, ahead, one, state)


def combine(earlier, later):
    return (earlier[0] * later[0], later[0] * earlier[1] + later[1])


def level_chain(values, decays, reverse):
    level_count = values.shape[0]
    visit_order = range(level_count - 1, -1, -1) if reverse else range(level_count)
    carry_state = jnp.zeros_like(values[0])
    level_gain = jnp.ones((values.shape[1],), f32)
    outputs = [None] * level_count
    carried = [None] * level_count
    for level_index in visit_order:
        factor = decays[level_index][:, None, None]
        carry_state = factor * carry_state + (1.0 - factor) * values[level_index]
        level_gain = level_gain * decays[level_index]
        outputs[level_index] = carry_state
        carried[level_index] = level_gain
    total_decay = level_gain[:, None, None]
    identity = (jnp.ones_like(total_decay), jnp.zeros_like(carry_state))
    incoming = prefix((total_decay, carry_state), "band", combine, identity, reverse)[1]
    return jnp.stack(
        [
            outputs[level_index] + carried[level_index][:, None, None] * incoming
            for level_index in range(level_count)
        ]
    )


def any_bands(swept, weights, exits, chain, vert_length):
    column_count, group_count, row_count, _ = swept.shape
    exits = lax.all_to_all(exits, "sub", split_axis=0, concat_axis=0, tiled=True)
    messages = lax.all_to_all(chain(exits), "sub", split_axis=0, concat_axis=0, tiled=True)
    (values,) = longitude(swept, weights, group_count, 0, 1)
    messages = messages.reshape(group_count, -1, LANES)
    states = messages[:, : 4 * column_count].reshape(group_count, 4, -1)
    inside = messages[:, 4 * column_count : 4 * column_count + 4, :row_count]
    values = values + jnp.einsum("gkr,gkc->grc", inside, states, precision=highest)
    decay = jnp.exp(-1.0 / vert_length)
    values = values.reshape(decay.shape + values.shape[1:])
    return level_chain(level_chain(values, decay, False), decay, True)


def per_device(background, obs_columns, obs_owner, obs_cell, lat_length, lon_length, vert_length):
    level_count, var_count, row_count, lon_count = background.shape
    sub_count = lax.axis_size("sub")
    group_count = level_count * var_count
    strip = row_count * lon_count
    column_count = lon_count // LANES
    capacity = 2 * obs_owner.shape[0] // sub_count
    chunk_count = capacity // LANES
    two_chips = lax.axis_size("band") == 4 and level_count == 2
    index = lax.axis_index("sub").astype(i32).reshape(1)
    band = lax.axis_index("band").astype(i32).reshape(1)

    packed = pack_observations(
        obs_columns.reshape(group_count, -1), obs_owner[:, 0], obs_cell, sub_count, strip, capacity
    )
    if two_chips:
        decay = jnp.exp(-1.0 / vert_length).reshape(-1, 1)
        decays = of_all_bands(jnp.broadcast_to(decay, (8, LANES)))
    lengths = lat_length.reshape(group_count, sub_count, row_count)
    lengths = jnp.pad(lengths, ((0, 0), (0, 0), (0, LANES - row_count)), constant_values=1.0)
    got = lax.all_to_all(packed, "sub", split_axis=0, concat_axis=0, tiled=True)
    *weights, inside, leaving = prepare(
        index, after(lon_length.reshape(-1), packed), lengths, row_count, lon_count
    )
    ready = [inside]
    if two_chips:
        table, mix = tables(band, after(decays, packed))
        ready.append(table)

    sizes = (sub_count, group_count, row_count, column_count, chunk_count, strip)
    swept, exits = deposit_and_sweep(
        index,
        lengths,
        after(got, *ready),
        background.reshape(group_count * row_count, lon_count),
        sizes,
    )
    swept = swept.reshape(column_count, group_count, row_count, LANES)
    exits = exits.reshape(group_count, 4 * column_count, LANES)

    def chain(arrived):
        return chain_states(index, arrived, leaving, inside, weights)

    if two_chips:
        return four_bands(swept, weights, exits, chain, table, mix)
    return any_bands(swept, weights, exits, chain, vert_length)


def solution(mesh):
    placed = (
        P("band", None, "sub", None),
        P("band", None, "sub"),
        P("sub", None),
        P("sub"),
        P("band", None, None),
        P("band", None),
        P("band", None),
    )
    return jax.shard_map(
        per_device,
        mesh=mesh,
        in_specs=placed,
        out_specs=P("band", None, "sub", None),
        check_vma=False,
    )
```

```python
import functools

import jax
import jax.numpy as jnp
from jax import lax
from jax.experimental import pallas as pl
from jax.experimental.pallas import tpu as pltpu
from jax.sharding import PartitionSpec as P

f32 = jnp.float32
i32 = jnp.int32
bf16 = jnp.bfloat16
highest = lax.Precision.HIGHEST

LANES = 128
SUBLANES = 8
BLOCK = 256
CHAINS = 4

VMEM = pl.BlockSpec(memory_space=pltpu.VMEM)
SMEM = pl.BlockSpec(memory_space=pltpu.SMEM)
HBM = pl.BlockSpec(memory_space=pltpu.HBM)


def params(mib):
    return pltpu.CompilerParams(vmem_limit_bytes=mib << 20)


def pinned(*arrays):
    return [pltpu.with_memory_space_constraint(array, pltpu.VMEM) for array in arrays]


def in_hbm(*arrays):
    return [pltpu.with_memory_space_constraint(array, pltpu.HBM) for array in arrays]


def exchange(parts, axis):
    count = len(parts)
    moved = [
        lax.ppermute(part, axis, [(at, at ^ k) for at in range(count)])
        for k, part in enumerate(parts)
        if k
    ]
    return list(parts[:1]) + moved


def cost(flops, read):
    return pl.CostEstimate(flops=flops, bytes_accessed=read, transcendentals=0)


def dot(a, b, dims=(((1,), (0,)), ((), ()))):
    return lax.dot_general(a, b, dims, preferred_element_type=f32)


def split(x):
    high = x.astype(bf16)
    return high, (x - high.astype(f32)).astype(bf16)


def pack_kernel(sizes, index, owners, cells, values, *rest):
    outs, (packed, places, tally, sorted_, joined, counts, sem) = rest[:-7], rest[-7:]
    sub_count, group_count, chunk_count, strip = sizes
    block_count = owners.shape[0]
    tiles = group_count // SUBLANES
    lane = lax.broadcasted_iota(i32, (SUBLANES, LANES), 1)
    square = lambda axis: lax.broadcasted_iota(i32, (LANES, LANES), axis)
    owner = owners[...]
    picked = [jnp.where(owner == sub, 1.0, 0.0) for sub in range(sub_count)]
    upto = jnp.where(square(0) <= square(1), 1.0, 0.0).astype(bf16)
    ranks = dot(jnp.concatenate(picked, axis=0).astype(bf16), upto)
    wide = lax.broadcasted_iota(i32, (block_count, LANES), 1)
    place = jnp.zeros((block_count, LANES), f32)
    base = jnp.zeros((block_count, LANES), f32)
    totals = jnp.zeros((block_count, LANES), f32)
    for sub in range(sub_count):
        rank = ranks[sub * block_count : (sub + 1) * block_count]
        total = jnp.broadcast_to(rank[:, LANES - 1 :], rank.shape)
        place = jnp.where(owner == sub, rank - 1.0 + base, place)
        totals = jnp.where(wide == sub, total, totals)
        base = base + total
    places[...] = place.astype(i32)
    tally[...] = totals.astype(i32)
    copy = pltpu.make_async_copy(tally, counts, sem)
    copy.start()
    extra = -(group_count + SUBLANES) % 16
    row = square(0)

    def sort_block(block, carry):
        at = pl.multiple_of(block * LANES, LANES)
        parts = [
            *[values[level, :, pl.ds(at, LANES)] for level in range(values.shape[0])],
            jnp.broadcast_to(cells[pl.ds(block, 1), :], (SUBLANES, LANES)).astype(f32),
        ]
        if extra:
            parts.append(jnp.zeros((extra, LANES), f32))
        whole = jnp.concatenate(parts, axis=0)
        rows = whole.shape[0]
        high, rest = whole.astype(bf16), whole
        rest = rest - high.astype(f32)
        middle = rest.astype(bf16)
        low = (rest - middle.astype(f32)).astype(bf16)
        move = jnp.where(row == places[pl.ds(block, 1), :], 1.0, 0.0).astype(bf16)
        moved = dot(
            jnp.concatenate([high, middle, low], axis=0), move, (((1,), (1,)), ((), ()))
        )
        moved = moved[:rows] + moved[rows : 2 * rows] + moved[2 * rows :]
        for tile in range(tiles + 1):
            sorted_[block, tile] = moved[tile * SUBLANES : (tile + 1) * SUBLANES]
        return carry

    lax.fori_loop(0, block_count, sort_block, 0, unroll=8)
    copy.wait()

    def join_block(block, ends):
        start = jnp.int32(0)
        writes, following = [], []
        for sub in range(sub_count):
            end = ends[sub]
            chunk, offset = lax.shift_right_logical(end, 7), end & 127
            for tile in range(tiles + 1):
                turned = pltpu.roll(sorted_[block, tile], (end - start) & 127, 1)
                kept = jnp.where(lane >= offset, turned, joined[sub, chunk, tile])
                writes.append((sub, chunk, tile, kept, turned))
            start = start + counts[block, sub]
            following.append(end + counts[block, sub])
        for sub, chunk, tile, kept, turned in writes:
            joined[sub, chunk, tile] = kept
            joined[sub, chunk + 1, tile] = turned
        return tuple(following)

    ends = lax.fori_loop(0, block_count, join_block, (jnp.int32(0),) * sub_count, unroll=2)
    word_row = chunk_count * group_count
    word_rows = packed.shape[1] - word_row
    for sub in range(sub_count):
        packed[sub, word_row:, :] = jnp.full((word_rows, LANES), float(strip), f32)
        for chunk in range(chunk_count):
            for tile in range(tiles):
                at = chunk * group_count + tile * SUBLANES
                packed[sub, at : at + SUBLANES, :] = joined[sub, chunk, tile]
            filled = lane + chunk * LANES < ends[sub]
            cell = jnp.where(filled, joined[sub, chunk, tiles], 0.0).astype(i32)
            word = (cell - (cell & 127)) + ((cell - lane) & 127)
            word = jnp.where(filled, word, strip).astype(f32)
            packed[sub, word_row + chunk : word_row + chunk + 1, :] = word[:1]
    for k, out in enumerate(outs):
        out[...] = packed[index[0] ^ k]


def pack_observations(index, obs_values, owners, cells, sub_count, strip, capacity):
    level_count, var_count, obs_count = obs_values.shape
    group_count = level_count * var_count
    chunk_count = capacity // LANES
    block_count = obs_count // LANES
    rows = chunk_count * group_count + SUBLANES * (-(-chunk_count // SUBLANES))
    tiles = group_count // SUBLANES
    return pl.pallas_call(
        functools.partial(pack_kernel, (sub_count, group_count, chunk_count, strip)),
        out_shape=[pltpu.VMEM((rows, LANES), f32)] * sub_count,
        in_specs=[SMEM, VMEM, VMEM, VMEM],
        out_specs=[VMEM] * sub_count,
        scratch_shapes=[
            pltpu.VMEM((sub_count, rows, LANES), f32),
            pltpu.VMEM((block_count, LANES), i32),
            pltpu.VMEM((block_count, LANES), i32),
            pltpu.VMEM((block_count, tiles + 1, SUBLANES, LANES), f32),
            pltpu.VMEM((sub_count, chunk_count + 2, tiles + 1, SUBLANES, LANES), f32),
            pltpu.SMEM((block_count, LANES), i32),
            pltpu.SemaphoreType.DMA,
        ],
        compiler_params=params(6),
        cost_estimate=cost(10, 10),
    )(index, *in_hbm(owners.reshape(block_count, LANES), cells.reshape(block_count, LANES), obs_values))


def deposit_kernel(sizes, index, lat_length, field, *rest):
    sub_count, group_count, row_count, column_count, chunk_count, strip = sizes
    arrived, swept, leaving = rest[:sub_count], rest[sub_count], rest[sub_count + 1 :][:sub_count]
    got, exits, loaded, *rest = rest[2 * sub_count + 1 :]
    totals, (decay, integers, words, word_sem, sems) = rest[:CHAINS], rest[CHAINS:]
    tiles = group_count // SUBLANES
    word_row = chunk_count * group_count
    word_rows = got.shape[1] - word_row
    span = row_count * column_count

    def load(group):
        return pltpu.make_async_copy(field.at[group], loaded.at[group], sems.at[group])

    for group in range(group_count):
        load(group).start()
    for source in range(sub_count):
        got[source] = arrived[source][...]
        integers[source * word_rows : (source + 1) * word_rows, :] = arrived[source][
            word_row:, :
        ].astype(i32)
    hand_over = pltpu.make_async_copy(integers, words, word_sem)
    hand_over.start()
    here = index[0] * row_count
    for tile in range(tiles):
        lengths = jnp.concatenate(
            [lat_length[2 * tile + k].astype(f32) for k in range(SUBLANES // 4)], axis=0
        )
        lengths = pltpu.roll(lengths, jnp.where(here > 0, lengths.shape[1] - here, 0), 1)
        keep = jnp.exp(-1.0 / lengths[:, :LANES])
        for row in range(row_count):
            decay[row, tile] = jnp.broadcast_to(keep[:, row : row + 1], (SUBLANES, LANES))

    def clear(row, carry):
        for total in totals:
            for tile in range(tiles):
                for column in range(column_count):
                    total[tile, row, column] = jnp.zeros((SUBLANES, LANES), f32)
        return carry

    lax.fori_loop(0, row_count, clear, 0)
    lane = lax.broadcasted_iota(i32, (SUBLANES, LANES), 1)
    hand_over.wait()

    def one_source(source, carry):
        first = source * word_rows

        def more(chunk):
            last = jnp.minimum(chunk, chunk_count - 1)
            return (chunk < chunk_count) & (words[first + last, 0] < strip)

        def one_chunk(chunk):
            blocks = [
                got[
                    source,
                    pl.ds(pl.multiple_of(chunk * group_count + tile * SUBLANES, 8), SUBLANES),
                    :,
                ]
                for tile in range(tiles)
            ]
            for slot in range(LANES):
                word = words[first + chunk, slot]
                target = lax.shift_right_logical(word, 7)
                turn = word & 127
                for tile in range(tiles):
                    value = pltpu.roll(jnp.where(lane == slot, blocks[tile], 0.0), turn, 1)
                    total = flat[slot % CHAINS]
                    total[tile, target] = total[tile, target] + value
            return chunk + 1

        lax.while_loop(more, one_chunk, jnp.int32(0))
        return carry

    flat = [total.reshape(tiles, -1, SUBLANES, LANES) for total in totals]
    lax.fori_loop(0, sub_count, one_source, 0)
    for group in range(group_count):
        load(group).wait()

    for tile in range(tiles):
        groups = slice(tile * SUBLANES, (tile + 1) * SUBLANES)

        def add_rows(at, carry):
            rows = pl.ds(pl.multiple_of(at * SUBLANES, SUBLANES), SUBLANES)
            for column in range(column_count):
                lanes = slice(column * LANES, (column + 1) * LANES)
                value = jnp.swapaxes(loaded[groups, rows, lanes], 0, 1)
                for total in totals:
                    value = value + total[tile, rows, column]
                totals[0][tile, rows, column] = value
            return carry

        lax.fori_loop(0, row_count // SUBLANES, add_rows, 0)

        def sweep(source, target, turn):
            def one_row(step, state):
                row = row_count - 1 - step if turn % 2 else step
                keep = decay[row, tile]
                take = 1.0 - keep
                following = []
                for column in range(column_count):
                    value = keep * state[column] + take * source[tile, row, column]
                    target[tile, row, column] = value
                    following.append(value)
                return tuple(following)

            nothing = tuple(jnp.zeros((SUBLANES, LANES), f32) for _ in range(column_count))
            state = lax.fori_loop(0, row_count, one_row, nothing, unroll=4)
            message_rows = 4 * column_count
            for column in range(column_count):
                at = tile * SUBLANES * message_rows + turn * column_count + column
                exits[pl.ds(at, SUBLANES, stride=message_rows), :] = state[column]

        for turn in range(4):
            sweep(totals[turn % 2], totals[1 - turn % 2], turn)

        def turn_rows(at, carry):
            rows = pl.ds(pl.multiple_of(at * SUBLANES, SUBLANES), SUBLANES)
            for column in range(column_count):
                swept[column, groups, rows, :] = jnp.swapaxes(totals[0][tile, rows, column], 0, 1)
            return carry

        lax.fori_loop(0, row_count // SUBLANES, turn_rows, 0)
    rows = 4 * column_count
    for k, out in enumerate(leaving):
        out[...] = exits[pl.ds(pl.multiple_of((index[0] ^ k) * rows, SUBLANES), rows), :]


def deposit_and_sweep(index, lat_length, got, field, sizes):
    sub_count, group_count, row_count, column_count, chunk_count, strip = sizes
    tiles = group_count // SUBLANES
    rows = got[0].shape[0]
    word_rows = rows - chunk_count * group_count
    exit_rows = 4 * column_count
    plain = (group_count, row_count, column_count * LANES)
    dump = (tiles, row_count + 1, column_count, SUBLANES, LANES)
    return pl.pallas_call(
        functools.partial(deposit_kernel, sizes),
        out_shape=[
            pltpu.VMEM((column_count, group_count, row_count, LANES), f32),
        ]
        + [pltpu.VMEM((exit_rows, LANES), f32)] * sub_count,
        in_specs=[SMEM, VMEM, HBM] + [VMEM] * sub_count,
        out_specs=[VMEM] * (sub_count + 1),
        scratch_shapes=[
            pltpu.VMEM((sub_count, rows, LANES), f32),
            pltpu.VMEM((group_count * exit_rows, LANES), f32),
            pltpu.VMEM(plain, f32),
        ]
        + [pltpu.VMEM(dump, f32)] * CHAINS
        + [
            pltpu.VMEM((row_count, tiles, SUBLANES, LANES), f32),
            pltpu.VMEM((sub_count * word_rows, LANES), i32),
            pltpu.SMEM((sub_count * word_rows, LANES), i32),
            pltpu.SemaphoreType.DMA,
            pltpu.SemaphoreType.DMA((group_count,)),
        ],
        compiler_params=params(26),
        cost_estimate=cost(10, 10),
    )(index, lat_length, *in_hbm(field), *pinned(*got))


def unit_kernel(sizes, index, lat_length, inside, leaving, decay, held):
    sub_count, row_count = sizes
    group = index[0]
    decay[...] = jnp.zeros(decay.shape, f32)
    lengths = lat_length[group // 4, pl.ds(group % 4, 1), :]
    keep = jnp.exp(-1.0 / lengths)
    for sub in range(sub_count):
        part = keep[:, sub * row_count : (sub + 1) * row_count]
        decay[4 * sub : 4 * sub + 4, :row_count] = jnp.broadcast_to(part, (4, row_count))
    decay[...] = jnp.transpose(decay[...], (1, 0))
    held[...] = jnp.zeros(held.shape, f32)
    state_of = lax.broadcasted_iota(i32, (1, LANES), 1) & 3
    for turn in range(4):

        def one_row(step, state, turn=turn):
            row = row_count - 1 - step if turn % 2 else step
            keep = decay[pl.ds(row, 1), :]
            value = keep * state + (1.0 - keep) * held[pl.ds(row, 1), :]
            held[pl.ds(row, 1), :] = value
            return value

        enter = jnp.where(state_of == turn, 1.0, 0.0)
        state = lax.fori_loop(0, row_count, one_row, enter, unroll=8)
        leaving[turn : turn + 1, :] = state
    inside[...] = jnp.transpose(held[...], (1, 0))


def unit_responses(index, lat_length, sub_count, row_count):
    return pl.pallas_call(
        functools.partial(unit_kernel, (sub_count, row_count)),
        in_specs=[SMEM, VMEM],
        out_specs=[VMEM, VMEM],
        out_shape=[
            pltpu.VMEM((LANES, LANES), f32),
            jax.ShapeDtypeStruct((4, LANES), f32),
        ],
        scratch_shapes=[pltpu.VMEM((LANES, LANES), f32)] * 2,
        compiler_params=params(4),
        cost_estimate=cost(10, 10),
    )(index, lat_length)


def circle_weights(length, block_count, near_high, near_low, moment, spread):
    def ramp(shape, axis):
        return lax.broadcasted_iota(i32, shape, axis)

    def twice(x):
        return jnp.concatenate([x, x], axis=1)

    rate = -1.0 / jnp.full((1, LANES), length, f32)
    decay = jnp.exp(rate)
    gain = ((1.0 - decay) / (1.0 + decay)) ** 2
    centre = (1.0 + decay * decay) / (1.0 - decay * decay)
    turn = jnp.exp(rate * float(BLOCK * block_count))
    lag = float(BLOCK * block_count) * turn / (1.0 - turn)
    full_gain = gain / (1.0 - turn)

    shape = (BLOCK, BLOCK)
    gap = jnp.abs(ramp(shape, 0) - ramp(shape, 1)).astype(f32)
    near = twice(gain) * jnp.exp(twice(rate) * gap) * (gap + twice(centre))
    high, low = split(near)
    near_high[0] = high
    near_low[0] = low
    shape = (BLOCK, LANES)
    kind = ramp(shape, 1) & 3
    spot = ramp(shape, 0)
    far = jnp.where(kind < 2, BLOCK - spot, spot).astype(f32)
    sums = jnp.exp(rate * far) * jnp.where((kind & 1) == 1, far, 1.0)
    high, low = split(sums)
    moment[0, :, :LANES] = high
    moment[0, :, LANES:] = low
    shape = (32, BLOCK)
    kind = ramp(shape, 0) & 3
    block = lax.shift_right_logical(ramp(shape, 0), 2)
    spot = ramp(shape, 1)
    reach = jnp.where(kind < 2, spot, BLOCK - spot).astype(f32)
    for at in range(block_count):
        ahead = jnp.where(kind < 2, at - block, block - at) - 1
        steps = jnp.where(ahead < 0, ahead + block_count, ahead)
        full = reach + (steps * BLOCK).astype(f32)
        weight = twice(full_gain) * jnp.exp(twice(rate) * full)
        lead = full + twice(centre + lag)
        value = jnp.where((kind & 1) == 1, weight, weight * lead)
        value = jnp.where(block < block_count, value, 0.0)
        high, low = split(value)
        spread[0, :32, at * BLOCK : (at + 1) * BLOCK] = high
        spread[0, 32:, at * BLOCK : (at + 1) * BLOCK] = low


def weight_kernel(block_count, lon_length, *outs):
    group = pl.program_id(0)
    circle_weights(lon_length[group // 4, group % 4], block_count, *outs)


def weight_shapes(column_total):
    return [(BLOCK, BLOCK)] * 3 + [(64, column_total)]


def prepare(lon_length, column_total, space):
    group_count = lon_length.size
    shapes = weight_shapes(column_total)
    return pl.pallas_call(
        functools.partial(weight_kernel, column_total // BLOCK),
        grid=(group_count,),
        in_specs=[SMEM],
        out_specs=[pl.BlockSpec((1,) + shape, lambda i: (i, 0, 0)) for shape in shapes],
        out_shape=[space((group_count,) + shape, bf16) for shape in shapes],
        compiler_params=params(10),
        cost_estimate=cost(10, 10),
    )(lon_length)


def circle(pieces, near_high, near_low, moment, spread):
    row_count = pieces[0].shape[0]
    whole = jnp.concatenate(pieces, axis=0)
    high, low = split(whole)
    near = dot(high, near_high) + dot(low, near_high) + dot(high, near_low)
    sums = dot(high, moment)
    sums = sums[:, :LANES] + sums[:, LANES:] + dot(low, moment[:, :LANES])
    lane = lax.broadcasted_iota(i32, (row_count, LANES), 1)
    slot = lax.shift_right_logical(lane, 2) & 7
    moments = jnp.zeros((row_count, LANES), f32)
    for at in range(len(pieces)):
        part = sums[at * row_count : (at + 1) * row_count]
        moments = jnp.where(slot == at, part, moments)
    rest = moments - moments.astype(bf16).astype(f32)
    moments = jnp.where((lax.shift_right_logical(lane, 5) & 1) == 1, rest, moments).astype(bf16)
    spread = jnp.concatenate([spread[:32], spread[:32], spread[32:], spread[32:]], axis=0)
    far = dot(moments, spread)
    return [
        near[at * row_count : (at + 1) * row_count] + far[:, at * BLOCK : (at + 1) * BLOCK]
        for at in range(len(pieces))
    ]


def longitude_kernel(swept, near_high, near_low, moment, spread, out):
    column_count = swept.shape[0]
    pieces = [
        jnp.concatenate([swept[2 * at, 0], swept[2 * at + 1, 0]], axis=1)
        for at in range(column_count // 2)
    ]
    pieces = circle(pieces, near_high[0], near_low[0], moment[0], spread[0])
    for at, piece in enumerate(pieces):
        out[0, :, at * BLOCK : (at + 1) * BLOCK] = piece


def pair_kernel(variable, swept, near_high, near_low, moment, spread, table, own, sent, part):
    column_count = swept.shape[0]
    for level in range(2):
        group = level * 4 + variable
        pieces = [
            jnp.concatenate([swept[2 * at, group], swept[2 * at + 1, group]], axis=1)
            for at in range(column_count // 2)
        ]
        pieces = circle(
            pieces, near_high[group], near_low[group], moment[group], spread[group]
        )
        for target, first in ((sent, 0), (part, 2)):
            weight = table[variable, first + level : first + level + 1, :]
            weight = jnp.concatenate([weight, weight], axis=1)
            for at, piece in enumerate(pieces):
                spot = slice(at * BLOCK, (at + 1) * BLOCK)
                value = weight * piece
                target[:, spot] = target[:, spot] + value if level else value
        for at, piece in enumerate(pieces):
            own[level, :, at * BLOCK : (at + 1) * BLOCK] = piece


def longitude_pair(variable, swept, weights, table):
    column_count, _, row_count, _ = swept.shape
    shape = (row_count, column_count * LANES)
    return pl.pallas_call(
        functools.partial(pair_kernel, variable),
        in_specs=[VMEM] * 6,
        out_specs=[VMEM] * 3,
        out_shape=[pltpu.VMEM((2,) + shape, f32), pltpu.VMEM(shape, f32), pltpu.VMEM(shape, f32)],
        compiler_params=params(10),
        cost_estimate=cost(10, 10),
    )(*pinned(swept, *weights, table))


def longitude(swept, weights, count, first, stride):
    column_count, _, row_count, _ = swept.shape
    column_total = column_count * LANES

    def of(i):
        return first + stride * i

    in_specs = [
        pl.BlockSpec((column_count, 1, row_count, LANES), lambda i: (0, of(i), 0, 0)),
        pl.BlockSpec((1, BLOCK, BLOCK), lambda i: (of(i), 0, 0)),
        pl.BlockSpec((1, BLOCK, BLOCK), lambda i: (of(i), 0, 0)),
        pl.BlockSpec((1, BLOCK, BLOCK), lambda i: (of(i), 0, 0)),
        pl.BlockSpec((1, 64, column_total), lambda i: (of(i), 0, 0)),
    ]
    out_specs = [pl.BlockSpec((1, row_count, column_total), lambda i: (i, 0, 0))]
    out_shape = [jax.ShapeDtypeStruct((count, row_count, column_total), f32)]
    operands = [swept, *weights]
    return pl.pallas_call(
        longitude_kernel,
        grid=(count,),
        in_specs=in_specs,
        out_specs=out_specs,
        out_shape=out_shape,
        compiler_params=params(14),
        cost_estimate=cost(10, 10),
    )(*operands)


def chain_kernel(sub_count, index, lon_length, leaving, inside, *rest):
    arrived, outs = rest[:sub_count], rest[sub_count : 2 * sub_count]
    exits, out, held, *weights = rest[2 * sub_count :]
    for k, part in enumerate(arrived):
        exits[index[0] ^ k] = part[...]
    column_count = exits.shape[1] // 4
    shape = (column_count, LANES)
    group = index[0]
    circle_weights(lon_length[group // 4, group % 4], column_count // 2, *weights)
    entering = {}
    for turn in range(4):
        order = list(range(sub_count))
        if turn % 2:
            order.reverse()
        state = jnp.zeros(shape, f32)
        for block in order:
            entering[turn, block] = state
            at = (turn * sub_count + block) * column_count
            held[at : at + column_count, :] = state
            state = exits[block, turn * column_count : (turn + 1) * column_count, :]
            for other in range(turn + 1):
                state = state + leaving[turn, block * 4 + other] * entering[other, block]
    pieces = []
    for at in range(column_count // 2):
        pair = [
            held[pl.ds(2 * at + k, 4 * sub_count, stride=column_count), :] for k in range(2)
        ]
        pieces.append(jnp.concatenate(pair, axis=1))
    pieces = circle(pieces, *[weight[0] for weight in weights])
    message_rows = out.shape[0] // sub_count
    for at, piece in enumerate(pieces):
        for k in range(2):
            for turn in range(4):
                place = turn * column_count + 2 * at + k
                out[pl.ds(place, sub_count, stride=message_rows), :] = piece[
                    turn * sub_count : (turn + 1) * sub_count, k * LANES : (k + 1) * LANES
                ]
    for block in range(sub_count):
        at = block * message_rows + 4 * column_count
        out[at : at + 4, :] = inside[block * 4 : (block + 1) * 4, :]
        out[at + 4 : (block + 1) * message_rows, :] = jnp.zeros(
            (message_rows - 4 * column_count - 4, LANES), f32
        )
    for k, target in enumerate(outs):
        at = pl.multiple_of((index[0] ^ k) * message_rows, SUBLANES)
        target[...] = out[pl.ds(at, message_rows), :]


def chain_states(index, lon_length, exits, leaving, inside):
    sub_count = len(exits)
    rows = exits[0].shape[0]
    column_total = rows // 4 * LANES
    message_rows = rows + 8
    return pl.pallas_call(
        functools.partial(chain_kernel, sub_count),
        in_specs=[SMEM, SMEM, SMEM, VMEM] + [VMEM] * sub_count,
        out_specs=[VMEM] * sub_count,
        scratch_shapes=[
            pltpu.VMEM((sub_count, rows, LANES), f32),
            pltpu.VMEM((sub_count * message_rows, LANES), f32),
            pltpu.VMEM((sub_count * rows, LANES), f32),
        ]
        + [pltpu.VMEM((1,) + shape, bf16) for shape in weight_shapes(column_total)],
        out_shape=[pltpu.VMEM((message_rows, LANES), f32)] * sub_count,
        compiler_params=params(16),
        cost_estimate=cost(10, 10),
    )(index, lon_length, leaving, *pinned(inside, *exits))


def gather_kernel(index, *rest):
    *parts, out = rest
    rows = parts[0].shape[0]
    for k, part in enumerate(parts):
        out[pl.ds(pl.multiple_of((index[0] ^ k) * rows, SUBLANES), rows), :] = part[...]


def gather_messages(index, parts):
    rows = parts[0].shape[0]
    return pl.pallas_call(
        gather_kernel,
        in_specs=[SMEM] + [VMEM] * len(parts),
        out_specs=VMEM,
        out_shape=pltpu.VMEM((len(parts) * rows, LANES), f32),
        compiler_params=params(4),
        cost_estimate=cost(10, 10),
    )(index, *pinned(*parts))


def pair_factors(top, low):
    top_take, low_take = 1.0 - top, 1.0 - low
    through = top * low
    sends = (low * top_take, low_take)
    low_out = (low_take * through, low, low_take * low * top_take, low_take * low_take)
    top_out = (
        top * low_out[0] + top_take * top,
        top * low_out[1],
        top * low_out[2] + top_take * top_take,
        top * low_out[3],
    )
    return through, sends, top_out, low_out


def tables_kernel(index, own, across_, beside_, corner_, table, mix, decay):
    band = index[0]
    for at, lengths in enumerate((own, across_, beside_, corner_)):
        for level in range(2):
            for variable in range(4):
                row = at * 8 + level * 4 + variable
                decay[row : row + 1, :] = jnp.full((1, LANES), lengths[level, variable], f32)
    decay[...] = jnp.exp(-1.0 / decay[...])

    def factors(at):
        return pair_factors(decay[at * 8 : at * 8 + 4, :], decay[at * 8 + 4 : at * 8 + 8, :])

    def by_band(*values):
        result = values[0]
        for at in range(1, 4):
            result = jnp.where(band == at, values[at], result)
        return result

    through, sends, top_out, low_out = factors(0)
    across, beside, corner = factors(1), factors(2), factors(3)
    through_n, echo_n = beside[0], beside[2][0]
    third = by_band(across[0], corner[0], across[0], across[0])
    third_echo = by_band(across[2][0], corner[2][0], across[2][0], across[2][0])
    fourth_echo = by_band(corner[2][0], across[2][0], corner[2][0], corner[2][0])
    zeta = third * third * fourth_echo + third_echo
    rows = []
    for i in range(2):
        reply = top_out[2 + i]
        rows.append(by_band(sends[i], reply + through * zeta * sends[i], sends[i], reply))
    for i in range(2):
        rows.append(
            by_band(
                sends[i], sends[i], through * echo_n * sends[i] + top_out[2 + i], sends[i]
            )
        )
    rows.append(through)
    for fin, back, *own in (top_out, low_out):
        for i in range(2):
            rows.append(
                by_band(
                    own[i] + back * (through_n * through_n * zeta + echo_n) * sends[i],
                    own[i] + back * zeta * sends[i],
                    own[i] + back * echo_n * sends[i],
                    own[i],
                )
            )
        none = jnp.zeros_like(fin)
        rows.append(by_band(back, fin + back * zeta * through, back, fin))
        rows.append(by_band(back * through_n, none, none, fin * through_n))
        rows.append(by_band(none, back, fin + back * echo_n * through, none))
    for variable in range(4):
        for at, row in enumerate(rows):
            table[variable, at : at + 1, :] = row[variable : variable + 1]
    row = lax.broadcasted_iota(i32, (SUBLANES, LANES), 0)
    for variable in range(4):
        value = jnp.zeros((SUBLANES, LANES), f32)
        downward, keeps = [], []
        for level in range(8):
            other = (level // 2) ^ band
            place = (other & 1) * 2 + lax.shift_right_logical(other, 1)
            at = place * 8 + (level % 2) * 4 + variable
            keep = jnp.broadcast_to(decay[pl.ds(at, 1), :], (SUBLANES, LANES))
            unit = jnp.where(row == place * 2 + level % 2, 1.0, 0.0)
            value = keep * value + (1.0 - keep) * unit
            downward.append(value)
            keeps.append(keep)
        value = jnp.zeros((SUBLANES, LANES), f32)
        upward = [None] * 8
        for level in reversed(range(8)):
            value = keeps[level] * value + (1.0 - keeps[level]) * downward[level]
            upward[level] = value
        for level in range(2):
            mix[level, variable] = by_band(*[upward[2 * at + level] for at in range(4)])


def tables(index, lengths):
    return pl.pallas_call(
        tables_kernel,
        in_specs=[SMEM] * 5,
        out_specs=[VMEM, VMEM],
        out_shape=[
            jax.ShapeDtypeStruct((4, 16, LANES), f32),
            jax.ShapeDtypeStruct((2, 4, SUBLANES, LANES), f32),
        ],
        scratch_shapes=[pltpu.VMEM((32, LANES), f32)],
        compiler_params=params(4),
        cost_estimate=cost(10, 10),
    )(index, *lengths)


ADD_FLOPS = 10


def add_kernel(variable, part, near, table, total):
    weight = table[variable, 4:5, :]
    for column in range(part.shape[1] // LANES):
        at = slice(column * LANES, (column + 1) * LANES)
        total[:, at] = part[:, at] + weight * near[:, at]


def add_near(variable, part, near, table):
    return pl.pallas_call(
        functools.partial(add_kernel, variable),
        in_specs=[VMEM] * 3,
        out_specs=VMEM,
        out_shape=pltpu.VMEM(part.shape, f32),
        compiler_params=params(4),
        cost_estimate=cost(ADD_FLOPS, 10),
    )(*pinned(part, near, table))


def last_kernel(variable, own, near, far, met, mix, table, *rest):
    out, added, message, sems = rest[-4:]
    row_count, column_total = near.shape
    column_count = column_total // LANES
    stride = message.shape[0] // SUBLANES
    first = 0
    for at, part in enumerate(rest[:4]):
        for level in range(2):
            source = (level * 4 + variable) * stride
            target = (2 * at + level) * stride
            message[target : target + stride, :] = part[source : source + stride, :]
    lanes = []
    for column in range(column_count):
        lanes.append(
            jnp.concatenate(
                [
                    message[pl.ds(first + k * column_count + column, SUBLANES, stride=stride), :]
                    for k in range(4)
                ],
                axis=0,
            )
        )
    high, low = split(jnp.concatenate(lanes, axis=1))
    states = jnp.concatenate([high, high, low, low], axis=0)
    inside = [
        message[pl.ds(first + 4 * column_count + k, SUBLANES, stride=stride), :] for k in range(4)
    ]
    copies = []
    for level in range(2):
        mixed = jnp.concatenate([part * mix[level, variable] for part in inside], axis=0)
        high, low = split(mixed)
        mixed = jnp.concatenate([high, low, high, low], axis=0)
        total = dot(mixed, states, (((0,), (0,)), ((), ())))[:row_count]
        weights = [table[variable, 5 + level * 5 + k : 6 + level * 5 + k, :] for k in range(5)]
        for column in range(column_count):
            at = slice(column * LANES, (column + 1) * LANES)
            value = total[:, at] + weights[0] * own[0, :, at] + weights[1] * own[1, :, at]
            value = value + weights[2] * near[:, at] + weights[3] * far[:, at]
            added[level, :, at] = value + weights[4] * met[:, at]
        copy = pltpu.make_async_copy(added.at[level], out.at[level, variable], sems.at[level])
        copy.start()
        copies.append(copy)
    for copy in copies:
        copy.wait()


def last_step(variable, own, near, far, met, messages, mix, table, so_far):
    _, row_count, column_total = own.shape
    operands = pinned(own, near, far, met, mix, table, *messages)
    in_specs = [VMEM] * 10
    aliases = {}
    if so_far is not None:
        operands.append(so_far)
        in_specs.append(HBM)
        aliases = {10: 0}
    return pl.pallas_call(
        functools.partial(last_kernel, variable),
        in_specs=in_specs,
        out_specs=HBM,
        out_shape=pltpu.HBM((2, 4, row_count, column_total), f32),
        scratch_shapes=[
            pltpu.VMEM((2, row_count, column_total), f32),
            pltpu.VMEM(messages[0].shape, f32),
            pltpu.SemaphoreType.DMA((2,)),
        ],
        input_output_aliases=aliases,
        compiler_params=params(10),
        cost_estimate=cost(10, 10),
    )(*operands)


SWAP = [(0, 1), (1, 0), (2, 3), (3, 2)]
CROSS = [(0, 2), (2, 0), (1, 3), (3, 1)]
CORNER = [(0, 3), (3, 0), (1, 2), (2, 1)]
MIDDLE = [(0, 0), (1, 2), (2, 1), (3, 3)]


def after(value, *earlier):
    return lax.optimization_barrier((value,) + earlier)[0]


def four_bands(swept, weights, exits, chain, gather, table, mix):
    owns, parts, nears, mets = [], [], [], []

    def filter_one(variable, *earlier):
        own, sent, part = longitude_pair(variable, after(swept, *earlier), weights, table)
        owns.append(own)
        parts.append(part)
        nears.append(lax.ppermute(sent, "band", SWAP))
        return part

    def cross_one(variable, *earlier):
        part = after(parts[variable], *earlier)
        total = add_near(variable, part, nears[variable], table)
        mets.append(lax.ppermute(total, "band", MIDDLE))
        return total

    exits = exchange(exits, "sub")
    mark = filter_one(0)
    mark = filter_one(1, mark)
    mark = cross_one(0, mark)
    mark = cross_one(1, mark)
    chained = chain([after(exits[0], mark)] + exits[1:])
    messages = exchange(chained, "sub")
    mark = filter_one(2, chained[0])
    mark = filter_one(3, mark)
    mark = cross_one(2, mark, mets[0])
    mark = cross_one(3, mark)
    messages = gather(messages, mark)
    across = lax.ppermute(messages, "band", CROSS)
    beside = lax.ppermute(messages, "band", SWAP)
    corner = lax.ppermute(across, "band", SWAP)
    messages = (messages, across, beside, corner)
    fars = [lax.ppermute(met, "band", SWAP) for met in mets]
    result = None
    for v in range(4):
        result = last_step(v, owns[v], nears[v], fars[v], mets[v], messages, mix, table, result)
    return result


def prefix(part, axis, combine, identity, reverse):
    count = lax.axis_size(axis)
    place = lax.axis_index(axis)
    ahead = count - 1 - place if reverse else place
    gathered = jax.tree.map(lambda a: lax.all_gather(a, axis), part)
    state = jax.tree.map(lambda a, e: jnp.zeros_like(a) + jnp.asarray(e, a.dtype), part, identity)

    def one(turn, state):
        source = count - 1 - turn if reverse else turn
        return combine(
            state, jax.tree.map(lambda a: lax.dynamic_index_in_dim(a, source, 0, False), gathered)
        )

    return lax.fori_loop(0, ahead, one, state)


def combine(earlier, later):
    return (earlier[0] * later[0], later[0] * earlier[1] + later[1])


def level_chain(values, decays, reverse):
    level_count = values.shape[0]
    visit_order = range(level_count - 1, -1, -1) if reverse else range(level_count)
    carry_state = jnp.zeros_like(values[0])
    level_gain = jnp.ones((values.shape[1],), f32)
    outputs = [None] * level_count
    carried = [None] * level_count
    for level_index in visit_order:
        factor = decays[level_index][:, None, None]
        carry_state = factor * carry_state + (1.0 - factor) * values[level_index]
        level_gain = level_gain * decays[level_index]
        outputs[level_index] = carry_state
        carried[level_index] = level_gain
    total_decay = level_gain[:, None, None]
    identity = (jnp.ones_like(total_decay), jnp.zeros_like(carry_state))
    incoming = prefix((total_decay, carry_state), "band", combine, identity, reverse)[1]
    return jnp.stack(
        [
            outputs[level_index] + carried[level_index][:, None, None] * incoming
            for level_index in range(level_count)
        ]
    )


def any_bands(swept, weights, exits, chain, gather, vert_length):
    column_count, group_count, row_count, _ = swept.shape
    messages = gather(exchange(chain(exchange(exits, "sub")), "sub"))
    (values,) = longitude(swept, weights, group_count, 0, 1)
    messages = messages.reshape(group_count, -1, LANES)
    states = messages[:, : 4 * column_count].reshape(group_count, 4, -1)
    inside = messages[:, 4 * column_count : 4 * column_count + 4, :row_count]
    values = values + jnp.einsum("gkr,gkc->grc", inside, states, precision=highest)
    decay = jnp.exp(-1.0 / vert_length)
    values = values.reshape(decay.shape + values.shape[1:])
    return level_chain(level_chain(values, decay, False), decay, True)


def per_device(background, obs_columns, obs_owner, obs_cell, lat_length, lon_length, vert_length):
    level_count, var_count, row_count, lon_count = background.shape
    sub_count = lax.axis_size("sub")
    group_count = level_count * var_count
    strip = row_count * lon_count
    column_count = lon_count // LANES
    capacity = 2 * obs_owner.shape[0] // sub_count
    chunk_count = capacity // LANES
    two_chips = lax.axis_size("band") == 4 and level_count == 2
    index = lax.axis_index("sub").astype(i32).reshape(1)
    band = lax.axis_index("band").astype(i32).reshape(1)

    if two_chips:
        vert_lengths = [vert_length] + [
            lax.ppermute(vert_length, "band", pairs) for pairs in (CROSS, SWAP, CORNER)
        ]
    packed = pack_observations(
        after(index, band),
        obs_columns, obs_owner[:, 0], obs_cell, sub_count, strip, capacity
    )
    got = exchange(packed, "sub")
    space = pltpu.VMEM if two_chips else pltpu.HBM
    weights = prepare(after(lon_length, packed[0]), lon_count, space)
    ready = list(weights)
    if two_chips:
        table, mix = tables(after(band, packed[0]), vert_lengths)
        ready.append(table)

    sizes = (sub_count, group_count, row_count, column_count, chunk_count, strip)
    swept, *exits = deposit_and_sweep(
        index,
        lat_length,
        [after(got[0], *ready)] + got[1:],
        background.reshape(group_count, row_count, lon_count),
        sizes,
    )

    def chain(arrived):
        inside, leaving = unit_responses(
            after(index, swept), lat_length, sub_count, row_count
        )
        return chain_states(index, lon_length, arrived, leaving, inside)

    def gather(parts, *earlier):
        return gather_messages(after(index, *earlier), parts)

    if two_chips:
        return four_bands(swept, weights, exits, chain, gather, table, mix)
    return any_bands(swept, weights, exits, chain, gather, vert_length)


def solution(mesh):
    placed = (
        P("band", None, "sub", None),
        P("band", None, "sub"),
        P("sub", None),
        P("sub"),
        P("band", None, None),
        P("band", None),
        P("band", None),
    )
    return jax.shard_map(
        per_device,
        mesh=mesh,
        in_specs=placed,
        out_specs=P("band", None, "sub", None),
        check_vma=False,
    )
```

```python
import functools

import jax
import jax.numpy as jnp
from jax import lax
from jax.experimental import pallas as pl
from jax.experimental.pallas import tpu as pltpu
from jax.sharding import PartitionSpec as P

f32 = jnp.float32
i32 = jnp.int32
bf16 = jnp.bfloat16
highest = lax.Precision.HIGHEST

LANES = 128
SUBLANES = 8
BLOCK = 256
CHAINS = 4

VMEM = pl.BlockSpec(memory_space=pltpu.VMEM)
SMEM = pl.BlockSpec(memory_space=pltpu.SMEM)
HBM = pl.BlockSpec(memory_space=pltpu.HBM)


def params(mib):
    return pltpu.CompilerParams(vmem_limit_bytes=mib << 20)


def pinned(*arrays):
    return [pltpu.with_memory_space_constraint(array, pltpu.VMEM) for array in arrays]


def in_hbm(*arrays):
    return [pltpu.with_memory_space_constraint(array, pltpu.HBM) for array in arrays]


def exchange(parts, axis):
    count = len(parts)
    moved = [
        lax.ppermute(part, axis, [(at, at ^ k) for at in range(count)])
        for k, part in enumerate(parts)
        if k
    ]
    return list(parts[:1]) + moved


def cost(flops, read):
    return pl.CostEstimate(flops=flops, bytes_accessed=read, transcendentals=0)


def dot(a, b, dims=(((1,), (0,)), ((), ()))):
    return lax.dot_general(a, b, dims, preferred_element_type=f32)


def split(x):
    high = x.astype(bf16)
    return high, (x - high.astype(f32)).astype(bf16)


def pack_kernel(sizes, index, owners, cells, values, *rest):
    outs, (packed, places, tally, sorted_, joined, counts, sem) = rest[:-7], rest[-7:]
    sub_count, group_count, chunk_count, strip = sizes
    block_count = owners.shape[0]
    tiles = group_count // SUBLANES
    lane = lax.broadcasted_iota(i32, (SUBLANES, LANES), 1)
    square = lambda axis: lax.broadcasted_iota(i32, (LANES, LANES), axis)
    owner = owners[...]
    picked = [jnp.where(owner == sub, 1.0, 0.0) for sub in range(sub_count)]
    upto = jnp.where(square(0) <= square(1), 1.0, 0.0).astype(bf16)
    ranks = dot(jnp.concatenate(picked, axis=0).astype(bf16), upto)
    wide = lax.broadcasted_iota(i32, (block_count, LANES), 1)
    place = jnp.zeros((block_count, LANES), f32)
    base = jnp.zeros((block_count, LANES), f32)
    totals = jnp.zeros((block_count, LANES), f32)
    for sub in range(sub_count):
        rank = ranks[sub * block_count : (sub + 1) * block_count]
        total = jnp.broadcast_to(rank[:, LANES - 1 :], rank.shape)
        place = jnp.where(owner == sub, rank - 1.0 + base, place)
        totals = jnp.where(wide == sub, total, totals)
        base = base + total
    places[...] = place.astype(i32)
    tally[...] = totals.astype(i32)
    copy = pltpu.make_async_copy(tally, counts, sem)
    copy.start()
    extra = -(group_count + SUBLANES) % 16
    row = square(0)

    def sort_block(block, carry):
        at = pl.multiple_of(block * LANES, LANES)
        parts = [
            *[values[level, :, pl.ds(at, LANES)] for level in range(values.shape[0])],
            jnp.broadcast_to(cells[pl.ds(block, 1), :], (SUBLANES, LANES)).astype(f32),
        ]
        if extra:
            parts.append(jnp.zeros((extra, LANES), f32))
        whole = jnp.concatenate(parts, axis=0)
        rows = whole.shape[0]
        high, rest = whole.astype(bf16), whole
        rest = rest - high.astype(f32)
        middle = rest.astype(bf16)
        low = (rest - middle.astype(f32)).astype(bf16)
        move = jnp.where(row == places[pl.ds(block, 1), :], 1.0, 0.0).astype(bf16)
        moved = dot(
            jnp.concatenate([high, middle, low], axis=0), move, (((1,), (1,)), ((), ()))
        )
        moved = moved[:rows] + moved[rows : 2 * rows] + moved[2 * rows :]
        for tile in range(tiles + 1):
            sorted_[block, tile] = moved[tile * SUBLANES : (tile + 1) * SUBLANES]
        return carry

    lax.fori_loop(0, block_count, sort_block, 0, unroll=8)
    copy.wait()

    def join_block(block, ends):
        start = jnp.int32(0)
        writes, following = [], []
        for sub in range(sub_count):
            end = ends[sub]
            chunk, offset = lax.shift_right_logical(end, 7), end & 127
            for tile in range(tiles + 1):
                turned = pltpu.roll(sorted_[block, tile], (end - start) & 127, 1)
                kept = jnp.where(lane >= offset, turned, joined[sub, chunk, tile])
                writes.append((sub, chunk, tile, kept, turned))
            start = start + counts[block, sub]
            following.append(end + counts[block, sub])
        for sub, chunk, tile, kept, turned in writes:
            joined[sub, chunk, tile] = kept
            joined[sub, chunk + 1, tile] = turned
        return tuple(following)

    ends = lax.fori_loop(0, block_count, join_block, (jnp.int32(0),) * sub_count, unroll=2)
    word_row = chunk_count * group_count
    word_rows = packed.shape[1] - word_row
    for sub in range(sub_count):
        packed[sub, word_row:, :] = jnp.full((word_rows, LANES), float(strip), f32)
        for chunk in range(chunk_count):
            for tile in range(tiles):
                at = chunk * group_count + tile * SUBLANES
                packed[sub, at : at + SUBLANES, :] = joined[sub, chunk, tile]
            filled = lane + chunk * LANES < ends[sub]
            cell = jnp.where(filled, joined[sub, chunk, tiles], 0.0).astype(i32)
            word = (cell - (cell & 127)) + ((cell - lane) & 127)
            word = jnp.where(filled, word, strip).astype(f32)
            packed[sub, word_row + chunk : word_row + chunk + 1, :] = word[:1]
    for k, out in enumerate(outs):
        out[...] = packed[index[0] ^ k]


def pack_observations(index, obs_values, owners, cells, sub_count, strip, capacity):
    level_count, var_count, obs_count = obs_values.shape
    group_count = level_count * var_count
    chunk_count = capacity // LANES
    block_count = obs_count // LANES
    rows = chunk_count * group_count + SUBLANES * (-(-chunk_count // SUBLANES))
    tiles = group_count // SUBLANES
    return pl.pallas_call(
        functools.partial(pack_kernel, (sub_count, group_count, chunk_count, strip)),
        out_shape=[pltpu.VMEM((rows, LANES), f32)] * sub_count,
        in_specs=[SMEM, VMEM, VMEM, VMEM],
        out_specs=[VMEM] * sub_count,
        scratch_shapes=[
            pltpu.VMEM((sub_count, rows, LANES), f32),
            pltpu.VMEM((block_count, LANES), i32),
            pltpu.VMEM((block_count, LANES), i32),
            pltpu.VMEM((block_count, tiles + 1, SUBLANES, LANES), f32),
            pltpu.VMEM((sub_count, chunk_count + 2, tiles + 1, SUBLANES, LANES), f32),
            pltpu.SMEM((block_count, LANES), i32),
            pltpu.SemaphoreType.DMA,
        ],
        compiler_params=params(6),
        cost_estimate=cost(10, 10),
    )(index, *in_hbm(owners.reshape(block_count, LANES), cells.reshape(block_count, LANES), obs_values))


def deposit_kernel(sizes, index, lat_length, field, *rest):
    sub_count, group_count, row_count, column_count, chunk_count, strip = sizes
    arrived, swept, leaving = rest[:sub_count], rest[sub_count], rest[sub_count + 1 :][:sub_count]
    got, exits, loaded, all_lengths, length_sem, *rest = rest[2 * sub_count + 1 :]
    totals, (decay, integers, words, word_sem, sems) = rest[:CHAINS], rest[CHAINS:]
    tiles = group_count // SUBLANES
    word_row = chunk_count * group_count
    word_rows = got.shape[1] - word_row
    span = row_count * column_count

    def load(group):
        return pltpu.make_async_copy(field.at[group], loaded.at[group], sems.at[group])

    for group in range(group_count):
        load(group).start()
    fetch = pltpu.make_async_copy(lat_length, all_lengths, length_sem)
    fetch.start()
    for source in range(sub_count):
        got[source] = arrived[source][...]
        integers[source * word_rows : (source + 1) * word_rows, :] = arrived[source][
            word_row:, :
        ].astype(i32)
    hand_over = pltpu.make_async_copy(integers, words, word_sem)
    hand_over.start()
    def clear(row, carry):
        for total in totals:
            for tile in range(tiles):
                for column in range(column_count):
                    total[tile, row, column] = jnp.zeros((SUBLANES, LANES), f32)
        return carry

    lax.fori_loop(0, row_count, clear, 0)
    lane = lax.broadcasted_iota(i32, (SUBLANES, LANES), 1)
    hand_over.wait()

    def one_source(source, carry):
        first = source * word_rows

        def more(chunk):
            last = jnp.minimum(chunk, chunk_count - 1)
            return (chunk < chunk_count) & (words[first + last, 0] < strip)

        def one_chunk(chunk):
            blocks = [
                got[
                    source,
                    pl.ds(pl.multiple_of(chunk * group_count + tile * SUBLANES, 8), SUBLANES),
                    :,
                ]
                for tile in range(tiles)
            ]
            for slot in range(LANES):
                word = words[first + chunk, slot]
                target = lax.shift_right_logical(word, 7)
                turn = word & 127
                for tile in range(tiles):
                    value = pltpu.roll(jnp.where(lane == slot, blocks[tile], 0.0), turn, 1)
                    total = flat[slot % CHAINS]
                    total[tile, target] = total[tile, target] + value
            return chunk + 1

        lax.while_loop(more, one_chunk, jnp.int32(0))
        return carry

    flat = [total.reshape(tiles, -1, SUBLANES, LANES) for total in totals]
    lax.fori_loop(0, sub_count, one_source, 0)
    fetch.wait()
    here = index[0] * row_count
    for tile in range(tiles):
        lengths = jnp.concatenate(
            [all_lengths[2 * tile + k] for k in range(SUBLANES // 4)], axis=0
        )
        lengths = pltpu.roll(lengths, jnp.where(here > 0, lengths.shape[1] - here, 0), 1)
        keep = jnp.exp(-1.0 / lengths[:, :LANES])
        for row in range(row_count):
            decay[row, tile] = jnp.broadcast_to(keep[:, row : row + 1], (SUBLANES, LANES))

    for group in range(group_count):
        load(group).wait()


    for tile in range(tiles):
        groups = slice(tile * SUBLANES, (tile + 1) * SUBLANES)

        def add_rows(at, carry):
            rows = pl.ds(pl.multiple_of(at * SUBLANES, SUBLANES), SUBLANES)
            for column in range(column_count):
                lanes = slice(column * LANES, (column + 1) * LANES)
                value = jnp.swapaxes(loaded[groups, rows, lanes], 0, 1)
                for total in totals:
                    value = value + total[tile, rows, column]
                totals[0][tile, rows, column] = value
            return carry

        lax.fori_loop(0, row_count // SUBLANES, add_rows, 0)

        def sweep(source, target, turn):
            def one_row(step, state):
                row = row_count - 1 - step if turn % 2 else step
                keep = decay[row, tile]
                take = 1.0 - keep
                following = []
                for column in range(column_count):
                    value = keep * state[column] + take * source[tile, row, column]
                    target[tile, row, column] = value
                    following.append(value)
                return tuple(following)

            nothing = tuple(jnp.zeros((SUBLANES, LANES), f32) for _ in range(column_count))
            state = lax.fori_loop(0, row_count, one_row, nothing, unroll=4)
            message_rows = 4 * column_count
            for column in range(column_count):
                at = tile * SUBLANES * message_rows + turn * column_count + column
                exits[pl.ds(at, SUBLANES, stride=message_rows), :] = state[column]

        for turn in range(4):
            sweep(totals[turn % 2], totals[1 - turn % 2], turn)

        def turn_rows(at, carry):
            rows = pl.ds(pl.multiple_of(at * SUBLANES, SUBLANES), SUBLANES)
            for column in range(column_count):
                swept[column, groups, rows, :] = jnp.swapaxes(totals[0][tile, rows, column], 0, 1)
            return carry

        lax.fori_loop(0, row_count // SUBLANES, turn_rows, 0)
    rows = 4 * column_count
    for k, out in enumerate(leaving):
        out[...] = exits[pl.ds(pl.multiple_of((index[0] ^ k) * rows, SUBLANES), rows), :]


def deposit_and_sweep(index, lat_length, got, field, sizes):
    sub_count, group_count, row_count, column_count, chunk_count, strip = sizes
    tiles = group_count // SUBLANES
    rows = got[0].shape[0]
    word_rows = rows - chunk_count * group_count
    exit_rows = 4 * column_count
    plain = (group_count, row_count, column_count * LANES)
    dump = (tiles, row_count + 1, column_count, SUBLANES, LANES)
    return pl.pallas_call(
        functools.partial(deposit_kernel, sizes),
        out_shape=[
            pltpu.VMEM((column_count, group_count, row_count, LANES), f32),
        ]
        + [pltpu.VMEM((exit_rows, LANES), f32)] * sub_count,
        in_specs=[SMEM, HBM, HBM] + [VMEM] * sub_count,
        out_specs=[VMEM] * (sub_count + 1),
        scratch_shapes=[
            pltpu.VMEM((sub_count, rows, LANES), f32),
            pltpu.VMEM((group_count * exit_rows, LANES), f32),
            pltpu.VMEM(plain, f32),
            pltpu.VMEM(lat_length.shape, f32),
            pltpu.SemaphoreType.DMA,
        ]
        + [pltpu.VMEM(dump, f32)] * CHAINS
        + [
            pltpu.VMEM((row_count, tiles, SUBLANES, LANES), f32),
            pltpu.VMEM((sub_count * word_rows, LANES), i32),
            pltpu.SMEM((sub_count * word_rows, LANES), i32),
            pltpu.SemaphoreType.DMA,
            pltpu.SemaphoreType.DMA((group_count,)),
        ],
        compiler_params=params(26),
        cost_estimate=cost(10, 10),
    )(index, *in_hbm(lat_length, field), *pinned(*got))


def unit_kernel(sizes, index, lat_length, inside, leaving, decay, held):
    sub_count, row_count = sizes
    group = index[0]
    decay[...] = jnp.zeros(decay.shape, f32)
    lengths = lat_length[group // 4, pl.ds(group % 4, 1), :]
    keep = jnp.exp(-1.0 / lengths)
    for sub in range(sub_count):
        part = keep[:, sub * row_count : (sub + 1) * row_count]
        decay[4 * sub : 4 * sub + 4, :row_count] = jnp.broadcast_to(part, (4, row_count))
    decay[...] = jnp.transpose(decay[...], (1, 0))
    held[...] = jnp.zeros(held.shape, f32)
    state_of = lax.broadcasted_iota(i32, (1, LANES), 1) & 3
    for turn in range(4):

        def one_row(step, state, turn=turn):
            row = row_count - 1 - step if turn % 2 else step
            keep = decay[pl.ds(row, 1), :]
            value = keep * state + (1.0 - keep) * held[pl.ds(row, 1), :]
            held[pl.ds(row, 1), :] = value
            return value

        enter = jnp.where(state_of == turn, 1.0, 0.0)
        state = lax.fori_loop(0, row_count, one_row, enter, unroll=8)
        leaving[turn : turn + 1, :] = state
    inside[...] = jnp.transpose(held[...], (1, 0))


def unit_responses(index, lat_length, sub_count, row_count):
    return pl.pallas_call(
        functools.partial(unit_kernel, (sub_count, row_count)),
        in_specs=[SMEM, VMEM],
        out_specs=[VMEM, VMEM],
        out_shape=[
            pltpu.VMEM((LANES, LANES), f32),
            jax.ShapeDtypeStruct((4, LANES), f32),
        ],
        scratch_shapes=[pltpu.VMEM((LANES, LANES), f32)] * 2,
        compiler_params=params(4),
        cost_estimate=cost(10, 10),
    )(index, lat_length)


def circle_weights(length, block_count, near_high, near_low, moment, spread):
    def ramp(shape, axis):
        return lax.broadcasted_iota(i32, shape, axis)

    def twice(x):
        return jnp.concatenate([x, x], axis=1)

    rate = -1.0 / jnp.full((1, LANES), length, f32)
    decay = jnp.exp(rate)
    gain = ((1.0 - decay) / (1.0 + decay)) ** 2
    centre = (1.0 + decay * decay) / (1.0 - decay * decay)
    turn = jnp.exp(rate * float(BLOCK * block_count))
    lag = float(BLOCK * block_count) * turn / (1.0 - turn)
    full_gain = gain / (1.0 - turn)

    shape = (BLOCK, BLOCK)
    gap = jnp.abs(ramp(shape, 0) - ramp(shape, 1)).astype(f32)
    near = twice(gain) * jnp.exp(twice(rate) * gap) * (gap + twice(centre))
    high, low = split(near)
    near_high[0] = high
    near_low[0] = low
    shape = (BLOCK, LANES)
    kind = ramp(shape, 1) & 3
    spot = ramp(shape, 0)
    far = jnp.where(kind < 2, BLOCK - spot, spot).astype(f32)
    sums = jnp.exp(rate * far) * jnp.where((kind & 1) == 1, far, 1.0)
    high, low = split(sums)
    moment[0, :, :LANES] = high
    moment[0, :, LANES:] = low
    shape = (32, BLOCK)
    kind = ramp(shape, 0) & 3
    block = lax.shift_right_logical(ramp(shape, 0), 2)
    spot = ramp(shape, 1)
    reach = jnp.where(kind < 2, spot, BLOCK - spot).astype(f32)
    for at in range(block_count):
        ahead = jnp.where(kind < 2, at - block, block - at) - 1
        steps = jnp.where(ahead < 0, ahead + block_count, ahead)
        full = reach + (steps * BLOCK).astype(f32)
        weight = twice(full_gain) * jnp.exp(twice(rate) * full)
        lead = full + twice(centre + lag)
        value = jnp.where((kind & 1) == 1, weight, weight * lead)
        value = jnp.where(block < block_count, value, 0.0)
        high, low = split(value)
        spread[0, :32, at * BLOCK : (at + 1) * BLOCK] = high
        spread[0, 32:, at * BLOCK : (at + 1) * BLOCK] = low


def weight_kernel(block_count, lon_length, *outs):
    group = pl.program_id(0)
    circle_weights(lon_length[group // 4, group % 4], block_count, *outs)


def weight_shapes(column_total):
    return [(BLOCK, BLOCK)] * 3 + [(64, column_total)]


def prepare(lon_length, column_total, space):
    group_count = lon_length.size
    shapes = weight_shapes(column_total)
    return pl.pallas_call(
        functools.partial(weight_kernel, column_total // BLOCK),
        grid=(group_count,),
        in_specs=[SMEM],
        out_specs=[pl.BlockSpec((1,) + shape, lambda i: (i, 0, 0)) for shape in shapes],
        out_shape=[space((group_count,) + shape, bf16) for shape in shapes],
        compiler_params=params(10),
        cost_estimate=cost(10, 10),
    )(lon_length)


def circle(pieces, near_high, near_low, moment, spread):
    row_count = pieces[0].shape[0]
    whole = jnp.concatenate(pieces, axis=0)
    high, low = split(whole)
    near = dot(high, near_high) + dot(low, near_high) + dot(high, near_low)
    sums = dot(high, moment)
    sums = sums[:, :LANES] + sums[:, LANES:] + dot(low, moment[:, :LANES])
    lane = lax.broadcasted_iota(i32, (row_count, LANES), 1)
    slot = lax.shift_right_logical(lane, 2) & 7
    moments = jnp.zeros((row_count, LANES), f32)
    for at in range(len(pieces)):
        part = sums[at * row_count : (at + 1) * row_count]
        moments = jnp.where(slot == at, part, moments)
    rest = moments - moments.astype(bf16).astype(f32)
    moments = jnp.where((lax.shift_right_logical(lane, 5) & 1) == 1, rest, moments).astype(bf16)
    spread = jnp.concatenate([spread[:32], spread[:32], spread[32:], spread[32:]], axis=0)
    far = dot(moments, spread)
    return [
        near[at * row_count : (at + 1) * row_count] + far[:, at * BLOCK : (at + 1) * BLOCK]
        for at in range(len(pieces))
    ]


def longitude_kernel(swept, near_high, near_low, moment, spread, out):
    column_count = swept.shape[0]
    pieces = [
        jnp.concatenate([swept[2 * at, 0], swept[2 * at + 1, 0]], axis=1)
        for at in range(column_count // 2)
    ]
    pieces = circle(pieces, near_high[0], near_low[0], moment[0], spread[0])
    for at, piece in enumerate(pieces):
        out[0, :, at * BLOCK : (at + 1) * BLOCK] = piece


def pair_kernel(variables, swept, near_high, near_low, moment, spread, table, own, sent, part):
    column_count = swept.shape[0]
    for place, variable in enumerate(variables):
        for level in range(2):
            group = level * 4 + variable
            pieces = [
                jnp.concatenate([swept[2 * at, group], swept[2 * at + 1, group]], axis=1)
                for at in range(column_count // 2)
            ]
            pieces = circle(
                pieces, near_high[group], near_low[group], moment[group], spread[group]
            )
            for target, first in ((sent, 0), (part, 2)):
                weight = table[variable, first + level : first + level + 1, :]
                weight = jnp.concatenate([weight, weight], axis=1)
                for at, piece in enumerate(pieces):
                    spot = slice(at * BLOCK, (at + 1) * BLOCK)
                    value = weight * piece
                    target[place, :, spot] = target[place, :, spot] + value if level else value
            for at, piece in enumerate(pieces):
                own[place, level, :, at * BLOCK : (at + 1) * BLOCK] = piece


def longitude_pair(variables, swept, weights, table):
    column_count, _, row_count, _ = swept.shape
    shape = (row_count, column_count * LANES)
    count = len(variables)
    return pl.pallas_call(
        functools.partial(pair_kernel, variables),
        in_specs=[VMEM] * 6,
        out_specs=[VMEM] * 3,
        out_shape=[
            pltpu.VMEM((count, 2) + shape, f32),
            pltpu.VMEM((count,) + shape, f32),
            pltpu.VMEM((count,) + shape, f32),
        ],
        compiler_params=params(10),
        cost_estimate=cost(10, 10),
    )(*pinned(swept, *weights, table))


def longitude(swept, weights, count, first, stride):
    column_count, _, row_count, _ = swept.shape
    column_total = column_count * LANES

    def of(i):
        return first + stride * i

    in_specs = [
        pl.BlockSpec((column_count, 1, row_count, LANES), lambda i: (0, of(i), 0, 0)),
        pl.BlockSpec((1, BLOCK, BLOCK), lambda i: (of(i), 0, 0)),
        pl.BlockSpec((1, BLOCK, BLOCK), lambda i: (of(i), 0, 0)),
        pl.BlockSpec((1, BLOCK, BLOCK), lambda i: (of(i), 0, 0)),
        pl.BlockSpec((1, 64, column_total), lambda i: (of(i), 0, 0)),
    ]
    out_specs = [pl.BlockSpec((1, row_count, column_total), lambda i: (i, 0, 0))]
    out_shape = [jax.ShapeDtypeStruct((count, row_count, column_total), f32)]
    operands = [swept, *weights]
    return pl.pallas_call(
        longitude_kernel,
        grid=(count,),
        in_specs=in_specs,
        out_specs=out_specs,
        out_shape=out_shape,
        compiler_params=params(14),
        cost_estimate=cost(10, 10),
    )(*operands)


def chain_kernel(sub_count, layout, index, lon_length, leaving, inside, *rest):
    arrived, outs = rest[:sub_count], rest[sub_count:][: len(layout)]
    exits, out, held, *weights = rest[sub_count + len(layout) :]
    for k, part in enumerate(arrived):
        exits[index[0] ^ k] = part[...]
    column_count = exits.shape[1] // 4
    shape = (column_count, LANES)
    group = index[0]
    circle_weights(lon_length[group // 4, group % 4], column_count // 2, *weights)
    entering = {}
    for turn in range(4):
        order = list(range(sub_count))
        if turn % 2:
            order.reverse()
        state = jnp.zeros(shape, f32)
        for block in order:
            entering[turn, block] = state
            at = (turn * sub_count + block) * column_count
            held[at : at + column_count, :] = state
            state = exits[block, turn * column_count : (turn + 1) * column_count, :]
            for other in range(turn + 1):
                state = state + leaving[turn, block * 4 + other] * entering[other, block]
    pieces = []
    for at in range(column_count // 2):
        pair = [
            held[pl.ds(2 * at + k, 4 * sub_count, stride=column_count), :] for k in range(2)
        ]
        pieces.append(jnp.concatenate(pair, axis=1))
    pieces = circle(pieces, *[weight[0] for weight in weights])
    message_rows = out.shape[0] // sub_count
    for at, piece in enumerate(pieces):
        for k in range(2):
            for turn in range(4):
                place = turn * column_count + 2 * at + k
                out[pl.ds(place, sub_count, stride=message_rows), :] = piece[
                    turn * sub_count : (turn + 1) * sub_count, k * LANES : (k + 1) * LANES
                ]
    for block in range(sub_count):
        at = block * message_rows + 4 * column_count
        out[at : at + 4, :] = inside[block * 4 : (block + 1) * 4, :]
        out[at + 4 : (block + 1) * message_rows, :] = jnp.zeros(
            (message_rows - 4 * column_count - 4, LANES), f32
        )
    for target, members in zip(outs, layout):
        for place, k in enumerate(members):
            at = pl.multiple_of((index[0] ^ k) * message_rows, SUBLANES)
            to = place * message_rows
            target[to : to + message_rows, :] = out[pl.ds(at, message_rows), :]


def chain_states(layout, index, lon_length, exits, leaving, inside):
    sub_count = len(exits)
    rows = exits[0].shape[0]
    column_total = rows // 4 * LANES
    message_rows = rows + 8
    return pl.pallas_call(
        functools.partial(chain_kernel, sub_count, layout),
        in_specs=[SMEM, SMEM, SMEM, VMEM] + [VMEM] * sub_count,
        out_specs=[VMEM] * len(layout),
        scratch_shapes=[
            pltpu.VMEM((sub_count, rows, LANES), f32),
            pltpu.VMEM((sub_count * message_rows, LANES), f32),
            pltpu.VMEM((sub_count * rows, LANES), f32),
        ]
        + [pltpu.VMEM((1,) + shape, bf16) for shape in weight_shapes(column_total)],
        out_shape=[
            pltpu.VMEM((len(members) * message_rows, LANES), f32) for members in layout
        ],
        compiler_params=params(16),
        cost_estimate=cost(10, 10),
    )(index, lon_length, leaving, *pinned(inside, *exits))


def join_kernel(kept, came, *outs):
    rows = kept.shape[0] // len(outs)
    for at, out in enumerate(outs):
        out[:rows, :] = kept[at * rows : (at + 1) * rows, :]
        out[rows:, :] = came[at * rows : (at + 1) * rows, :]


def join_pairs(kept, came, count):
    rows = 2 * kept.shape[0] // count
    return pl.pallas_call(
        join_kernel,
        in_specs=[VMEM] * 2,
        out_specs=[VMEM] * count,
        out_shape=[pltpu.VMEM((rows, LANES), f32)] * count,
        compiler_params=params(4),
        cost_estimate=cost(10, 10),
    )(*pinned(kept, came))


def gather_kernel(layout, index, *rest):
    *parts, out = rest
    rows = out.shape[0] // sum(len(members) for members in layout)
    for part, members in zip(parts, layout):
        for place, k in enumerate(members):
            at = pl.multiple_of((index[0] ^ k) * rows, SUBLANES)
            out[pl.ds(at, rows), :] = part[place * rows : (place + 1) * rows, :]


def gather_messages(layout, index, parts):
    return pl.pallas_call(
        functools.partial(gather_kernel, layout),
        in_specs=[SMEM] + [VMEM] * len(parts),
        out_specs=VMEM,
        out_shape=pltpu.VMEM((sum(part.shape[0] for part in parts), LANES), f32),
        compiler_params=params(4),
        cost_estimate=cost(10, 10),
    )(index, *pinned(*parts))


def pair_factors(top, low):
    top_take, low_take = 1.0 - top, 1.0 - low
    through = top * low
    sends = (low * top_take, low_take)
    low_out = (low_take * through, low, low_take * low * top_take, low_take * low_take)
    top_out = (
        top * low_out[0] + top_take * top,
        top * low_out[1],
        top * low_out[2] + top_take * top_take,
        top * low_out[3],
    )
    return through, sends, top_out, low_out


def tables_kernel(index, own, across_, beside_, corner_, table, mix, decay):
    band = index[0]
    for at, lengths in enumerate((own, across_, beside_, corner_)):
        for level in range(2):
            for variable in range(4):
                row = at * 8 + level * 4 + variable
                decay[row : row + 1, :] = jnp.full((1, LANES), lengths[level, variable], f32)
    decay[...] = jnp.exp(-1.0 / decay[...])

    def factors(at):
        return pair_factors(decay[at * 8 : at * 8 + 4, :], decay[at * 8 + 4 : at * 8 + 8, :])

    def by_band(*values):
        result = values[0]
        for at in range(1, 4):
            result = jnp.where(band == at, values[at], result)
        return result

    through, sends, top_out, low_out = factors(0)
    across, beside, corner = factors(1), factors(2), factors(3)
    through_n, echo_n = beside[0], beside[2][0]
    third = by_band(across[0], corner[0], across[0], across[0])
    third_echo = by_band(across[2][0], corner[2][0], across[2][0], across[2][0])
    fourth_echo = by_band(corner[2][0], across[2][0], corner[2][0], corner[2][0])
    zeta = third * third * fourth_echo + third_echo
    rows = []
    for i in range(2):
        reply = top_out[2 + i]
        rows.append(by_band(sends[i], reply + through * zeta * sends[i], sends[i], reply))
    for i in range(2):
        rows.append(
            by_band(
                sends[i], sends[i], through * echo_n * sends[i] + top_out[2 + i], sends[i]
            )
        )
    rows.append(through)
    for fin, back, *own in (top_out, low_out):
        for i in range(2):
            rows.append(
                by_band(
                    own[i] + back * (through_n * through_n * zeta + echo_n) * sends[i],
                    own[i] + back * zeta * sends[i],
                    own[i] + back * echo_n * sends[i],
                    own[i],
                )
            )
        none = jnp.zeros_like(fin)
        rows.append(by_band(back, fin + back * zeta * through, back, fin))
        rows.append(by_band(back * through_n, none, none, fin * through_n))
        rows.append(by_band(none, back, fin + back * echo_n * through, none))
    for variable in range(4):
        for at, row in enumerate(rows):
            table[variable, at : at + 1, :] = row[variable : variable + 1]
    row = lax.broadcasted_iota(i32, (SUBLANES, LANES), 0)
    for variable in range(4):
        value = jnp.zeros((SUBLANES, LANES), f32)
        downward, keeps = [], []
        for level in range(8):
            other = (level // 2) ^ band
            place = (other & 1) * 2 + lax.shift_right_logical(other, 1)
            at = place * 8 + (level % 2) * 4 + variable
            keep = jnp.broadcast_to(decay[pl.ds(at, 1), :], (SUBLANES, LANES))
            unit = jnp.where(row == place * 2 + level % 2, 1.0, 0.0)
            value = keep * value + (1.0 - keep) * unit
            downward.append(value)
            keeps.append(keep)
        value = jnp.zeros((SUBLANES, LANES), f32)
        upward = [None] * 8
        for level in reversed(range(8)):
            value = keeps[level] * value + (1.0 - keeps[level]) * downward[level]
            upward[level] = value
        for level in range(2):
            mix[level, variable] = by_band(*[upward[2 * at + level] for at in range(4)])


def tables(index, lengths):
    return pl.pallas_call(
        tables_kernel,
        in_specs=[SMEM] * 5,
        out_specs=[VMEM, VMEM],
        out_shape=[
            jax.ShapeDtypeStruct((4, 16, LANES), f32),
            jax.ShapeDtypeStruct((2, 4, SUBLANES, LANES), f32),
        ],
        scratch_shapes=[pltpu.VMEM((32, LANES), f32)],
        compiler_params=params(4),
        cost_estimate=cost(10, 10),
    )(index, *lengths)


def add_kernel(variables, part, near, table, total):
    for place, variable in enumerate(variables):
        weight = table[variable, 4:5, :]
        for column in range(part.shape[2] // LANES):
            at = slice(column * LANES, (column + 1) * LANES)
            total[place, :, at] = part[place, :, at] + weight * near[place, :, at]


def add_near(variables, part, near, table):
    return pl.pallas_call(
        functools.partial(add_kernel, variables),
        in_specs=[VMEM] * 3,
        out_specs=VMEM,
        out_shape=pltpu.VMEM(part.shape, f32),
        compiler_params=params(4),
        cost_estimate=cost(10, 10),
    )(*pinned(part, near, table))


def last_kernel(variable, place, own, near, far, met, mix, table, *rest):
    out, added, message, sems = rest[-4:]
    _, row_count, column_total = near.shape
    column_count = column_total // LANES
    stride = message.shape[0] // SUBLANES
    first = 0
    for at, part in enumerate(rest[:4]):
        for level in range(2):
            source = (level * 4 + variable) * stride
            target = (2 * at + level) * stride
            message[target : target + stride, :] = part[source : source + stride, :]
    lanes = []
    for column in range(column_count):
        lanes.append(
            jnp.concatenate(
                [
                    message[pl.ds(first + k * column_count + column, SUBLANES, stride=stride), :]
                    for k in range(4)
                ],
                axis=0,
            )
        )
    high, low = split(jnp.concatenate(lanes, axis=1))
    states = jnp.concatenate([high, high, low, low], axis=0)
    inside = [
        message[pl.ds(first + 4 * column_count + k, SUBLANES, stride=stride), :] for k in range(4)
    ]
    copies = []
    for level in range(2):
        mixed = jnp.concatenate([part * mix[level, variable] for part in inside], axis=0)
        high, low = split(mixed)
        mixed = jnp.concatenate([high, low, high, low], axis=0)
        total = dot(mixed, states, (((0,), (0,)), ((), ())))[:row_count]
        weights = [table[variable, 5 + level * 5 + k : 6 + level * 5 + k, :] for k in range(5)]
        for column in range(column_count):
            at = slice(column * LANES, (column + 1) * LANES)
            value = total[:, at] + weights[0] * own[place, 0, :, at]
            value = value + weights[1] * own[place, 1, :, at]
            value = value + weights[2] * near[place, :, at] + weights[3] * far[place, :, at]
            added[level, :, at] = value + weights[4] * met[place, :, at]
        copy = pltpu.make_async_copy(added.at[level], out.at[level, variable], sems.at[level])
        copy.start()
        copies.append(copy)
    for copy in copies:
        copy.wait()


def last_step(variable, place, own, near, far, met, messages, mix, table, so_far):
    _, _, row_count, column_total = own.shape
    operands = pinned(own, near, far, met, mix, table, *messages)
    in_specs = [VMEM] * 10
    aliases = {}
    if so_far is not None:
        operands.append(so_far)
        in_specs.append(HBM)
        aliases = {10: 0}
    return pl.pallas_call(
        functools.partial(last_kernel, variable, place),
        in_specs=in_specs,
        out_specs=HBM,
        out_shape=pltpu.HBM((2, 4, row_count, column_total), f32),
        scratch_shapes=[
            pltpu.VMEM((2, row_count, column_total), f32),
            pltpu.VMEM(messages[0].shape, f32),
            pltpu.SemaphoreType.DMA((2,)),
        ],
        input_output_aliases=aliases,
        compiler_params=params(10),
        cost_estimate=cost(10, 10),
    )(*operands)


CHUNKS = ((0, 1), (2, 3))
SWAP = [(0, 1), (1, 0), (2, 3), (3, 2)]
CROSS = [(0, 2), (2, 0), (1, 3), (3, 1)]
CORNER = [(0, 3), (3, 0), (1, 2), (2, 1)]
MIDDLE = [(0, 0), (1, 2), (2, 1), (3, 3)]


def after(value, *earlier):
    return lax.optimization_barrier((value,) + earlier)[0]


def four_bands(swept, weights, exits, units, chain, gather, table, mix):
    owns, parts, nears, mets = [], [], [], []

    def filter_some(at, *earlier):
        own, sent, part = longitude_pair(CHUNKS[at], after(swept, *earlier), weights, table)
        owns.append(own)
        parts.append(part)
        nears.append(lax.ppermute(sent, "band", SWAP))
        return part

    def cross_some(at, *earlier):
        part = after(parts[at], *earlier)
        total = add_near(CHUNKS[at], part, nears[at], table)
        mets.append(lax.ppermute(total, "band", MIDDLE))
        return total

    last = len(CHUNKS) - 1
    mark = filter_some(0)
    mark = filter_some(1, mark)
    mark = cross_some(0, mark)
    exits = exchange([after(part, mark) for part in exits], "sub")
    response = units(mark)
    if last > 1:
        mark = filter_some(2, mark)
    mark = cross_some(1, mark, *response)
    if last > 1:
        mark = cross_some(2, mark)
    kept, sent = chain(
        [[0, 2, 4, 6], [1, 3, 5, 7]], [after(exits[0], mark)] + exits[1:], response
    )
    came = lax.ppermute(sent, "sub", [(at, at ^ 1) for at in range(8)])
    pairs = join_pairs(kept, came, 4)
    pairs = [pairs[0]] + [
        lax.ppermute(pairs[k], "sub", [(at, at ^ (2 * k)) for at in range(8)]) for k in (1, 2, 3)
    ]
    messages = gather([[0, 1], [2, 3], [4, 5], [6, 7]], pairs)
    mets = [after(met, messages) for met in mets]
    across = lax.ppermute(messages, "band", CROSS)
    beside = lax.ppermute(messages, "band", SWAP)
    corner = lax.ppermute(across, "band", SWAP)
    messages = (messages, across, beside, corner)
    fars = [lax.ppermute(met, "band", SWAP) for met in mets]
    result = None
    for at, variables in enumerate(CHUNKS):
        for place, variable in enumerate(variables):
            result = last_step(
                variable,
                place,
                owns[at],
                nears[at],
                fars[at],
                mets[at],
                messages,
                mix,
                table,
                result,
            )
    return result


def prefix(part, axis, combine, identity, reverse):
    count = lax.axis_size(axis)
    place = lax.axis_index(axis)
    ahead = count - 1 - place if reverse else place
    gathered = jax.tree.map(lambda a: lax.all_gather(a, axis), part)
    state = jax.tree.map(lambda a, e: jnp.zeros_like(a) + jnp.asarray(e, a.dtype), part, identity)

    def one(turn, state):
        source = count - 1 - turn if reverse else turn
        return combine(
            state, jax.tree.map(lambda a: lax.dynamic_index_in_dim(a, source, 0, False), gathered)
        )

    return lax.fori_loop(0, ahead, one, state)


def combine(earlier, later):
    return (earlier[0] * later[0], later[0] * earlier[1] + later[1])


def level_chain(values, decays, reverse):
    level_count = values.shape[0]
    visit_order = range(level_count - 1, -1, -1) if reverse else range(level_count)
    carry_state = jnp.zeros_like(values[0])
    level_gain = jnp.ones((values.shape[1],), f32)
    outputs = [None] * level_count
    carried = [None] * level_count
    for level_index in visit_order:
        factor = decays[level_index][:, None, None]
        carry_state = factor * carry_state + (1.0 - factor) * values[level_index]
        level_gain = level_gain * decays[level_index]
        outputs[level_index] = carry_state
        carried[level_index] = level_gain
    total_decay = level_gain[:, None, None]
    identity = (jnp.ones_like(total_decay), jnp.zeros_like(carry_state))
    incoming = prefix((total_decay, carry_state), "band", combine, identity, reverse)[1]
    return jnp.stack(
        [
            outputs[level_index] + carried[level_index][:, None, None] * incoming
            for level_index in range(level_count)
        ]
    )


def any_bands(swept, weights, exits, units, chain, gather, vert_length):
    column_count, group_count, row_count, _ = swept.shape
    layout = [[k] for k in range(len(exits))]
    chained = chain(layout, exchange(exits, "sub"), units())
    messages = gather(layout, exchange(chained, "sub"))
    (values,) = longitude(swept, weights, group_count, 0, 1)
    messages = messages.reshape(group_count, -1, LANES)
    states = messages[:, : 4 * column_count].reshape(group_count, 4, -1)
    inside = messages[:, 4 * column_count : 4 * column_count + 4, :row_count]
    values = values + jnp.einsum("gkr,gkc->grc", inside, states, precision=highest)
    decay = jnp.exp(-1.0 / vert_length)
    values = values.reshape(decay.shape + values.shape[1:])
    return level_chain(level_chain(values, decay, False), decay, True)


def per_device(background, obs_columns, obs_owner, obs_cell, lat_length, lon_length, vert_length):
    level_count, var_count, row_count, lon_count = background.shape
    sub_count = lax.axis_size("sub")
    group_count = level_count * var_count
    strip = row_count * lon_count
    column_count = lon_count // LANES
    capacity = 2 * obs_owner.shape[0] // sub_count
    chunk_count = capacity // LANES
    two_chips = lax.axis_size("band") == 4 and level_count == 2 and sub_count == 8
    index = lax.axis_index("sub").astype(i32).reshape(1)
    band = lax.axis_index("band").astype(i32).reshape(1)

    packed = pack_observations(
        after(index, band),
        obs_columns, obs_owner[:, 0], obs_cell, sub_count, strip, capacity
    )
    got = exchange(packed, "sub")
    space = pltpu.VMEM if two_chips else pltpu.HBM
    weights = prepare(after(lon_length, packed[0]), lon_count, space)
    ready = list(weights)
    if two_chips:
        vert_length = after(vert_length, *packed)
        vert_lengths = [vert_length] + [
            lax.ppermute(vert_length, "band", pairs) for pairs in (CROSS, SWAP, CORNER)
        ]
        table, mix = tables(after(band, packed[0]), vert_lengths)
        ready.append(table)

    sizes = (sub_count, group_count, row_count, column_count, chunk_count, strip)
    swept, *exits = deposit_and_sweep(
        index,
        lat_length,
        [after(got[0], *ready)] + got[1:],
        background.reshape(group_count, row_count, lon_count),
        sizes,
    )

    def units(*earlier):
        start = after(index, swept, *earlier)
        return unit_responses(start, lat_length, sub_count, row_count)

    def chain(layout, arrived, response):
        inside, leaving = response
        return chain_states(layout, index, lon_length, arrived, leaving, inside)

    def gather(layout, parts, *earlier):
        return gather_messages(layout, after(index, *earlier), parts)

    if two_chips:
        return four_bands(swept, weights, exits, units, chain, gather, table, mix)
    return any_bands(swept, weights, exits, units, chain, gather, vert_length)


def solution(mesh):
    placed = (
        P("band", None, "sub", None),
        P("band", None, "sub"),
        P("sub", None),
        P("sub"),
        P("band", None, None),
        P("band", None),
        P("band", None),
    )
    return jax.shard_map(
        per_device,
        mesh=mesh,
        in_specs=placed,
        out_specs=P("band", None, "sub", None),
        check_vma=False,
    )
```

```python
import functools

import jax
import jax.numpy as jnp
from jax import lax
from jax.experimental import pallas as pl
from jax.experimental.pallas import tpu as pltpu
from jax.sharding import PartitionSpec as P

f32 = jnp.float32
i32 = jnp.int32
bf16 = jnp.bfloat16
highest = lax.Precision.HIGHEST

LANES = 128
SUBLANES = 8
BLOCK = 256
CHAINS = 4

VMEM = pl.BlockSpec(memory_space=pltpu.VMEM)
SMEM = pl.BlockSpec(memory_space=pltpu.SMEM)
HBM = pl.BlockSpec(memory_space=pltpu.HBM)


def params(mib):
    return pltpu.CompilerParams(vmem_limit_bytes=mib << 20)


def pinned(*arrays):
    return [pltpu.with_memory_space_constraint(array, pltpu.VMEM) for array in arrays]


def in_hbm(*arrays):
    return [pltpu.with_memory_space_constraint(array, pltpu.HBM) for array in arrays]


EVEN_ODD = ((0, 2, 4, 6), (1, 3, 5, 7))
BY_PAIRS = ((0, 1), (2, 3), (4, 5), (6, 7))


def leaving_layout(sub_count):
    return EVEN_ODD if sub_count == 8 else tuple((k,) for k in range(sub_count))


def arriving_layout(sub_count):
    return BY_PAIRS if sub_count == 8 else tuple((k,) for k in range(sub_count))


def join_kernel(kept, came, *outs):
    rows = kept.shape[0] // len(outs)
    for at, out in enumerate(outs):
        out[:rows, :] = kept[at * rows : (at + 1) * rows, :]
        out[rows:, :] = came[at * rows : (at + 1) * rows, :]


def join_pairs(kept, came, count):
    rows = 2 * kept.shape[0] // count
    return pl.pallas_call(
        join_kernel,
        in_specs=[VMEM] * 2,
        out_specs=[VMEM] * count,
        out_shape=[pltpu.VMEM((rows, LANES), f32)] * count,
        compiler_params=params(4),
        cost_estimate=cost(10, 10),
    )(*pinned(kept, came))


def after(value, *earlier):
    return lax.optimization_barrier((value,) + earlier)[0]


def exchange(parts, sub_count, meanwhile=None):
    def move(part, k):
        return lax.ppermute(part, "sub", [(at, at ^ k) for at in range(sub_count)])

    if sub_count != 8:
        return [parts[0]] + [move(parts[k], k) for k in range(1, sub_count)]
    kept, sent = parts
    came = move(sent, 1)
    if meanwhile is not None:
        kept = after(kept, *meanwhile(came))
    pairs = join_pairs(kept, came, 4)
    return [pairs[0]] + [move(pairs[k], 2 * k) for k in (1, 2, 3)]


def cost(flops, read):
    return pl.CostEstimate(flops=flops, bytes_accessed=read, transcendentals=0)


def dot(a, b, dims=(((1,), (0,)), ((), ()))):
    return lax.dot_general(a, b, dims, preferred_element_type=f32)


def split(x):
    high = x.astype(bf16)
    return high, (x - high.astype(f32)).astype(bf16)


def pack_kernel(sizes, layout, index, owners, cells, values, *rest):
    outs, (packed, places, tally, sorted_, joined, counts, sem) = rest[:-7], rest[-7:]
    sub_count, group_count, chunk_count, strip = sizes
    block_count = owners.shape[0]
    tiles = group_count // SUBLANES
    lane = lax.broadcasted_iota(i32, (SUBLANES, LANES), 1)
    square = lambda axis: lax.broadcasted_iota(i32, (LANES, LANES), axis)
    owner = owners[...]
    picked = [jnp.where(owner == sub, 1.0, 0.0) for sub in range(sub_count)]
    upto = jnp.where(square(0) <= square(1), 1.0, 0.0).astype(bf16)
    ranks = dot(jnp.concatenate(picked, axis=0).astype(bf16), upto)
    wide = lax.broadcasted_iota(i32, (block_count, LANES), 1)
    place = jnp.zeros((block_count, LANES), f32)
    base = jnp.zeros((block_count, LANES), f32)
    totals = jnp.zeros((block_count, LANES), f32)
    for sub in range(sub_count):
        rank = ranks[sub * block_count : (sub + 1) * block_count]
        total = jnp.broadcast_to(rank[:, LANES - 1 :], rank.shape)
        place = jnp.where(owner == sub, rank - 1.0 + base, place)
        totals = jnp.where(wide == sub, total, totals)
        base = base + total
    places[...] = place.astype(i32)
    tally[...] = totals.astype(i32)
    copy = pltpu.make_async_copy(tally, counts, sem)
    copy.start()
    extra = -(group_count + SUBLANES) % 16
    row = square(0)

    def sort_block(block, carry):
        at = pl.multiple_of(block * LANES, LANES)
        parts = [
            *[values[level, :, pl.ds(at, LANES)] for level in range(values.shape[0])],
            jnp.broadcast_to(cells[pl.ds(block, 1), :], (SUBLANES, LANES)).astype(f32),
        ]
        if extra:
            parts.append(jnp.zeros((extra, LANES), f32))
        whole = jnp.concatenate(parts, axis=0)
        rows = whole.shape[0]
        high, rest = whole.astype(bf16), whole
        rest = rest - high.astype(f32)
        middle = rest.astype(bf16)
        low = (rest - middle.astype(f32)).astype(bf16)
        move = jnp.where(row == places[pl.ds(block, 1), :], 1.0, 0.0).astype(bf16)
        moved = dot(
            jnp.concatenate([high, middle, low], axis=0), move, (((1,), (1,)), ((), ()))
        )
        moved = moved[:rows] + moved[rows : 2 * rows] + moved[2 * rows :]
        for tile in range(tiles + 1):
            sorted_[block, tile] = moved[tile * SUBLANES : (tile + 1) * SUBLANES]
        return carry

    lax.fori_loop(0, block_count, sort_block, 0, unroll=8)
    copy.wait()

    def join_block(block, ends):
        start = jnp.int32(0)
        writes, following = [], []
        for sub in range(sub_count):
            end = ends[sub]
            chunk, offset = lax.shift_right_logical(end, 7), end & 127
            for tile in range(tiles + 1):
                turned = pltpu.roll(sorted_[block, tile], (end - start) & 127, 1)
                kept = jnp.where(lane >= offset, turned, joined[sub, chunk, tile])
                writes.append((sub, chunk, tile, kept, turned))
            start = start + counts[block, sub]
            following.append(end + counts[block, sub])
        for sub, chunk, tile, kept, turned in writes:
            joined[sub, chunk, tile] = kept
            joined[sub, chunk + 1, tile] = turned
        return tuple(following)

    ends = lax.fori_loop(0, block_count, join_block, (jnp.int32(0),) * sub_count, unroll=2)
    word_row = chunk_count * group_count
    word_rows = packed.shape[1] - word_row
    for sub in range(sub_count):
        packed[sub, word_row:, :] = jnp.full((word_rows, LANES), float(strip), f32)
        for chunk in range(chunk_count):
            for tile in range(tiles):
                at = chunk * group_count + tile * SUBLANES
                packed[sub, at : at + SUBLANES, :] = joined[sub, chunk, tile]
            filled = lane + chunk * LANES < ends[sub]
            cell = jnp.where(filled, joined[sub, chunk, tiles], 0.0).astype(i32)
            word = (cell - (cell & 127)) + ((cell - lane) & 127)
            word = jnp.where(filled, word, strip).astype(f32)
            packed[sub, word_row + chunk : word_row + chunk + 1, :] = word[:1]
    rows = packed.shape[1]
    for out, members in zip(outs, layout):
        for at, k in enumerate(members):
            out[at * rows : (at + 1) * rows, :] = packed[index[0] ^ k]


def pack_observations(index, obs_values, owners, cells, sub_count, strip, capacity):
    level_count, var_count, obs_count = obs_values.shape
    group_count = level_count * var_count
    chunk_count = capacity // LANES
    block_count = obs_count // LANES
    rows = chunk_count * group_count + SUBLANES * (-(-chunk_count // SUBLANES))
    tiles = group_count // SUBLANES
    layout = leaving_layout(sub_count)
    return pl.pallas_call(
        functools.partial(pack_kernel, (sub_count, group_count, chunk_count, strip), layout),
        out_shape=[pltpu.VMEM((len(members) * rows, LANES), f32) for members in layout],
        in_specs=[SMEM, VMEM, VMEM, VMEM],
        out_specs=[VMEM] * len(layout),
        scratch_shapes=[
            pltpu.VMEM((sub_count, rows, LANES), f32),
            pltpu.VMEM((block_count, LANES), i32),
            pltpu.VMEM((block_count, LANES), i32),
            pltpu.VMEM((block_count, tiles + 1, SUBLANES, LANES), f32),
            pltpu.VMEM((sub_count, chunk_count + 2, tiles + 1, SUBLANES, LANES), f32),
            pltpu.SMEM((block_count, LANES), i32),
            pltpu.SemaphoreType.DMA,
        ],
        compiler_params=params(6),
        cost_estimate=cost(10, 10),
    )(index, *in_hbm(owners.reshape(block_count, LANES), cells.reshape(block_count, LANES), obs_values))


def ready_kernel(sizes, index, lat_length, field, decay, *rest):
    sub_count, group_count, row_count, column_count, chunk_count, strip = sizes
    totals, (loaded, all_lengths, sem, sems) = rest[:CHAINS], rest[CHAINS:]
    tiles = group_count // SUBLANES

    def load(group):
        return pltpu.make_async_copy(field.at[group], loaded.at[group], sems.at[group])

    fetch = pltpu.make_async_copy(lat_length, all_lengths, sem)
    fetch.start()
    for group in range(group_count):
        load(group).start()

    def clear(row, carry):
        for total in totals[1:]:
            for tile in range(tiles):
                for column in range(column_count):
                    total[tile, row, column] = jnp.zeros((SUBLANES, LANES), f32)
        return carry

    lax.fori_loop(0, row_count, clear, 0)
    fetch.wait()
    shift = index[0] * row_count
    for tile in range(tiles):
        lengths = jnp.concatenate(
            [all_lengths[2 * tile + k] for k in range(SUBLANES // 4)], axis=0
        )
        lengths = pltpu.roll(lengths, jnp.where(shift > 0, lengths.shape[1] - shift, 0), 1)
        keep = jnp.exp(-1.0 / lengths[:, :LANES])
        for row in range(row_count):
            decay[row, tile] = jnp.broadcast_to(keep[:, row : row + 1], (SUBLANES, LANES))
    for group in range(group_count):
        load(group).wait()
    for tile in range(tiles):
        groups = slice(tile * SUBLANES, (tile + 1) * SUBLANES)

        def turn_rows(at, carry):
            rows = pl.ds(pl.multiple_of(at * SUBLANES, SUBLANES), SUBLANES)
            for column in range(column_count):
                lanes = slice(column * LANES, (column + 1) * LANES)
                totals[0][tile, rows, column] = jnp.swapaxes(loaded[groups, rows, lanes], 0, 1)
            return carry

        lax.fori_loop(0, row_count // SUBLANES, turn_rows, 0)


def dump_shape(sizes):
    _, group_count, row_count, column_count, _, _ = sizes
    return (group_count // SUBLANES, row_count + 1, column_count, SUBLANES, LANES)


def make_ready(index, lat_length, field, sizes):
    sub_count, group_count, row_count, column_count, chunk_count, strip = sizes
    tiles = group_count // SUBLANES
    return pl.pallas_call(
        functools.partial(ready_kernel, sizes),
        in_specs=[SMEM, HBM, HBM],
        out_specs=[VMEM] * (1 + CHAINS),
        out_shape=[pltpu.VMEM((row_count, tiles, SUBLANES, LANES), f32)]
        + [pltpu.VMEM(dump_shape(sizes), f32)] * CHAINS,
        scratch_shapes=[
            pltpu.VMEM((group_count, row_count, column_count * LANES), f32),
            pltpu.VMEM(lat_length.shape, f32),
            pltpu.SemaphoreType.DMA,
            pltpu.SemaphoreType.DMA((group_count,)),
        ],
        compiler_params=params(6),
        cost_estimate=cost(10, 10),
    )(index, *in_hbm(lat_length, field))


def deposit_kernel(sizes, index, decay, *rest):
    sub_count, group_count, row_count, column_count, chunk_count, strip = sizes
    here, away = arriving_layout(sub_count), leaving_layout(sub_count)
    arrived, swept = rest[: len(here)], rest[len(here) + CHAINS]
    rest = rest[len(here) + CHAINS + 1 :]
    leaving, totals = rest[: len(away)], rest[len(away) :][:CHAINS]
    got, exits, integers, words, word_sems = rest[len(away) + CHAINS :]
    tiles = group_count // SUBLANES
    word_row = chunk_count * group_count
    block_rows = got.shape[1]
    word_rows = block_rows - word_row
    sources = [(part, at) for part, members in zip(arrived, here) for at in range(len(members))]
    for source, (part, at) in enumerate(sources):
        block = part[at * block_rows : (at + 1) * block_rows, :]
        integers[source * word_rows : (source + 1) * word_rows, :] = block[word_row:].astype(i32)

    def hand_over(source):
        span = pl.ds(source * word_rows, word_rows)
        return pltpu.make_async_copy(integers.at[span], words.at[span], word_sems.at[source])

    for source in range(sub_count):
        hand_over(source).start()
    for source, (part, at) in enumerate(sources):
        got[source] = part[at * block_rows : (at + 1) * block_rows, :]
    lane = lax.broadcasted_iota(i32, (SUBLANES, LANES), 1)

    def one_source(source, carry):
        first = source * word_rows
        hand_over(source).wait()

        def more(chunk):
            last = jnp.minimum(chunk, chunk_count - 1)
            return (chunk < chunk_count) & (words[first + last, 0] < strip)

        def one_chunk(chunk):
            blocks = [
                got[
                    source,
                    pl.ds(pl.multiple_of(chunk * group_count + tile * SUBLANES, 8), SUBLANES),
                    :,
                ]
                for tile in range(tiles)
            ]
            for slot in range(LANES):
                word = words[first + chunk, slot]
                target = lax.shift_right_logical(word, 7)
                turn = word & 127
                for tile in range(tiles):
                    value = pltpu.roll(jnp.where(lane == slot, blocks[tile], 0.0), turn, 1)
                    total = flat[slot % CHAINS]
                    total[tile, target] = total[tile, target] + value
            return chunk + 1

        lax.while_loop(more, one_chunk, jnp.int32(0))
        return carry

    flat = [total.reshape(tiles, -1, SUBLANES, LANES) for total in totals]
    lax.fori_loop(0, sub_count, one_source, 0)
    for tile in range(tiles):
        groups = slice(tile * SUBLANES, (tile + 1) * SUBLANES)

        def add_rows(at, carry):
            rows = pl.ds(pl.multiple_of(at * SUBLANES, SUBLANES), SUBLANES)
            for column in range(column_count):
                value = totals[0][tile, rows, column]
                for total in totals[1:]:
                    value = value + total[tile, rows, column]
                totals[0][tile, rows, column] = value
            return carry

        lax.fori_loop(0, row_count // SUBLANES, add_rows, 0)

        def sweep(source, target, turn):
            def one_row(step, state):
                row = row_count - 1 - step if turn % 2 else step
                keep = decay[row, tile]
                take = 1.0 - keep
                following = []
                for column in range(column_count):
                    value = keep * state[column] + take * source[tile, row, column]
                    target[tile, row, column] = value
                    following.append(value)
                return tuple(following)

            nothing = tuple(jnp.zeros((SUBLANES, LANES), f32) for _ in range(column_count))
            state = lax.fori_loop(0, row_count, one_row, nothing, unroll=4)
            message_rows = 4 * column_count
            for column in range(column_count):
                at = tile * SUBLANES * message_rows + turn * column_count + column
                exits[pl.ds(at, SUBLANES, stride=message_rows), :] = state[column]

        for turn in range(4):
            sweep(totals[turn % 2], totals[1 - turn % 2], turn)

        def turn_rows(at, carry):
            rows = pl.ds(pl.multiple_of(at * SUBLANES, SUBLANES), SUBLANES)
            for column in range(column_count):
                swept[column, groups, rows, :] = jnp.swapaxes(totals[0][tile, rows, column], 0, 1)
            return carry

        lax.fori_loop(0, row_count // SUBLANES, turn_rows, 0)
    rows = 4 * column_count
    for out, members in zip(leaving, away):
        for at, k in enumerate(members):
            first = pl.multiple_of((index[0] ^ k) * rows, SUBLANES)
            out[at * rows : (at + 1) * rows, :] = exits[pl.ds(first, rows), :]


def deposit_and_sweep(index, decay, totals, got, sizes):
    sub_count, group_count, row_count, column_count, chunk_count, strip = sizes
    here, away = arriving_layout(sub_count), leaving_layout(sub_count)
    rows = got[0].shape[0] // len(here[0])
    word_rows = rows - chunk_count * group_count
    exit_rows = 4 * column_count
    results = pl.pallas_call(
        functools.partial(deposit_kernel, sizes),
        out_shape=[pltpu.VMEM((column_count, group_count, row_count, LANES), f32)]
        + [pltpu.VMEM((len(members) * exit_rows, LANES), f32) for members in away]
        + [pltpu.VMEM(dump_shape(sizes), f32)] * CHAINS,
        in_specs=[SMEM] + [VMEM] * (1 + len(here) + CHAINS),
        out_specs=[VMEM] * (1 + len(away) + CHAINS),
        scratch_shapes=[
            pltpu.VMEM((sub_count, rows, LANES), f32),
            pltpu.VMEM((group_count * exit_rows, LANES), f32),
            pltpu.VMEM((sub_count * word_rows, LANES), i32),
            pltpu.SMEM((sub_count * word_rows, LANES), i32),
            pltpu.SemaphoreType.DMA((sub_count,)),
        ],
        input_output_aliases={
            2 + len(here) + k: 1 + len(away) + k for k in range(CHAINS)
        },
        compiler_params=params(6),
        cost_estimate=cost(10, 10),
    )(index, *pinned(decay, *got, *totals))
    return results[: 1 + len(away)]


def unit_kernel(sizes, index, lat_length, inside, leaving, decay, held):
    sub_count, row_count = sizes
    group = index[0]
    decay[...] = jnp.zeros(decay.shape, f32)
    lengths = lat_length[group // 4, pl.ds(group % 4, 1), :]
    keep = jnp.exp(-1.0 / lengths)
    for sub in range(sub_count):
        part = keep[:, sub * row_count : (sub + 1) * row_count]
        decay[4 * sub : 4 * sub + 4, :row_count] = jnp.broadcast_to(part, (4, row_count))
    decay[...] = jnp.transpose(decay[...], (1, 0))
    held[...] = jnp.zeros(held.shape, f32)
    state_of = lax.broadcasted_iota(i32, (1, LANES), 1) & 3
    for turn in range(4):

        def one_row(step, state, turn=turn):
            row = row_count - 1 - step if turn % 2 else step
            keep = decay[pl.ds(row, 1), :]
            value = keep * state + (1.0 - keep) * held[pl.ds(row, 1), :]
            held[pl.ds(row, 1), :] = value
            return value

        enter = jnp.where(state_of == turn, 1.0, 0.0)
        state = lax.fori_loop(0, row_count, one_row, enter, unroll=8)
        leaving[turn : turn + 1, :] = state
    inside[...] = jnp.transpose(held[...], (1, 0))


def unit_responses(index, lat_length, sub_count, row_count):
    return pl.pallas_call(
        functools.partial(unit_kernel, (sub_count, row_count)),
        in_specs=[SMEM, VMEM],
        out_specs=[VMEM, VMEM],
        out_shape=[
            pltpu.VMEM((LANES, LANES), f32),
            jax.ShapeDtypeStruct((4, LANES), f32),
        ],
        scratch_shapes=[pltpu.VMEM((LANES, LANES), f32)] * 2,
        compiler_params=params(4),
        cost_estimate=cost(10, 10),
    )(index, lat_length)


def circle_weights(length, block_count, near_high, near_low, moment, spread):
    def ramp(shape, axis):
        return lax.broadcasted_iota(i32, shape, axis)

    def twice(x):
        return jnp.concatenate([x, x], axis=1)

    rate = -1.0 / jnp.full((1, LANES), length, f32)
    decay = jnp.exp(rate)
    gain = ((1.0 - decay) / (1.0 + decay)) ** 2
    centre = (1.0 + decay * decay) / (1.0 - decay * decay)
    turn = jnp.exp(rate * float(BLOCK * block_count))
    lag = float(BLOCK * block_count) * turn / (1.0 - turn)
    full_gain = gain / (1.0 - turn)

    shape = (BLOCK, BLOCK)
    gap = jnp.abs(ramp(shape, 0) - ramp(shape, 1)).astype(f32)
    near = twice(gain) * jnp.exp(twice(rate) * gap) * (gap + twice(centre))
    high, low = split(near)
    near_high[0] = high
    near_low[0] = low
    shape = (BLOCK, LANES)
    kind = ramp(shape, 1) & 3
    spot = ramp(shape, 0)
    far = jnp.where(kind < 2, BLOCK - spot, spot).astype(f32)
    sums = jnp.exp(rate * far) * jnp.where((kind & 1) == 1, far, 1.0)
    high, low = split(sums)
    moment[0, :, :LANES] = high
    moment[0, :, LANES:] = low
    shape = (32, BLOCK)
    kind = ramp(shape, 0) & 3
    block = lax.shift_right_logical(ramp(shape, 0), 2)
    spot = ramp(shape, 1)
    reach = jnp.where(kind < 2, spot, BLOCK - spot).astype(f32)
    for at in range(block_count):
        ahead = jnp.where(kind < 2, at - block, block - at) - 1
        steps = jnp.where(ahead < 0, ahead + block_count, ahead)
        full = reach + (steps * BLOCK).astype(f32)
        weight = twice(full_gain) * jnp.exp(twice(rate) * full)
        lead = full + twice(centre + lag)
        value = jnp.where((kind & 1) == 1, weight, weight * lead)
        value = jnp.where(block < block_count, value, 0.0)
        high, low = split(value)
        spread[0, :32, at * BLOCK : (at + 1) * BLOCK] = high
        spread[0, 32:, at * BLOCK : (at + 1) * BLOCK] = low


def weight_kernel(block_count, lon_length, *outs):
    group = pl.program_id(0)
    circle_weights(lon_length[group // 4, group % 4], block_count, *outs)


def weight_shapes(column_total):
    return [(BLOCK, BLOCK)] * 3 + [(64, column_total)]


def prepare(lon_length, column_total, space):
    group_count = lon_length.size
    shapes = weight_shapes(column_total)
    return pl.pallas_call(
        functools.partial(weight_kernel, column_total // BLOCK),
        grid=(group_count,),
        in_specs=[SMEM],
        out_specs=[pl.BlockSpec((1,) + shape, lambda i: (i, 0, 0)) for shape in shapes],
        out_shape=[space((group_count,) + shape, bf16) for shape in shapes],
        compiler_params=params(10),
        cost_estimate=cost(10, 10),
    )(lon_length)


def circle(pieces, near_high, near_low, moment, spread):
    row_count = pieces[0].shape[0]
    whole = jnp.concatenate(pieces, axis=0)
    high, low = split(whole)
    near = dot(high, near_high) + dot(low, near_high) + dot(high, near_low)
    sums = dot(high, moment)
    sums = sums[:, :LANES] + sums[:, LANES:] + dot(low, moment[:, :LANES])
    lane = lax.broadcasted_iota(i32, (row_count, LANES), 1)
    slot = lax.shift_right_logical(lane, 2) & 7
    moments = jnp.zeros((row_count, LANES), f32)
    for at in range(len(pieces)):
        part = sums[at * row_count : (at + 1) * row_count]
        moments = jnp.where(slot == at, part, moments)
    rest = moments - moments.astype(bf16).astype(f32)
    moments = jnp.where((lax.shift_right_logical(lane, 5) & 1) == 1, rest, moments).astype(bf16)
    spread = jnp.concatenate([spread[:32], spread[:32], spread[32:], spread[32:]], axis=0)
    far = dot(moments, spread)
    return [
        near[at * row_count : (at + 1) * row_count] + far[:, at * BLOCK : (at + 1) * BLOCK]
        for at in range(len(pieces))
    ]


def longitude_kernel(swept, near_high, near_low, moment, spread, out):
    column_count = swept.shape[0]
    pieces = [
        jnp.concatenate([swept[2 * at, 0], swept[2 * at + 1, 0]], axis=1)
        for at in range(column_count // 2)
    ]
    pieces = circle(pieces, near_high[0], near_low[0], moment[0], spread[0])
    for at, piece in enumerate(pieces):
        out[0, :, at * BLOCK : (at + 1) * BLOCK] = piece


def pair_kernel(variables, swept, near_high, near_low, moment, spread, table, own, sent, part):
    column_count = swept.shape[0]
    for place, variable in enumerate(variables):
        for level in range(2):
            group = level * 4 + variable
            pieces = [
                jnp.concatenate([swept[2 * at, group], swept[2 * at + 1, group]], axis=1)
                for at in range(column_count // 2)
            ]
            pieces = circle(
                pieces, near_high[group], near_low[group], moment[group], spread[group]
            )
            for target, first in ((sent, 0), (part, 2)):
                weight = table[variable, first + level : first + level + 1, :]
                weight = jnp.concatenate([weight, weight], axis=1)
                for at, piece in enumerate(pieces):
                    spot = slice(at * BLOCK, (at + 1) * BLOCK)
                    value = weight * piece
                    target[place, :, spot] = target[place, :, spot] + value if level else value
            for at, piece in enumerate(pieces):
                own[place, level, :, at * BLOCK : (at + 1) * BLOCK] = piece


def longitude_pair(variables, swept, weights, table):
    column_count, _, row_count, _ = swept.shape
    shape = (row_count, column_count * LANES)
    count = len(variables)
    return pl.pallas_call(
        functools.partial(pair_kernel, variables),
        in_specs=[VMEM] * 6,
        out_specs=[VMEM] * 3,
        out_shape=[
            pltpu.VMEM((count, 2) + shape, f32),
            pltpu.VMEM((count,) + shape, f32),
            pltpu.VMEM((count,) + shape, f32),
        ],
        compiler_params=params(10),
        cost_estimate=cost(10, 10),
    )(*pinned(swept, *weights, table))


def longitude(swept, weights, count, first, stride):
    column_count, _, row_count, _ = swept.shape
    column_total = column_count * LANES

    def of(i):
        return first + stride * i

    in_specs = [
        pl.BlockSpec((column_count, 1, row_count, LANES), lambda i: (0, of(i), 0, 0)),
        pl.BlockSpec((1, BLOCK, BLOCK), lambda i: (of(i), 0, 0)),
        pl.BlockSpec((1, BLOCK, BLOCK), lambda i: (of(i), 0, 0)),
        pl.BlockSpec((1, BLOCK, BLOCK), lambda i: (of(i), 0, 0)),
        pl.BlockSpec((1, 64, column_total), lambda i: (of(i), 0, 0)),
    ]
    out_specs = [pl.BlockSpec((1, row_count, column_total), lambda i: (i, 0, 0))]
    out_shape = [jax.ShapeDtypeStruct((count, row_count, column_total), f32)]
    operands = [swept, *weights]
    return pl.pallas_call(
        longitude_kernel,
        grid=(count,),
        in_specs=in_specs,
        out_specs=out_specs,
        out_shape=out_shape,
        compiler_params=params(14),
        cost_estimate=cost(10, 10),
    )(*operands)


def chain_kernel(sub_count, index, lon_length, leaving, inside, *rest):
    here, away = arriving_layout(sub_count), leaving_layout(sub_count)
    arrived, outs = rest[: len(here)], rest[len(here) :][: len(away)]
    exits, out, held, *weights = rest[len(here) + len(away) :]
    rows = exits.shape[1]
    for part, members in zip(arrived, here):
        for at, k in enumerate(members):
            exits[index[0] ^ k] = part[at * rows : (at + 1) * rows, :]
    column_count = exits.shape[1] // 4
    shape = (column_count, LANES)
    group = index[0]
    circle_weights(lon_length[group // 4, group % 4], column_count // 2, *weights)
    entering = {}
    for turn in range(4):
        order = list(range(sub_count))
        if turn % 2:
            order.reverse()
        state = jnp.zeros(shape, f32)
        for block in order:
            entering[turn, block] = state
            at = (turn * sub_count + block) * column_count
            held[at : at + column_count, :] = state
            state = exits[block, turn * column_count : (turn + 1) * column_count, :]
            for other in range(turn + 1):
                state = state + leaving[turn, block * 4 + other] * entering[other, block]
    pieces = []
    for at in range(column_count // 2):
        pair = [
            held[pl.ds(2 * at + k, 4 * sub_count, stride=column_count), :] for k in range(2)
        ]
        pieces.append(jnp.concatenate(pair, axis=1))
    pieces = circle(pieces, *[weight[0] for weight in weights])
    message_rows = out.shape[0] // sub_count
    for at, piece in enumerate(pieces):
        for k in range(2):
            for turn in range(4):
                place = turn * column_count + 2 * at + k
                out[pl.ds(place, sub_count, stride=message_rows), :] = piece[
                    turn * sub_count : (turn + 1) * sub_count, k * LANES : (k + 1) * LANES
                ]
    for block in range(sub_count):
        at = block * message_rows + 4 * column_count
        out[at : at + 4, :] = inside[block * 4 : (block + 1) * 4, :]
        out[at + 4 : (block + 1) * message_rows, :] = jnp.zeros(
            (message_rows - 4 * column_count - 4, LANES), f32
        )
    for target, members in zip(outs, away):
        for place, k in enumerate(members):
            at = pl.multiple_of((index[0] ^ k) * message_rows, SUBLANES)
            to = place * message_rows
            target[to : to + message_rows, :] = out[pl.ds(at, message_rows), :]


def chain_states(sub_count, index, lon_length, exits, leaving, inside):
    here, away = arriving_layout(sub_count), leaving_layout(sub_count)
    rows = exits[0].shape[0] // len(here[0])
    column_total = rows // 4 * LANES
    message_rows = rows + 8
    return pl.pallas_call(
        functools.partial(chain_kernel, sub_count),
        in_specs=[SMEM, SMEM, SMEM, VMEM] + [VMEM] * len(here),
        out_specs=[VMEM] * len(away),
        scratch_shapes=[
            pltpu.VMEM((sub_count, rows, LANES), f32),
            pltpu.VMEM((sub_count * message_rows, LANES), f32),
            pltpu.VMEM((sub_count * rows, LANES), f32),
        ]
        + [pltpu.VMEM((1,) + shape, bf16) for shape in weight_shapes(column_total)],
        out_shape=[
            pltpu.VMEM((len(members) * message_rows, LANES), f32) for members in away
        ],
        compiler_params=params(16),
        cost_estimate=cost(10, 10),
    )(index, lon_length, leaving, *pinned(inside, *exits))


def gather_kernel(layout, index, *rest):
    *parts, out = rest
    rows = out.shape[0] // sum(len(members) for members in layout)
    for part, members in zip(parts, layout):
        for place, k in enumerate(members):
            at = pl.multiple_of((index[0] ^ k) * rows, SUBLANES)
            out[pl.ds(at, rows), :] = part[place * rows : (place + 1) * rows, :]


def gather_messages(layout, index, parts):
    return pl.pallas_call(
        functools.partial(gather_kernel, layout),
        in_specs=[SMEM] + [VMEM] * len(parts),
        out_specs=VMEM,
        out_shape=pltpu.VMEM((sum(part.shape[0] for part in parts), LANES), f32),
        compiler_params=params(4),
        cost_estimate=cost(10, 10),
    )(index, *pinned(*parts))


def pair_factors(top, low):
    top_take, low_take = 1.0 - top, 1.0 - low
    through = top * low
    sends = (low * top_take, low_take)
    low_out = (low_take * through, low, low_take * low * top_take, low_take * low_take)
    top_out = (
        top * low_out[0] + top_take * top,
        top * low_out[1],
        top * low_out[2] + top_take * top_take,
        top * low_out[3],
    )
    return through, sends, top_out, low_out


def tables_kernel(index, own, across_, beside_, corner_, table, mix, decay):
    band = index[0]
    for at, lengths in enumerate((own, across_, beside_, corner_)):
        for level in range(2):
            for variable in range(4):
                row = at * 8 + level * 4 + variable
                decay[row : row + 1, :] = jnp.full((1, LANES), lengths[level, variable], f32)
    decay[...] = jnp.exp(-1.0 / decay[...])

    def factors(at):
        return pair_factors(decay[at * 8 : at * 8 + 4, :], decay[at * 8 + 4 : at * 8 + 8, :])

    def by_band(*values):
        result = values[0]
        for at in range(1, 4):
            result = jnp.where(band == at, values[at], result)
        return result

    through, sends, top_out, low_out = factors(0)
    across, beside, corner = factors(1), factors(2), factors(3)
    through_n, echo_n = beside[0], beside[2][0]
    third = by_band(across[0], corner[0], across[0], across[0])
    third_echo = by_band(across[2][0], corner[2][0], across[2][0], across[2][0])
    fourth_echo = by_band(corner[2][0], across[2][0], corner[2][0], corner[2][0])
    zeta = third * third * fourth_echo + third_echo
    rows = []
    for i in range(2):
        reply = top_out[2 + i]
        rows.append(by_band(sends[i], reply + through * zeta * sends[i], sends[i], reply))
    for i in range(2):
        rows.append(
            by_band(
                sends[i], sends[i], through * echo_n * sends[i] + top_out[2 + i], sends[i]
            )
        )
    rows.append(through)
    for fin, back, *own in (top_out, low_out):
        for i in range(2):
            rows.append(
                by_band(
                    own[i] + back * (through_n * through_n * zeta + echo_n) * sends[i],
                    own[i] + back * zeta * sends[i],
                    own[i] + back * echo_n * sends[i],
                    own[i],
                )
            )
        none = jnp.zeros_like(fin)
        rows.append(by_band(back, fin + back * zeta * through, back, fin))
        rows.append(by_band(back * through_n, none, none, fin * through_n))
        rows.append(by_band(none, back, fin + back * echo_n * through, none))
    for variable in range(4):
        for at, row in enumerate(rows):
            table[variable, at : at + 1, :] = row[variable : variable + 1]
    row = lax.broadcasted_iota(i32, (SUBLANES, LANES), 0)
    for variable in range(4):
        value = jnp.zeros((SUBLANES, LANES), f32)
        downward, keeps = [], []
        for level in range(8):
            other = (level // 2) ^ band
            place = (other & 1) * 2 + lax.shift_right_logical(other, 1)
            at = place * 8 + (level % 2) * 4 + variable
            keep = jnp.broadcast_to(decay[pl.ds(at, 1), :], (SUBLANES, LANES))
            unit = jnp.where(row == place * 2 + level % 2, 1.0, 0.0)
            value = keep * value + (1.0 - keep) * unit
            downward.append(value)
            keeps.append(keep)
        value = jnp.zeros((SUBLANES, LANES), f32)
        upward = [None] * 8
        for level in reversed(range(8)):
            value = keeps[level] * value + (1.0 - keeps[level]) * downward[level]
            upward[level] = value
        for level in range(2):
            mix[level, variable] = by_band(*[upward[2 * at + level] for at in range(4)])


def tables(index, lengths):
    return pl.pallas_call(
        tables_kernel,
        in_specs=[SMEM] * 5,
        out_specs=[VMEM, VMEM],
        out_shape=[
            jax.ShapeDtypeStruct((4, 16, LANES), f32),
            jax.ShapeDtypeStruct((2, 4, SUBLANES, LANES), f32),
        ],
        scratch_shapes=[pltpu.VMEM((32, LANES), f32)],
        compiler_params=params(4),
        cost_estimate=cost(10, 10),
    )(index, *lengths)


def add_kernel(variables, part, near, table, total):
    for place, variable in enumerate(variables):
        weight = table[variable, 4:5, :]
        for column in range(part.shape[2] // LANES):
            at = slice(column * LANES, (column + 1) * LANES)
            total[place, :, at] = part[place, :, at] + weight * near[place, :, at]


def add_near(variables, part, near, table):
    return pl.pallas_call(
        functools.partial(add_kernel, variables),
        in_specs=[VMEM] * 3,
        out_specs=VMEM,
        out_shape=pltpu.VMEM(part.shape, f32),
        compiler_params=params(4),
        cost_estimate=cost(10, 10),
    )(*pinned(part, near, table))


def dense_kernel(variables, own, near, far, met, table, out):
    for place, variable in enumerate(variables):
        for level in range(2):
            weights = [table[variable, 5 + level * 5 + k : 6 + level * 5 + k, :] for k in range(5)]
            for column in range(near.shape[2] // LANES):
                at = slice(column * LANES, (column + 1) * LANES)
                value = weights[0] * own[place, 0, :, at] + weights[1] * own[place, 1, :, at]
                value = value + weights[2] * near[place, :, at] + weights[3] * far[place, :, at]
                out[place, level, :, at] = value + weights[4] * met[place, :, at]


def dense_part(variables, own, near, far, met, table):
    return pl.pallas_call(
        functools.partial(dense_kernel, variables),
        in_specs=[VMEM] * 5,
        out_specs=VMEM,
        out_shape=pltpu.VMEM(own.shape, f32),
        compiler_params=params(4),
        cost_estimate=cost(10, 10),
    )(*pinned(own, near, far, met, table))


def finish_kernel(mix, *rest):
    *dense, out, added, message, sems = rest
    messages, dense = dense[:4], dense[4:]
    _, _, row_count, column_total = dense[0].shape
    column_count = column_total // LANES
    stride = message.shape[0] // SUBLANES
    copies = []
    for chunk, variables in enumerate(CHUNKS):
        for place, variable in enumerate(variables):
            for at, part in enumerate(messages):
                for level in range(2):
                    source = (level * 4 + variable) * stride
                    target = (2 * at + level) * stride
                    message[target : target + stride, :] = part[source : source + stride, :]
            lanes = []
            for column in range(column_count):
                lanes.append(
                    jnp.concatenate(
                        [
                            message[pl.ds(k * column_count + column, SUBLANES, stride=stride), :]
                            for k in range(4)
                        ],
                        axis=0,
                    )
                )
            high, low = split(jnp.concatenate(lanes, axis=1))
            states = jnp.concatenate([high, high, low, low], axis=0)
            inside = [
                message[pl.ds(4 * column_count + k, SUBLANES, stride=stride), :] for k in range(4)
            ]
            for level in range(2):
                mixed = jnp.concatenate([part * mix[level, variable] for part in inside], axis=0)
                high, low = split(mixed)
                mixed = jnp.concatenate([high, low, high, low], axis=0)
                total = dot(mixed, states, (((0,), (0,)), ((), ())))[:row_count]
                added[variable, level] = total + dense[chunk][place, level]
                copies.append(
                    pltpu.make_async_copy(
                        added.at[variable, level],
                        out.at[level, variable],
                        sems.at[2 * variable + level],
                    )
                )
                copies[-1].start()
    for copy in copies:
        copy.wait()


def finish(mix, messages, dense):
    _, _, row_count, column_total = dense[0].shape
    return pl.pallas_call(
        finish_kernel,
        in_specs=[VMEM] * (1 + len(messages) + len(dense)),
        out_specs=HBM,
        out_shape=pltpu.HBM((2, 4, row_count, column_total), f32),
        scratch_shapes=[
            pltpu.VMEM((4, 2, row_count, column_total), f32),
            pltpu.VMEM(messages[0].shape, f32),
            pltpu.SemaphoreType.DMA((8,)),
        ],
        compiler_params=params(12),
        cost_estimate=cost(10, 10),
    )(*pinned(mix, *messages, *dense))


CHUNKS = ((0, 1), (2, 3))
SWAP = [(0, 1), (1, 0), (2, 3), (3, 2)]
CROSS = [(0, 2), (2, 0), (1, 3), (3, 1)]
CORNER = [(0, 3), (3, 0), (1, 2), (2, 1)]
MIDDLE = [(0, 0), (1, 2), (2, 1), (3, 3)]


def four_bands(swept, weights, exits, units, chain, gather, table, mix):
    owns, parts, nears, mets = [], [], [], []

    def filter_some(at, *earlier):
        own, sent, part = longitude_pair(CHUNKS[at], after(swept, *earlier), weights, table)
        owns.append(own)
        parts.append(part)
        nears.append(lax.ppermute(sent, "band", SWAP))
        return part

    def cross_some(at, *earlier):
        part = after(parts[at], *earlier)
        total = add_near(CHUNKS[at], part, nears[at], table)
        mets.append(lax.ppermute(total, "band", MIDDLE))
        return total

    first = filter_some(0)
    response = units(first)

    def before_second_stage(came):
        return (cross_some(0, filter_some(1, came, *response)),)

    exits = exchange(exits, 8, before_second_stage)
    mark = cross_some(1, exits[0])
    messages = exchange(chain([after(exits[0], mark)] + exits[1:], response), 8)
    messages = gather(messages)
    across = lax.ppermute(messages, "band", CROSS)
    beside = lax.ppermute(messages, "band", SWAP)
    dense = []
    for at, variables in enumerate(CHUNKS):
        met = after(mets[at], messages)
        far = lax.ppermute(met, "band", SWAP)
        dense.append(dense_part(variables, owns[at], nears[at], far, met, table))
    corner = lax.ppermute(after(across, *dense), "band", SWAP)
    return finish(mix, (messages, across, beside, corner), dense)


def prefix(part, axis, combine, identity, reverse):
    count = lax.axis_size(axis)
    place = lax.axis_index(axis)
    ahead = count - 1 - place if reverse else place
    gathered = jax.tree.map(lambda a: lax.all_gather(a, axis), part)
    state = jax.tree.map(lambda a, e: jnp.zeros_like(a) + jnp.asarray(e, a.dtype), part, identity)

    def one(turn, state):
        source = count - 1 - turn if reverse else turn
        return combine(
            state, jax.tree.map(lambda a: lax.dynamic_index_in_dim(a, source, 0, False), gathered)
        )

    return lax.fori_loop(0, ahead, one, state)


def combine(earlier, later):
    return (earlier[0] * later[0], later[0] * earlier[1] + later[1])


def level_chain(values, decays, reverse):
    level_count = values.shape[0]
    visit_order = range(level_count - 1, -1, -1) if reverse else range(level_count)
    carry_state = jnp.zeros_like(values[0])
    level_gain = jnp.ones((values.shape[1],), f32)
    outputs = [None] * level_count
    carried = [None] * level_count
    for level_index in visit_order:
        factor = decays[level_index][:, None, None]
        carry_state = factor * carry_state + (1.0 - factor) * values[level_index]
        level_gain = level_gain * decays[level_index]
        outputs[level_index] = carry_state
        carried[level_index] = level_gain
    total_decay = level_gain[:, None, None]
    identity = (jnp.ones_like(total_decay), jnp.zeros_like(carry_state))
    incoming = prefix((total_decay, carry_state), "band", combine, identity, reverse)[1]
    return jnp.stack(
        [
            outputs[level_index] + carried[level_index][:, None, None] * incoming
            for level_index in range(level_count)
        ]
    )


def any_bands(swept, weights, exits, units, chain, gather, vert_length):
    column_count, group_count, row_count, _ = swept.shape
    sub_count = lax.axis_size("sub")
    chained = chain(exchange(exits, sub_count), units())
    messages = gather(exchange(chained, sub_count))
    (values,) = longitude(swept, weights, group_count, 0, 1)
    messages = messages.reshape(group_count, -1, LANES)
    states = messages[:, : 4 * column_count].reshape(group_count, 4, -1)
    inside = messages[:, 4 * column_count : 4 * column_count + 4, :row_count]
    values = values + jnp.einsum("gkr,gkc->grc", inside, states, precision=highest)
    decay = jnp.exp(-1.0 / vert_length)
    values = values.reshape(decay.shape + values.shape[1:])
    return level_chain(level_chain(values, decay, False), decay, True)


def per_device(background, obs_columns, obs_owner, obs_cell, lat_length, lon_length, vert_length):
    level_count, var_count, row_count, lon_count = background.shape
    sub_count = lax.axis_size("sub")
    group_count = level_count * var_count
    strip = row_count * lon_count
    column_count = lon_count // LANES
    capacity = 2 * obs_owner.shape[0] // sub_count
    chunk_count = capacity // LANES
    two_chips = lax.axis_size("band") == 4 and level_count == 2 and sub_count == 8
    index = lax.axis_index("sub").astype(i32).reshape(1)
    band = lax.axis_index("band").astype(i32).reshape(1)

    packed = pack_observations(
        after(index, band),
        obs_columns, obs_owner[:, 0], obs_cell, sub_count, strip, capacity
    )
    vert_lengths = []
    if two_chips:
        vert_length = after(vert_length, *packed)
        vert_lengths = [vert_length] + [
            lax.ppermute(vert_length, "band", pairs) for pairs in (CROSS, SWAP, CORNER)
        ]
    space = pltpu.VMEM if two_chips else pltpu.HBM
    weights = prepare(after(lon_length, *packed), lon_count, space)
    got = exchange(packed, sub_count, lambda came: (*vert_lengths, weights[0]))
    ready = list(weights)
    if two_chips:
        table, mix = tables(after(band, got[0]), vert_lengths)
        ready.append(table)

    sizes = (sub_count, group_count, row_count, column_count, chunk_count, strip)
    decay, *totals = make_ready(
        after(index, got[0]),
        lat_length,
        background.reshape(group_count, row_count, lon_count),
        sizes,
    )
    swept, *exits = deposit_and_sweep(
        index, decay, totals, [after(got[0], *ready)] + got[1:], sizes
    )

    def units(*earlier):
        start = after(index, swept, *earlier)
        return unit_responses(start, lat_length, sub_count, row_count)

    def chain(arrived, response):
        inside, leaving = response
        return chain_states(sub_count, index, lon_length, arrived, leaving, inside)

    def gather(parts):
        return gather_messages(arriving_layout(sub_count), index, parts)

    if two_chips:
        return four_bands(swept, weights, exits, units, chain, gather, table, mix)
    return any_bands(swept, weights, exits, units, chain, gather, vert_length)


def solution(mesh):
    placed = (
        P("band", None, "sub", None),
        P("band", None, "sub"),
        P("sub", None),
        P("sub"),
        P("band", None, None),
        P("band", None),
        P("band", None),
    )
    return jax.shard_map(
        per_device,
        mesh=mesh,
        in_specs=placed,
        out_specs=P("band", None, "sub", None),
        check_vma=False,
    )
```

```python
import functools

import jax
import jax.numpy as jnp
from jax import lax
from jax.experimental import pallas as pl
from jax.experimental.pallas import tpu as pltpu
from jax.sharding import PartitionSpec as P

f32 = jnp.float32
i32 = jnp.int32
bf16 = jnp.bfloat16
highest = lax.Precision.HIGHEST

LANES = 128
SUBLANES = 8
BLOCK = 256
CHAINS = 4

VMEM = pl.BlockSpec(memory_space=pltpu.VMEM)
SMEM = pl.BlockSpec(memory_space=pltpu.SMEM)
HBM = pl.BlockSpec(memory_space=pltpu.HBM)


def params(mib):
    return pltpu.CompilerParams(vmem_limit_bytes=mib << 20)


def pinned(*arrays):
    return [pltpu.with_memory_space_constraint(array, pltpu.VMEM) for array in arrays]


def in_hbm(*arrays):
    return [pltpu.with_memory_space_constraint(array, pltpu.HBM) for array in arrays]


EVEN_ODD = ((0, 2, 4, 6), (1, 3, 5, 7))
BY_PAIRS = ((0, 1), (2, 3), (4, 5), (6, 7))


def leaving_layout(sub_count):
    return EVEN_ODD if sub_count == 8 else tuple((k,) for k in range(sub_count))


def arriving_layout(sub_count):
    return BY_PAIRS if sub_count == 8 else tuple((k,) for k in range(sub_count))


def join_kernel(kept, came, *outs):
    rows = kept.shape[0] // len(outs)
    for at, out in enumerate(outs):
        out[:rows, :] = kept[at * rows : (at + 1) * rows, :]
        out[rows:, :] = came[at * rows : (at + 1) * rows, :]


def join_pairs(kept, came, count):
    rows = 2 * kept.shape[0] // count
    return pl.pallas_call(
        join_kernel,
        in_specs=[VMEM] * 2,
        out_specs=[VMEM] * count,
        out_shape=[pltpu.VMEM((rows, LANES), f32)] * count,
        compiler_params=params(4),
        cost_estimate=cost(10, 10),
    )(*pinned(kept, came))


def after(value, *earlier):
    return lax.optimization_barrier((value,) + earlier)[0]


def exchange(parts, sub_count, meanwhile=None):
    def move(part, k):
        return lax.ppermute(part, "sub", [(at, at ^ k) for at in range(sub_count)])

    if sub_count != 8:
        return [parts[0]] + [move(parts[k], k) for k in range(1, sub_count)]
    kept, sent = parts
    came = move(sent, 1)
    if meanwhile is not None:
        kept = after(kept, *meanwhile(came))
    pairs = join_pairs(kept, came, 4)
    return [pairs[0]] + [move(pairs[k], 2 * k) for k in (1, 2, 3)]


def cost(flops, read):
    return pl.CostEstimate(flops=flops, bytes_accessed=read, transcendentals=0)


def dot(a, b, dims=(((1,), (0,)), ((), ()))):
    return lax.dot_general(a, b, dims, preferred_element_type=f32)


def split(x):
    high = x.astype(bf16)
    return high, (x - high.astype(f32)).astype(bf16)


def pack_kernel(sizes, layout, index, owners, cells, values, *rest):
    outs, (packed, places, tally, sorted_, joined, counts, sem) = rest[:-7], rest[-7:]
    sub_count, group_count, chunk_count, strip = sizes
    block_count = owners.shape[0]
    tiles = group_count // SUBLANES
    lane = lax.broadcasted_iota(i32, (SUBLANES, LANES), 1)
    square = lambda axis: lax.broadcasted_iota(i32, (LANES, LANES), axis)
    owner = owners[...]
    picked = [jnp.where(owner == sub, 1.0, 0.0) for sub in range(sub_count)]
    upto = jnp.where(square(0) <= square(1), 1.0, 0.0).astype(bf16)
    ranks = dot(jnp.concatenate(picked, axis=0).astype(bf16), upto)
    wide = lax.broadcasted_iota(i32, (block_count, LANES), 1)
    place = jnp.zeros((block_count, LANES), f32)
    base = jnp.zeros((block_count, LANES), f32)
    totals = jnp.zeros((block_count, LANES), f32)
    for sub in range(sub_count):
        rank = ranks[sub * block_count : (sub + 1) * block_count]
        total = jnp.broadcast_to(rank[:, LANES - 1 :], rank.shape)
        place = jnp.where(owner == sub, rank - 1.0 + base, place)
        totals = jnp.where(wide == sub, total, totals)
        base = base + total
    places[...] = place.astype(i32)
    tally[...] = totals.astype(i32)
    copy = pltpu.make_async_copy(tally, counts, sem)
    copy.start()
    extra = -(group_count + SUBLANES) % 16
    row = square(0)

    def sort_block(block, carry):
        at = pl.multiple_of(block * LANES, LANES)
        parts = [
            *[values[level, :, pl.ds(at, LANES)] for level in range(values.shape[0])],
            jnp.broadcast_to(cells[pl.ds(block, 1), :], (SUBLANES, LANES)).astype(f32),
        ]
        if extra:
            parts.append(jnp.zeros((extra, LANES), f32))
        whole = jnp.concatenate(parts, axis=0)
        rows = whole.shape[0]
        high, rest = whole.astype(bf16), whole
        rest = rest - high.astype(f32)
        middle = rest.astype(bf16)
        low = (rest - middle.astype(f32)).astype(bf16)
        move = jnp.where(row == places[pl.ds(block, 1), :], 1.0, 0.0).astype(bf16)
        moved = dot(
            jnp.concatenate([high, middle, low], axis=0), move, (((1,), (1,)), ((), ()))
        )
        moved = moved[:rows] + moved[rows : 2 * rows] + moved[2 * rows :]
        for tile in range(tiles + 1):
            sorted_[block, tile] = moved[tile * SUBLANES : (tile + 1) * SUBLANES]
        return carry

    lax.fori_loop(0, block_count, sort_block, 0, unroll=8)
    copy.wait()

    def join_block(block, ends):
        start = jnp.int32(0)
        writes, following = [], []
        for sub in range(sub_count):
            end = ends[sub]
            chunk, offset = lax.shift_right_logical(end, 7), end & 127
            for tile in range(tiles + 1):
                turned = pltpu.roll(sorted_[block, tile], (end - start) & 127, 1)
                kept = jnp.where(lane >= offset, turned, joined[sub, chunk, tile])
                writes.append((sub, chunk, tile, kept, turned))
            start = start + counts[block, sub]
            following.append(end + counts[block, sub])
        for sub, chunk, tile, kept, turned in writes:
            joined[sub, chunk, tile] = kept
            joined[sub, chunk + 1, tile] = turned
        return tuple(following)

    ends = lax.fori_loop(0, block_count, join_block, (jnp.int32(0),) * sub_count, unroll=2)
    word_row = chunk_count * group_count
    word_rows = packed.shape[1] - word_row
    for sub in range(sub_count):
        packed[sub, word_row:, :] = jnp.full((word_rows, LANES), 8.0 * strip, f32)
        for chunk in range(chunk_count):
            for tile in range(tiles):
                at = chunk * group_count + tile * SUBLANES
                packed[sub, at : at + SUBLANES, :] = joined[sub, chunk, tile]
            filled = lane + chunk * LANES < ends[sub]
            cell = jnp.where(filled, joined[sub, chunk, tiles], 0.0).astype(i32)
            word = 8 * (cell - (cell & 127)) + ((cell - lane) & 127)
            word = jnp.where(filled, word, 8 * strip).astype(f32)
            packed[sub, word_row + chunk : word_row + chunk + 1, :] = word[:1]
    rows = packed.shape[1]
    for out, members in zip(outs, layout):
        for at, k in enumerate(members):
            out[at * rows : (at + 1) * rows, :] = packed[index[0] ^ k]


def pack_observations(index, obs_values, owners, cells, sub_count, strip, capacity):
    level_count, var_count, obs_count = obs_values.shape
    group_count = level_count * var_count
    chunk_count = capacity // LANES
    block_count = obs_count // LANES
    rows = chunk_count * group_count + SUBLANES * (-(-chunk_count // SUBLANES))
    tiles = group_count // SUBLANES
    layout = leaving_layout(sub_count)
    return pl.pallas_call(
        functools.partial(pack_kernel, (sub_count, group_count, chunk_count, strip), layout),
        out_shape=[pltpu.VMEM((len(members) * rows, LANES), f32) for members in layout],
        in_specs=[SMEM, VMEM, VMEM, VMEM],
        out_specs=[VMEM] * len(layout),
        scratch_shapes=[
            pltpu.VMEM((sub_count, rows, LANES), f32),
            pltpu.VMEM((block_count, LANES), i32),
            pltpu.VMEM((block_count, LANES), i32),
            pltpu.VMEM((block_count, tiles + 1, SUBLANES, LANES), f32),
            pltpu.VMEM((sub_count, chunk_count + 2, tiles + 1, SUBLANES, LANES), f32),
            pltpu.SMEM((block_count, LANES), i32),
            pltpu.SemaphoreType.DMA,
        ],
        compiler_params=params(6),
        cost_estimate=cost(10, 10),
    )(index, *in_hbm(owners.reshape(block_count, LANES), cells.reshape(block_count, LANES), obs_values))


def ready_kernel(sizes, index, lat_length, field, decay, *rest):
    sub_count, group_count, row_count, column_count, chunk_count, strip = sizes
    totals, (loaded, all_lengths, sem, sems) = rest[:CHAINS], rest[CHAINS:]
    tiles = group_count // SUBLANES

    def load(group):
        return pltpu.make_async_copy(field.at[group], loaded.at[group], sems.at[group])

    fetch = pltpu.make_async_copy(lat_length, all_lengths, sem)
    fetch.start()
    for group in range(group_count):
        load(group).start()

    def clear(row, carry):
        for total in totals[1:]:
            for tile in range(tiles):
                for column in range(column_count):
                    total[tile, row, column] = jnp.zeros((SUBLANES, LANES), f32)
        return carry

    lax.fori_loop(0, row_count, clear, 0)
    fetch.wait()
    shift = index[0] * row_count
    for tile in range(tiles):
        lengths = jnp.concatenate(
            [all_lengths[2 * tile + k] for k in range(SUBLANES // 4)], axis=0
        )
        lengths = pltpu.roll(lengths, jnp.where(shift > 0, lengths.shape[1] - shift, 0), 1)
        keep = jnp.exp(-1.0 / lengths[:, :LANES])
        for row in range(row_count):
            decay[row, tile] = jnp.broadcast_to(keep[:, row : row + 1], (SUBLANES, LANES))
    for group in range(group_count):
        load(group).wait()
    for tile in range(tiles):
        groups = slice(tile * SUBLANES, (tile + 1) * SUBLANES)

        def turn_rows(at, carry):
            rows = pl.ds(pl.multiple_of(at * SUBLANES, SUBLANES), SUBLANES)
            for column in range(column_count):
                lanes = slice(column * LANES, (column + 1) * LANES)
                totals[0][tile, rows, column] = jnp.swapaxes(loaded[groups, rows, lanes], 0, 1)
            return carry

        lax.fori_loop(0, row_count // SUBLANES, turn_rows, 0)


def dump_shape(sizes):
    _, group_count, row_count, column_count, _, _ = sizes
    return (group_count // SUBLANES, row_count + 1, column_count, SUBLANES, LANES)


def make_ready(index, lat_length, field, sizes):
    sub_count, group_count, row_count, column_count, chunk_count, strip = sizes
    tiles = group_count // SUBLANES
    return pl.pallas_call(
        functools.partial(ready_kernel, sizes),
        in_specs=[SMEM, HBM, HBM],
        out_specs=[VMEM] * (1 + CHAINS),
        out_shape=[pltpu.VMEM((row_count, tiles, SUBLANES, LANES), f32)]
        + [pltpu.VMEM(dump_shape(sizes), f32)] * CHAINS,
        scratch_shapes=[
            pltpu.VMEM((group_count, row_count, column_count * LANES), f32),
            pltpu.VMEM(lat_length.shape, f32),
            pltpu.SemaphoreType.DMA,
            pltpu.SemaphoreType.DMA((group_count,)),
        ],
        compiler_params=params(6),
        cost_estimate=cost(10, 10),
    )(index, *in_hbm(lat_length, field))


def deposit_kernel(sizes, index, decay, *rest):
    sub_count, group_count, row_count, column_count, chunk_count, strip = sizes
    here, away = arriving_layout(sub_count), leaving_layout(sub_count)
    arrived, swept = rest[: len(here)], rest[len(here) + CHAINS]
    rest = rest[len(here) + CHAINS + 1 :]
    leaving, totals = rest[: len(away)], rest[len(away) :][:CHAINS]
    got, exits, integers, words, word_sems = rest[len(away) + CHAINS :]
    tiles = group_count // SUBLANES
    word_row = chunk_count * group_count
    block_rows = got.shape[1]
    word_rows = block_rows - word_row
    sources = [(part, at) for part, members in zip(arrived, here) for at in range(len(members))]
    for source, (part, at) in enumerate(sources):
        block = part[at * block_rows : (at + 1) * block_rows, :]
        integers[source * word_rows : (source + 1) * word_rows, :] = block[word_row:].astype(i32)

    def hand_over(source):
        span = pl.ds(source * word_rows, word_rows)
        return pltpu.make_async_copy(integers.at[span], words.at[span], word_sems.at[source])

    for source in range(sub_count):
        hand_over(source).start()
    for source, (part, at) in enumerate(sources):
        got[source] = part[at * block_rows : (at + 1) * block_rows, :]
    lane = lax.broadcasted_iota(i32, (SUBLANES, LANES), 1)

    def one_source(source, carry):
        first = source * word_rows
        hand_over(source).wait()

        def more(chunk):
            last = jnp.minimum(chunk, chunk_count - 1)
            return (chunk < chunk_count) & (words[first + last, 0] < 8 * strip)

        def one_chunk(chunk):
            blocks = [
                got[
                    source,
                    pl.ds(pl.multiple_of(chunk * group_count + tile * SUBLANES, 8), SUBLANES),
                    :,
                ]
                for tile in range(tiles)
            ]
            for slot in range(LANES):
                word = words[first + chunk, slot]
                target = pl.multiple_of(lax.shift_right_logical(word, 7), SUBLANES)
                turn = word & 127
                for tile in range(tiles):
                    value = pltpu.roll(jnp.where(lane == slot, blocks[tile], 0.0), turn, 1)
                    total = flat[slot % CHAINS]
                    at = pl.ds(target, SUBLANES)
                    total[tile, at, :] = total[tile, at, :] + value
            return chunk + 1

        lax.while_loop(more, one_chunk, jnp.int32(0))
        return carry

    flat = [total.reshape(tiles, -1, LANES) for total in totals]
    lax.fori_loop(0, sub_count, one_source, 0)
    for tile in range(tiles):
        groups = slice(tile * SUBLANES, (tile + 1) * SUBLANES)

        def sweep(sources, target, turn):
            def one_row(step, state):
                row = row_count - 1 - step if turn % 2 else step
                keep = decay[row, tile]
                take = 1.0 - keep
                following = []
                for column in range(column_count):
                    value = sources[0][tile, row, column]
                    for source in sources[1:]:
                        value = value + source[tile, row, column]
                    value = keep * state[column] + take * value
                    target[tile, row, column] = value
                    following.append(value)
                return tuple(following)

            nothing = tuple(jnp.zeros((SUBLANES, LANES), f32) for _ in range(column_count))
            state = lax.fori_loop(0, row_count, one_row, nothing, unroll=4)
            message_rows = 4 * column_count
            for column in range(column_count):
                at = tile * SUBLANES * message_rows + turn * column_count + column
                exits[pl.ds(at, SUBLANES, stride=message_rows), :] = state[column]

        for turn in range(4):
            sources = totals if turn == 0 else totals[turn % 2 : turn % 2 + 1]
            sweep(sources, totals[1 - turn % 2], turn)

        def turn_rows(at, carry):
            rows = pl.ds(pl.multiple_of(at * SUBLANES, SUBLANES), SUBLANES)
            for column in range(column_count):
                swept[column, groups, rows, :] = jnp.swapaxes(totals[0][tile, rows, column], 0, 1)
            return carry

        lax.fori_loop(0, row_count // SUBLANES, turn_rows, 0)
    rows = 4 * column_count
    for out, members in zip(leaving, away):
        for at, k in enumerate(members):
            first = pl.multiple_of((index[0] ^ k) * rows, SUBLANES)
            out[at * rows : (at + 1) * rows, :] = exits[pl.ds(first, rows), :]


def deposit_and_sweep(index, decay, totals, got, sizes):
    sub_count, group_count, row_count, column_count, chunk_count, strip = sizes
    here, away = arriving_layout(sub_count), leaving_layout(sub_count)
    rows = got[0].shape[0] // len(here[0])
    word_rows = rows - chunk_count * group_count
    exit_rows = 4 * column_count
    results = pl.pallas_call(
        functools.partial(deposit_kernel, sizes),
        out_shape=[pltpu.VMEM((column_count, group_count, row_count, LANES), f32)]
        + [pltpu.VMEM((len(members) * exit_rows, LANES), f32) for members in away]
        + [pltpu.VMEM(dump_shape(sizes), f32)] * CHAINS,
        in_specs=[SMEM] + [VMEM] * (1 + len(here) + CHAINS),
        out_specs=[VMEM] * (1 + len(away) + CHAINS),
        scratch_shapes=[
            pltpu.VMEM((sub_count, rows, LANES), f32),
            pltpu.VMEM((group_count * exit_rows, LANES), f32),
            pltpu.VMEM((sub_count * word_rows, LANES), i32),
            pltpu.SMEM((sub_count * word_rows, LANES), i32),
            pltpu.SemaphoreType.DMA((sub_count,)),
        ],
        input_output_aliases={
            2 + len(here) + k: 1 + len(away) + k for k in range(CHAINS)
        },
        compiler_params=params(6),
        cost_estimate=cost(10, 10),
    )(index, *pinned(decay, *got, *totals))
    return results[: 1 + len(away)]


def unit_kernel(sizes, index, lat_length, inside, leaving, decay, held):
    sub_count, row_count = sizes
    group = index[0]
    decay[...] = jnp.zeros(decay.shape, f32)
    lengths = lat_length[group // 4, pl.ds(group % 4, 1), :]
    keep = jnp.exp(-1.0 / lengths)
    for sub in range(sub_count):
        part = keep[:, sub * row_count : (sub + 1) * row_count]
        decay[4 * sub : 4 * sub + 4, :row_count] = jnp.broadcast_to(part, (4, row_count))
    decay[...] = jnp.transpose(decay[...], (1, 0))
    held[...] = jnp.zeros(held.shape, f32)
    state_of = lax.broadcasted_iota(i32, (1, LANES), 1) & 3
    for turn in range(4):

        def one_row(step, state, turn=turn):
            row = row_count - 1 - step if turn % 2 else step
            keep = decay[pl.ds(row, 1), :]
            value = keep * state + (1.0 - keep) * held[pl.ds(row, 1), :]
            held[pl.ds(row, 1), :] = value
            return value

        enter = jnp.where(state_of == turn, 1.0, 0.0)
        state = lax.fori_loop(0, row_count, one_row, enter, unroll=8)
        leaving[turn : turn + 1, :] = state
    inside[...] = jnp.transpose(held[...], (1, 0))


def unit_responses(index, lat_length, sub_count, row_count):
    return pl.pallas_call(
        functools.partial(unit_kernel, (sub_count, row_count)),
        in_specs=[SMEM, VMEM],
        out_specs=[VMEM, VMEM],
        out_shape=[
            pltpu.VMEM((LANES, LANES), f32),
            jax.ShapeDtypeStruct((4, LANES), f32),
        ],
        scratch_shapes=[pltpu.VMEM((LANES, LANES), f32)] * 2,
        compiler_params=params(4),
        cost_estimate=cost(10, 10),
    )(index, lat_length)


def circle_weights(length, block_count, near_high, near_low, moment, spread):
    def ramp(shape, axis):
        return lax.broadcasted_iota(i32, shape, axis)

    def twice(x):
        return jnp.concatenate([x, x], axis=1)

    rate = -1.0 / jnp.full((1, LANES), length, f32)
    decay = jnp.exp(rate)
    gain = ((1.0 - decay) / (1.0 + decay)) ** 2
    centre = (1.0 + decay * decay) / (1.0 - decay * decay)
    turn = jnp.exp(rate * float(BLOCK * block_count))
    lag = float(BLOCK * block_count) * turn / (1.0 - turn)
    full_gain = gain / (1.0 - turn)

    shape = (BLOCK, BLOCK)
    gap = jnp.abs(ramp(shape, 0) - ramp(shape, 1)).astype(f32)
    near = twice(gain) * jnp.exp(twice(rate) * gap) * (gap + twice(centre))
    high, low = split(near)
    near_high[0] = high
    near_low[0] = low
    shape = (BLOCK, LANES)
    kind = ramp(shape, 1) & 3
    spot = ramp(shape, 0)
    far = jnp.where(kind < 2, BLOCK - spot, spot).astype(f32)
    sums = jnp.exp(rate * far) * jnp.where((kind & 1) == 1, far, 1.0)
    high, low = split(sums)
    moment[0, :, :LANES] = high
    moment[0, :, LANES:] = low
    shape = (32, BLOCK)
    kind = ramp(shape, 0) & 3
    block = lax.shift_right_logical(ramp(shape, 0), 2)
    spot = ramp(shape, 1)
    reach = jnp.where(kind < 2, spot, BLOCK - spot).astype(f32)
    for at in range(block_count):
        ahead = jnp.where(kind < 2, at - block, block - at) - 1
        steps = jnp.where(ahead < 0, ahead + block_count, ahead)
        full = reach + (steps * BLOCK).astype(f32)
        weight = twice(full_gain) * jnp.exp(twice(rate) * full)
        lead = full + twice(centre + lag)
        value = jnp.where((kind & 1) == 1, weight, weight * lead)
        value = jnp.where(block < block_count, value, 0.0)
        high, low = split(value)
        spread[0, :32, at * BLOCK : (at + 1) * BLOCK] = high
        spread[0, 32:, at * BLOCK : (at + 1) * BLOCK] = low


def weight_kernel(block_count, lon_length, *outs):
    group = pl.program_id(0)
    circle_weights(lon_length[group // 4, group % 4], block_count, *outs)


def weight_shapes(column_total):
    return [(BLOCK, BLOCK)] * 3 + [(64, column_total)]


def prepare(lon_length, column_total, space):
    group_count = lon_length.size
    shapes = weight_shapes(column_total)
    return pl.pallas_call(
        functools.partial(weight_kernel, column_total // BLOCK),
        grid=(group_count,),
        in_specs=[SMEM],
        out_specs=[pl.BlockSpec((1,) + shape, lambda i: (i, 0, 0)) for shape in shapes],
        out_shape=[space((group_count,) + shape, bf16) for shape in shapes],
        compiler_params=params(10),
        cost_estimate=cost(10, 10),
    )(lon_length)


def circle(pieces, near_high, near_low, moment, spread):
    row_count = pieces[0].shape[0]
    whole = jnp.concatenate(pieces, axis=0)
    high, low = split(whole)
    near = dot(high, near_high) + dot(low, near_high) + dot(high, near_low)
    sums = dot(high, moment)
    sums = sums[:, :LANES] + sums[:, LANES:] + dot(low, moment[:, :LANES])
    lane = lax.broadcasted_iota(i32, (row_count, LANES), 1)
    slot = lax.shift_right_logical(lane, 2) & 7
    moments = jnp.zeros((row_count, LANES), f32)
    for at in range(len(pieces)):
        part = sums[at * row_count : (at + 1) * row_count]
        moments = jnp.where(slot == at, part, moments)
    rest = moments - moments.astype(bf16).astype(f32)
    moments = jnp.where((lax.shift_right_logical(lane, 5) & 1) == 1, rest, moments).astype(bf16)
    spread = jnp.concatenate([spread[:32], spread[:32], spread[32:], spread[32:]], axis=0)
    far = dot(moments, spread)
    return [
        near[at * row_count : (at + 1) * row_count] + far[:, at * BLOCK : (at + 1) * BLOCK]
        for at in range(len(pieces))
    ]


def longitude_kernel(swept, near_high, near_low, moment, spread, out):
    column_count = swept.shape[0]
    pieces = [
        jnp.concatenate([swept[2 * at, 0], swept[2 * at + 1, 0]], axis=1)
        for at in range(column_count // 2)
    ]
    pieces = circle(pieces, near_high[0], near_low[0], moment[0], spread[0])
    for at, piece in enumerate(pieces):
        out[0, :, at * BLOCK : (at + 1) * BLOCK] = piece


def pair_kernel(variables, swept, near_high, near_low, moment, spread, table, own, sent, part):
    column_count = swept.shape[0]
    for place, variable in enumerate(variables):
        for level in range(2):
            group = level * 4 + variable
            pieces = [
                jnp.concatenate([swept[2 * at, group], swept[2 * at + 1, group]], axis=1)
                for at in range(column_count // 2)
            ]
            pieces = circle(
                pieces, near_high[group], near_low[group], moment[group], spread[group]
            )
            for target, first in ((sent, 0), (part, 2)):
                weight = table[variable, first + level : first + level + 1, :]
                weight = jnp.concatenate([weight, weight], axis=1)
                for at, piece in enumerate(pieces):
                    spot = slice(at * BLOCK, (at + 1) * BLOCK)
                    value = weight * piece
                    target[place, :, spot] = target[place, :, spot] + value if level else value
            for at, piece in enumerate(pieces):
                own[place, level, :, at * BLOCK : (at + 1) * BLOCK] = piece


def longitude_pair(variables, swept, weights, table):
    column_count, _, row_count, _ = swept.shape
    shape = (row_count, column_count * LANES)
    count = len(variables)
    return pl.pallas_call(
        functools.partial(pair_kernel, variables),
        in_specs=[VMEM] * 6,
        out_specs=[VMEM] * 3,
        out_shape=[
            pltpu.VMEM((count, 2) + shape, f32),
            pltpu.VMEM((count,) + shape, f32),
            pltpu.VMEM((count,) + shape, f32),
        ],
        compiler_params=params(10),
        cost_estimate=cost(10, 10),
    )(*pinned(swept, *weights, table))


def longitude(swept, weights, count, first, stride):
    column_count, _, row_count, _ = swept.shape
    column_total = column_count * LANES

    def of(i):
        return first + stride * i

    in_specs = [
        pl.BlockSpec((column_count, 1, row_count, LANES), lambda i: (0, of(i), 0, 0)),
        pl.BlockSpec((1, BLOCK, BLOCK), lambda i: (of(i), 0, 0)),
        pl.BlockSpec((1, BLOCK, BLOCK), lambda i: (of(i), 0, 0)),
        pl.BlockSpec((1, BLOCK, BLOCK), lambda i: (of(i), 0, 0)),
        pl.BlockSpec((1, 64, column_total), lambda i: (of(i), 0, 0)),
    ]
    out_specs = [pl.BlockSpec((1, row_count, column_total), lambda i: (i, 0, 0))]
    out_shape = [jax.ShapeDtypeStruct((count, row_count, column_total), f32)]
    operands = [swept, *weights]
    return pl.pallas_call(
        longitude_kernel,
        grid=(count,),
        in_specs=in_specs,
        out_specs=out_specs,
        out_shape=out_shape,
        compiler_params=params(14),
        cost_estimate=cost(10, 10),
    )(*operands)


def chain_kernel(sub_count, index, lon_length, leaving, inside, *rest):
    here, away = arriving_layout(sub_count), leaving_layout(sub_count)
    arrived, outs = rest[: len(here)], rest[len(here) :][: len(away)]
    exits, out, held, *weights = rest[len(here) + len(away) :]
    rows = exits.shape[1]
    for part, members in zip(arrived, here):
        for at, k in enumerate(members):
            exits[index[0] ^ k] = part[at * rows : (at + 1) * rows, :]
    column_count = exits.shape[1] // 4
    shape = (column_count, LANES)
    group = index[0]
    circle_weights(lon_length[group // 4, group % 4], column_count // 2, *weights)
    entering = {}
    for turn in range(4):
        order = list(range(sub_count))
        if turn % 2:
            order.reverse()
        state = jnp.zeros(shape, f32)
        for block in order:
            entering[turn, block] = state
            at = (turn * sub_count + block) * column_count
            held[at : at + column_count, :] = state
            state = exits[block, turn * column_count : (turn + 1) * column_count, :]
            for other in range(turn + 1):
                state = state + leaving[turn, block * 4 + other] * entering[other, block]
    pieces = []
    for at in range(column_count // 2):
        pair = [
            held[pl.ds(2 * at + k, 4 * sub_count, stride=column_count), :] for k in range(2)
        ]
        pieces.append(jnp.concatenate(pair, axis=1))
    pieces = circle(pieces, *[weight[0] for weight in weights])
    message_rows = out.shape[0] // sub_count
    for at, piece in enumerate(pieces):
        for k in range(2):
            for turn in range(4):
                place = turn * column_count + 2 * at + k
                out[pl.ds(place, sub_count, stride=message_rows), :] = piece[
                    turn * sub_count : (turn + 1) * sub_count, k * LANES : (k + 1) * LANES
                ]
    for block in range(sub_count):
        at = block * message_rows + 4 * column_count
        out[at : at + 4, :] = inside[block * 4 : (block + 1) * 4, :]
        out[at + 4 : (block + 1) * message_rows, :] = jnp.zeros(
            (message_rows - 4 * column_count - 4, LANES), f32
        )
    for target, members in zip(outs, away):
        for place, k in enumerate(members):
            at = pl.multiple_of((index[0] ^ k) * message_rows, SUBLANES)
            to = place * message_rows
            target[to : to + message_rows, :] = out[pl.ds(at, message_rows), :]


def chain_states(sub_count, index, lon_length, exits, leaving, inside):
    here, away = arriving_layout(sub_count), leaving_layout(sub_count)
    rows = exits[0].shape[0] // len(here[0])
    column_total = rows // 4 * LANES
    message_rows = rows + 8
    return pl.pallas_call(
        functools.partial(chain_kernel, sub_count),
        in_specs=[SMEM, SMEM, SMEM, VMEM] + [VMEM] * len(here),
        out_specs=[VMEM] * len(away),
        scratch_shapes=[
            pltpu.VMEM((sub_count, rows, LANES), f32),
            pltpu.VMEM((sub_count * message_rows, LANES), f32),
            pltpu.VMEM((sub_count * rows, LANES), f32),
        ]
        + [pltpu.VMEM((1,) + shape, bf16) for shape in weight_shapes(column_total)],
        out_shape=[
            pltpu.VMEM((len(members) * message_rows, LANES), f32) for members in away
        ],
        compiler_params=params(16),
        cost_estimate=cost(10, 10),
    )(index, lon_length, leaving, *pinned(inside, *exits))


def gather_kernel(layout, index, *rest):
    *parts, out = rest
    rows = out.shape[0] // sum(len(members) for members in layout)
    for part, members in zip(parts, layout):
        for place, k in enumerate(members):
            at = pl.multiple_of((index[0] ^ k) * rows, SUBLANES)
            out[pl.ds(at, rows), :] = part[place * rows : (place + 1) * rows, :]


def gather_messages(layout, index, parts):
    return pl.pallas_call(
        functools.partial(gather_kernel, layout),
        in_specs=[SMEM] + [VMEM] * len(parts),
        out_specs=VMEM,
        out_shape=pltpu.VMEM((sum(part.shape[0] for part in parts), LANES), f32),
        compiler_params=params(4),
        cost_estimate=cost(10, 10),
    )(index, *pinned(*parts))


def pair_factors(top, low):
    top_take, low_take = 1.0 - top, 1.0 - low
    through = top * low
    sends = (low * top_take, low_take)
    low_out = (low_take * through, low, low_take * low * top_take, low_take * low_take)
    top_out = (
        top * low_out[0] + top_take * top,
        top * low_out[1],
        top * low_out[2] + top_take * top_take,
        top * low_out[3],
    )
    return through, sends, top_out, low_out


def tables_kernel(index, own, across_, beside_, corner_, table, mix, decay):
    band = index[0]
    for at, lengths in enumerate((own, across_, beside_, corner_)):
        for level in range(2):
            for variable in range(4):
                row = at * 8 + level * 4 + variable
                decay[row : row + 1, :] = jnp.full((1, LANES), lengths[level, variable], f32)
    decay[...] = jnp.exp(-1.0 / decay[...])

    def factors(at):
        return pair_factors(decay[at * 8 : at * 8 + 4, :], decay[at * 8 + 4 : at * 8 + 8, :])

    def by_band(*values):
        result = values[0]
        for at in range(1, 4):
            result = jnp.where(band == at, values[at], result)
        return result

    through, sends, top_out, low_out = factors(0)
    across, beside, corner = factors(1), factors(2), factors(3)
    through_n, echo_n = beside[0], beside[2][0]
    third = by_band(across[0], corner[0], across[0], across[0])
    third_echo = by_band(across[2][0], corner[2][0], across[2][0], across[2][0])
    fourth_echo = by_band(corner[2][0], across[2][0], corner[2][0], corner[2][0])
    zeta = third * third * fourth_echo + third_echo
    rows = []
    for i in range(2):
        reply = top_out[2 + i]
        rows.append(by_band(sends[i], reply + through * zeta * sends[i], sends[i], reply))
    for i in range(2):
        rows.append(
            by_band(
                sends[i], sends[i], through * echo_n * sends[i] + top_out[2 + i], sends[i]
            )
        )
    rows.append(through)
    for fin, back, *own in (top_out, low_out):
        for i in range(2):
            rows.append(
                by_band(
                    own[i] + back * (through_n * through_n * zeta + echo_n) * sends[i],
                    own[i] + back * zeta * sends[i],
                    own[i] + back * echo_n * sends[i],
                    own[i],
                )
            )
        none = jnp.zeros_like(fin)
        rows.append(by_band(back, fin + back * zeta * through, back, fin))
        rows.append(by_band(back * through_n, none, none, fin * through_n))
        rows.append(by_band(none, back, fin + back * echo_n * through, none))
    for variable in range(4):
        for at, row in enumerate(rows):
            table[variable, at : at + 1, :] = row[variable : variable + 1]
    row = lax.broadcasted_iota(i32, (SUBLANES, LANES), 0)
    for variable in range(4):
        value = jnp.zeros((SUBLANES, LANES), f32)
        downward, keeps = [], []
        for level in range(8):
            other = (level // 2) ^ band
            place = (other & 1) * 2 + lax.shift_right_logical(other, 1)
            at = place * 8 + (level % 2) * 4 + variable
            keep = jnp.broadcast_to(decay[pl.ds(at, 1), :], (SUBLANES, LANES))
            unit = jnp.where(row == place * 2 + level % 2, 1.0, 0.0)
            value = keep * value + (1.0 - keep) * unit
            downward.append(value)
            keeps.append(keep)
        value = jnp.zeros((SUBLANES, LANES), f32)
        upward = [None] * 8
        for level in reversed(range(8)):
            value = keeps[level] * value + (1.0 - keeps[level]) * downward[level]
            upward[level] = value
        for level in range(2):
            mix[level, variable] = by_band(*[upward[2 * at + level] for at in range(4)])


def tables(index, lengths):
    return pl.pallas_call(
        tables_kernel,
        in_specs=[SMEM] * 5,
        out_specs=[VMEM, VMEM],
        out_shape=[
            jax.ShapeDtypeStruct((4, 16, LANES), f32),
            jax.ShapeDtypeStruct((2, 4, SUBLANES, LANES), f32),
        ],
        scratch_shapes=[pltpu.VMEM((32, LANES), f32)],
        compiler_params=params(4),
        cost_estimate=cost(10, 10),
    )(index, *lengths)


def add_kernel(variables, part, near, table, total):
    for place, variable in enumerate(variables):
        weight = table[variable, 4:5, :]
        for column in range(part.shape[2] // LANES):
            at = slice(column * LANES, (column + 1) * LANES)
            total[place, :, at] = part[place, :, at] + weight * near[place, :, at]


def add_near(variables, part, near, table):
    return pl.pallas_call(
        functools.partial(add_kernel, variables),
        in_specs=[VMEM] * 3,
        out_specs=VMEM,
        out_shape=pltpu.VMEM(part.shape, f32),
        compiler_params=params(4),
        cost_estimate=cost(10, 10),
    )(*pinned(part, near, table))


def dense_kernel(variables, own, near, far, met, table, out):
    for place, variable in enumerate(variables):
        for level in range(2):
            weights = [table[variable, 5 + level * 5 + k : 6 + level * 5 + k, :] for k in range(5)]
            for column in range(near.shape[2] // LANES):
                at = slice(column * LANES, (column + 1) * LANES)
                value = weights[0] * own[place, 0, :, at] + weights[1] * own[place, 1, :, at]
                value = value + weights[2] * near[place, :, at] + weights[3] * far[place, :, at]
                out[place, level, :, at] = value + weights[4] * met[place, :, at]


def dense_part(variables, own, near, far, met, table):
    return pl.pallas_call(
        functools.partial(dense_kernel, variables),
        in_specs=[VMEM] * 5,
        out_specs=VMEM,
        out_shape=pltpu.VMEM(own.shape, f32),
        compiler_params=params(4),
        cost_estimate=cost(10, 10),
    )(*pinned(own, near, far, met, table))


def finish_kernel(mix, *rest):
    *dense, out, added, message, sems = rest
    messages, dense = dense[:4], dense[4:]
    _, _, row_count, column_total = dense[0].shape
    column_count = column_total // LANES
    stride = message.shape[0] // SUBLANES
    copies = []
    for chunk, variables in enumerate(CHUNKS):
        for place, variable in enumerate(variables):
            for at, part in enumerate(messages):
                for level in range(2):
                    source = (level * 4 + variable) * stride
                    target = (2 * at + level) * stride
                    message[target : target + stride, :] = part[source : source + stride, :]
            lanes = []
            for column in range(column_count):
                lanes.append(
                    jnp.concatenate(
                        [
                            message[pl.ds(k * column_count + column, SUBLANES, stride=stride), :]
                            for k in range(4)
                        ],
                        axis=0,
                    )
                )
            high, low = split(jnp.concatenate(lanes, axis=1))
            states = jnp.concatenate([high, high, low, low], axis=0)
            inside = [
                message[pl.ds(4 * column_count + k, SUBLANES, stride=stride), :] for k in range(4)
            ]
            for level in range(2):
                mixed = jnp.concatenate([part * mix[level, variable] for part in inside], axis=0)
                high, low = split(mixed)
                mixed = jnp.concatenate([high, low, high, low], axis=0)
                total = dot(mixed, states, (((0,), (0,)), ((), ())))[:row_count]
                added[variable, level] = total + dense[chunk][place, level]
                copies.append(
                    pltpu.make_async_copy(
                        added.at[variable, level],
                        out.at[level, variable],
                        sems.at[2 * variable + level],
                    )
                )
                copies[-1].start()
    for copy in copies:
        copy.wait()


def finish(mix, messages, dense):
    _, _, row_count, column_total = dense[0].shape
    return pl.pallas_call(
        finish_kernel,
        in_specs=[VMEM] * (1 + len(messages) + len(dense)),
        out_specs=HBM,
        out_shape=pltpu.HBM((2, 4, row_count, column_total), f32),
        scratch_shapes=[
            pltpu.VMEM((4, 2, row_count, column_total), f32),
            pltpu.VMEM(messages[0].shape, f32),
            pltpu.SemaphoreType.DMA((8,)),
        ],
        compiler_params=params(12),
        cost_estimate=cost(10, 10),
    )(*pinned(mix, *messages, *dense))


CHUNKS = ((0, 1), (2, 3))
SWAP = [(0, 1), (1, 0), (2, 3), (3, 2)]
CROSS = [(0, 2), (2, 0), (1, 3), (3, 1)]
CORNER = [(0, 3), (3, 0), (1, 2), (2, 1)]
MIDDLE = [(0, 0), (1, 2), (2, 1), (3, 3)]


def four_bands(swept, weights, exits, units, chain, gather, table, mix):
    owns, parts, nears, mets = [], [], [], []

    def filter_some(at, *earlier):
        own, sent, part = longitude_pair(CHUNKS[at], after(swept, *earlier), weights, table)
        owns.append(own)
        parts.append(part)
        nears.append(lax.ppermute(sent, "band", SWAP))
        return part

    def cross_some(at, *earlier):
        part = after(parts[at], *earlier)
        total = add_near(CHUNKS[at], part, nears[at], table)
        mets.append(lax.ppermute(total, "band", MIDDLE))
        return total

    first = filter_some(0)
    response = units(first)

    def before_second_stage(came):
        return (cross_some(0, filter_some(1, came, *response)),)

    exits = exchange(exits, 8, before_second_stage)
    mark = cross_some(1, exits[0])
    messages = exchange(chain([after(exits[0], mark)] + exits[1:], response), 8)
    messages = gather(messages)
    across = lax.ppermute(messages, "band", CROSS)
    beside = lax.ppermute(messages, "band", SWAP)
    dense = []
    for at, variables in enumerate(CHUNKS):
        met = after(mets[at], messages)
        far = lax.ppermute(met, "band", SWAP)
        dense.append(dense_part(variables, owns[at], nears[at], far, met, table))
    corner = lax.ppermute(after(across, *dense), "band", SWAP)
    return finish(mix, (messages, across, beside, corner), dense)


def prefix(part, axis, combine, identity, reverse):
    count = lax.axis_size(axis)
    place = lax.axis_index(axis)
    ahead = count - 1 - place if reverse else place
    gathered = jax.tree.map(lambda a: lax.all_gather(a, axis), part)
    state = jax.tree.map(lambda a, e: jnp.zeros_like(a) + jnp.asarray(e, a.dtype), part, identity)

    def one(turn, state):
        source = count - 1 - turn if reverse else turn
        return combine(
            state, jax.tree.map(lambda a: lax.dynamic_index_in_dim(a, source, 0, False), gathered)
        )

    return lax.fori_loop(0, ahead, one, state)


def combine(earlier, later):
    return (earlier[0] * later[0], later[0] * earlier[1] + later[1])


def level_chain(values, decays, reverse):
    level_count = values.shape[0]
    visit_order = range(level_count - 1, -1, -1) if reverse else range(level_count)
    carry_state = jnp.zeros_like(values[0])
    level_gain = jnp.ones((values.shape[1],), f32)
    outputs = [None] * level_count
    carried = [None] * level_count
    for level_index in visit_order:
        factor = decays[level_index][:, None, None]
        carry_state = factor * carry_state + (1.0 - factor) * values[level_index]
        level_gain = level_gain * decays[level_index]
        outputs[level_index] = carry_state
        carried[level_index] = level_gain
    total_decay = level_gain[:, None, None]
    identity = (jnp.ones_like(total_decay), jnp.zeros_like(carry_state))
    incoming = prefix((total_decay, carry_state), "band", combine, identity, reverse)[1]
    return jnp.stack(
        [
            outputs[level_index] + carried[level_index][:, None, None] * incoming
            for level_index in range(level_count)
        ]
    )


def any_bands(swept, weights, exits, units, chain, gather, vert_length):
    column_count, group_count, row_count, _ = swept.shape
    sub_count = lax.axis_size("sub")
    chained = chain(exchange(exits, sub_count), units())
    messages = gather(exchange(chained, sub_count))
    (values,) = longitude(swept, weights, group_count, 0, 1)
    messages = messages.reshape(group_count, -1, LANES)
    states = messages[:, : 4 * column_count].reshape(group_count, 4, -1)
    inside = messages[:, 4 * column_count : 4 * column_count + 4, :row_count]
    values = values + jnp.einsum("gkr,gkc->grc", inside, states, precision=highest)
    decay = jnp.exp(-1.0 / vert_length)
    values = values.reshape(decay.shape + values.shape[1:])
    return level_chain(level_chain(values, decay, False), decay, True)


def per_device(background, obs_columns, obs_owner, obs_cell, lat_length, lon_length, vert_length):
    level_count, var_count, row_count, lon_count = background.shape
    sub_count = lax.axis_size("sub")
    group_count = level_count * var_count
    strip = row_count * lon_count
    column_count = lon_count // LANES
    capacity = 2 * obs_owner.shape[0] // sub_count
    chunk_count = capacity // LANES
    two_chips = lax.axis_size("band") == 4 and level_count == 2 and sub_count == 8
    index = lax.axis_index("sub").astype(i32).reshape(1)
    band = lax.axis_index("band").astype(i32).reshape(1)

    packed = pack_observations(
        after(index, band),
        obs_columns, obs_owner[:, 0], obs_cell, sub_count, strip, capacity
    )
    vert_lengths = []
    if two_chips:
        vert_length = after(vert_length, *packed)
        vert_lengths = [vert_length] + [
            lax.ppermute(vert_length, "band", pairs) for pairs in (CROSS, SWAP, CORNER)
        ]
    space = pltpu.VMEM if two_chips else pltpu.HBM
    weights = prepare(after(lon_length, *packed), lon_count, space)
    got = exchange(packed, sub_count, lambda came: (*vert_lengths, weights[0]))
    ready = list(weights)
    if two_chips:
        table, mix = tables(after(band, got[0]), vert_lengths)
        ready.append(table)

    sizes = (sub_count, group_count, row_count, column_count, chunk_count, strip)
    decay, *totals = make_ready(
        after(index, got[0]),
        lat_length,
        background.reshape(group_count, row_count, lon_count),
        sizes,
    )
    swept, *exits = deposit_and_sweep(
        index, decay, totals, [after(got[0], *ready)] + got[1:], sizes
    )

    def units(*earlier):
        start = after(index, swept, *earlier)
        return unit_responses(start, lat_length, sub_count, row_count)

    def chain(arrived, response):
        inside, leaving = response
        return chain_states(sub_count, index, lon_length, arrived, leaving, inside)

    def gather(parts):
        return gather_messages(arriving_layout(sub_count), index, parts)

    if two_chips:
        return four_bands(swept, weights, exits, units, chain, gather, table, mix)
    return any_bands(swept, weights, exits, units, chain, gather, vert_length)


def solution(mesh):
    placed = (
        P("band", None, "sub", None),
        P("band", None, "sub"),
        P("sub", None),
        P("sub"),
        P("band", None, None),
        P("band", None),
        P("band", None),
    )
    return jax.shard_map(
        per_device,
        mesh=mesh,
        in_specs=placed,
        out_specs=P("band", None, "sub", None),
        check_vma=False,
    )
```

```python
import functools

import jax
import jax.numpy as jnp
from jax import lax
from jax.experimental import pallas as pl
from jax.experimental.pallas import tpu as pltpu
from jax.sharding import PartitionSpec as P

f32 = jnp.float32
i32 = jnp.int32
bf16 = jnp.bfloat16
highest = lax.Precision.HIGHEST

LANES = 128
SUBLANES = 8
BLOCK = 256
CHAINS = 4

VMEM = pl.BlockSpec(memory_space=pltpu.VMEM)
SMEM = pl.BlockSpec(memory_space=pltpu.SMEM)
HBM = pl.BlockSpec(memory_space=pltpu.HBM)


def params(mib):
    return pltpu.CompilerParams(vmem_limit_bytes=mib << 20)


def pinned(*arrays):
    return [pltpu.with_memory_space_constraint(array, pltpu.VMEM) for array in arrays]


def in_hbm(*arrays):
    return [pltpu.with_memory_space_constraint(array, pltpu.HBM) for array in arrays]


EVEN_ODD = ((0, 2, 4, 6), (1, 3, 5, 7))
BY_PAIRS = ((0, 1), (2, 3), (4, 5), (6, 7))


def leaving_layout(sub_count):
    return EVEN_ODD if sub_count == 8 else tuple((k,) for k in range(sub_count))


def arriving_layout(sub_count):
    return BY_PAIRS if sub_count == 8 else tuple((k,) for k in range(sub_count))


def join_kernel(kept, came, *outs):
    rows = kept.shape[0] // len(outs)
    for at, out in enumerate(outs):
        out[:rows, :] = kept[at * rows : (at + 1) * rows, :]
        out[rows:, :] = came[at * rows : (at + 1) * rows, :]


def join_pairs(kept, came, count):
    rows = 2 * kept.shape[0] // count
    return pl.pallas_call(
        join_kernel,
        in_specs=[VMEM] * 2,
        out_specs=[VMEM] * count,
        out_shape=[pltpu.VMEM((rows, LANES), f32)] * count,
        compiler_params=params(4),
        cost_estimate=cost(10, 10),
    )(*pinned(kept, came))


def after(value, *earlier):
    return lax.optimization_barrier((value,) + earlier)[0]


def exchange(parts, sub_count, meanwhile=None):
    def move(part, k):
        return lax.ppermute(part, "sub", [(at, at ^ k) for at in range(sub_count)])

    if sub_count != 8:
        return [parts[0]] + [move(parts[k], k) for k in range(1, sub_count)]
    kept, sent = parts
    came = move(sent, 1)
    if meanwhile is not None:
        kept = after(kept, *meanwhile(came))
    pairs = join_pairs(kept, came, 4)
    return [pairs[0]] + [move(pairs[k], 2 * k) for k in (1, 2, 3)]


def cost(flops, read):
    return pl.CostEstimate(flops=flops, bytes_accessed=read, transcendentals=0)


def dot(a, b, dims=(((1,), (0,)), ((), ()))):
    return lax.dot_general(a, b, dims, preferred_element_type=f32)


def split(x):
    high = x.astype(bf16)
    return high, (x - high.astype(f32)).astype(bf16)


def pack_kernel(sizes, layout, index, owners, cells, values, *rest):
    outs, (packed, places, tally, sorted_, joined, counts, sem) = rest[:-7], rest[-7:]
    sub_count, group_count, chunk_count, strip = sizes
    block_count = owners.shape[0]
    tiles = group_count // SUBLANES
    lane = lax.broadcasted_iota(i32, (SUBLANES, LANES), 1)
    square = lambda axis: lax.broadcasted_iota(i32, (LANES, LANES), axis)
    owner = owners[...]
    picked = [jnp.where(owner == sub, 1.0, 0.0) for sub in range(sub_count)]
    upto = jnp.where(square(0) <= square(1), 1.0, 0.0).astype(bf16)
    ranks = dot(jnp.concatenate(picked, axis=0).astype(bf16), upto)
    wide = lax.broadcasted_iota(i32, (block_count, LANES), 1)
    place = jnp.zeros((block_count, LANES), f32)
    base = jnp.zeros((block_count, LANES), f32)
    totals = jnp.zeros((block_count, LANES), f32)
    for sub in range(sub_count):
        rank = ranks[sub * block_count : (sub + 1) * block_count]
        total = jnp.broadcast_to(rank[:, LANES - 1 :], rank.shape)
        place = jnp.where(owner == sub, rank - 1.0 + base, place)
        totals = jnp.where(wide == sub, total, totals)
        base = base + total
    places[...] = place.astype(i32)
    tally[...] = totals.astype(i32)
    copy = pltpu.make_async_copy(tally, counts, sem)
    copy.start()
    extra = -(group_count + SUBLANES) % 16
    row = square(0)

    def sort_block(block, carry):
        at = pl.multiple_of(block * LANES, LANES)
        parts = [
            *[values[level, :, pl.ds(at, LANES)] for level in range(values.shape[0])],
            jnp.broadcast_to(cells[pl.ds(block, 1), :], (SUBLANES, LANES)).astype(f32),
        ]
        if extra:
            parts.append(jnp.zeros((extra, LANES), f32))
        whole = jnp.concatenate(parts, axis=0)
        rows = whole.shape[0]
        high, rest = whole.astype(bf16), whole
        rest = rest - high.astype(f32)
        middle = rest.astype(bf16)
        low = (rest - middle.astype(f32)).astype(bf16)
        move = jnp.where(row == places[pl.ds(block, 1), :], 1.0, 0.0).astype(bf16)
        moved = dot(
            jnp.concatenate([high, middle, low], axis=0), move, (((1,), (1,)), ((), ()))
        )
        moved = moved[:rows] + moved[rows : 2 * rows] + moved[2 * rows :]
        for tile in range(tiles + 1):
            sorted_[block, tile] = moved[tile * SUBLANES : (tile + 1) * SUBLANES]
        return carry

    lax.fori_loop(0, block_count, sort_block, 0, unroll=16)
    copy.wait()

    def join_block(block, ends):
        start = jnp.int32(0)
        writes, following = [], []
        for sub in range(sub_count):
            end = ends[sub]
            chunk, offset = lax.shift_right_logical(end, 7), end & 127
            for tile in range(tiles + 1):
                turned = pltpu.roll(sorted_[block, tile], (end - start) & 127, 1)
                kept = jnp.where(lane >= offset, turned, joined[sub, chunk, tile])
                writes.append((sub, chunk, tile, kept, turned))
            start = start + counts[block, sub]
            following.append(end + counts[block, sub])
        for sub, chunk, tile, kept, turned in writes:
            joined[sub, chunk, tile] = kept
            joined[sub, chunk + 1, tile] = turned
        return tuple(following)

    ends = lax.fori_loop(0, block_count, join_block, (jnp.int32(0),) * sub_count, unroll=8)
    word_row = chunk_count * group_count
    word_rows = packed.shape[1] - word_row
    for sub in range(sub_count):
        packed[sub, word_row:, :] = jnp.full((word_rows, LANES), 8.0 * strip, f32)
        for chunk in range(chunk_count):
            for tile in range(tiles):
                at = chunk * group_count + tile * SUBLANES
                packed[sub, at : at + SUBLANES, :] = joined[sub, chunk, tile]
            filled = lane + chunk * LANES < ends[sub]
            cell = jnp.where(filled, joined[sub, chunk, tiles], 0.0).astype(i32)
            word = 8 * (cell - (cell & 127)) + ((cell - lane) & 127)
            word = jnp.where(filled, word, 8 * strip).astype(f32)
            packed[sub, word_row + chunk : word_row + chunk + 1, :] = word[:1]
    rows = packed.shape[1]
    for out, members in zip(outs, layout):
        for at, k in enumerate(members):
            out[at * rows : (at + 1) * rows, :] = packed[index[0] ^ k]


def pack_observations(index, obs_values, owners, cells, sub_count, strip, capacity):
    level_count, var_count, obs_count = obs_values.shape
    group_count = level_count * var_count
    chunk_count = capacity // LANES
    block_count = obs_count // LANES
    rows = chunk_count * group_count + SUBLANES * (-(-chunk_count // SUBLANES))
    tiles = group_count // SUBLANES
    layout = leaving_layout(sub_count)
    return pl.pallas_call(
        functools.partial(pack_kernel, (sub_count, group_count, chunk_count, strip), layout),
        out_shape=[pltpu.VMEM((len(members) * rows, LANES), f32) for members in layout],
        in_specs=[SMEM, VMEM, VMEM, VMEM],
        out_specs=[VMEM] * len(layout),
        scratch_shapes=[
            pltpu.VMEM((sub_count, rows, LANES), f32),
            pltpu.VMEM((block_count, LANES), i32),
            pltpu.VMEM((block_count, LANES), i32),
            pltpu.VMEM((block_count, tiles + 1, SUBLANES, LANES), f32),
            pltpu.VMEM((sub_count, chunk_count + 2, tiles + 1, SUBLANES, LANES), f32),
            pltpu.SMEM((block_count, LANES), i32),
            pltpu.SemaphoreType.DMA,
        ],
        compiler_params=params(6),
        cost_estimate=cost(10, 10),
    )(index, *in_hbm(owners.reshape(block_count, LANES), cells.reshape(block_count, LANES), obs_values))


def ready_kernel(sizes, index, lat_length, field, decay, *rest):
    sub_count, group_count, row_count, column_count, chunk_count, strip = sizes
    totals, (loaded, all_lengths, sem, sems) = rest[:CHAINS], rest[CHAINS:]
    tiles = group_count // SUBLANES

    def load(group):
        return pltpu.make_async_copy(field.at[group], loaded.at[group], sems.at[group])

    fetch = pltpu.make_async_copy(lat_length, all_lengths, sem)
    fetch.start()
    for group in range(group_count):
        load(group).start()

    def clear(row, carry):
        for total in totals[1:]:
            for tile in range(tiles):
                for column in range(column_count):
                    total[tile, row, column] = jnp.zeros((SUBLANES, LANES), f32)
        return carry

    lax.fori_loop(0, row_count, clear, 0)
    fetch.wait()
    shift = index[0] * row_count
    for tile in range(tiles):
        lengths = jnp.concatenate(
            [all_lengths[2 * tile + k] for k in range(SUBLANES // 4)], axis=0
        )
        lengths = pltpu.roll(lengths, jnp.where(shift > 0, lengths.shape[1] - shift, 0), 1)
        keep = jnp.exp(-1.0 / lengths[:, :LANES])
        for row in range(row_count):
            decay[row, tile] = jnp.broadcast_to(keep[:, row : row + 1], (SUBLANES, LANES))
    for group in range(group_count):
        load(group).wait()
    for tile in range(tiles):
        groups = slice(tile * SUBLANES, (tile + 1) * SUBLANES)

        def turn_rows(at, carry):
            rows = pl.ds(pl.multiple_of(at * SUBLANES, SUBLANES), SUBLANES)
            for column in range(column_count):
                lanes = slice(column * LANES, (column + 1) * LANES)
                totals[0][tile, rows, column] = jnp.swapaxes(loaded[groups, rows, lanes], 0, 1)
            return carry

        lax.fori_loop(0, row_count // SUBLANES, turn_rows, 0)


def dump_shape(sizes):
    _, group_count, row_count, column_count, _, _ = sizes
    return (group_count // SUBLANES, row_count + 1, column_count, SUBLANES, LANES)


def make_ready(index, lat_length, field, sizes):
    sub_count, group_count, row_count, column_count, chunk_count, strip = sizes
    tiles = group_count // SUBLANES
    return pl.pallas_call(
        functools.partial(ready_kernel, sizes),
        in_specs=[SMEM, HBM, HBM],
        out_specs=[VMEM] * (1 + CHAINS),
        out_shape=[pltpu.VMEM((row_count, tiles, SUBLANES, LANES), f32)]
        + [pltpu.VMEM(dump_shape(sizes), f32)] * CHAINS,
        scratch_shapes=[
            pltpu.VMEM((group_count, row_count, column_count * LANES), f32),
            pltpu.VMEM(lat_length.shape, f32),
            pltpu.SemaphoreType.DMA,
            pltpu.SemaphoreType.DMA((group_count,)),
        ],
        compiler_params=params(6),
        cost_estimate=cost(10, 10),
    )(index, *in_hbm(lat_length, field))


def deposit_kernel(sizes, index, decay, *rest):
    sub_count, group_count, row_count, column_count, chunk_count, strip = sizes
    here, away = arriving_layout(sub_count), leaving_layout(sub_count)
    arrived, swept = rest[: len(here)], rest[len(here) + CHAINS]
    rest = rest[len(here) + CHAINS + 1 :]
    leaving, totals = rest[: len(away)], rest[len(away) :][:CHAINS]
    got, exits, integers, words, word_sems = rest[len(away) + CHAINS :]
    tiles = group_count // SUBLANES
    word_row = chunk_count * group_count
    block_rows = got.shape[1]
    word_rows = block_rows - word_row
    sources = [(part, at) for part, members in zip(arrived, here) for at in range(len(members))]
    for source, (part, at) in enumerate(sources):
        block = part[at * block_rows : (at + 1) * block_rows, :]
        integers[source * word_rows : (source + 1) * word_rows, :] = block[word_row:].astype(i32)

    def hand_over(source):
        span = pl.ds(source * word_rows, word_rows)
        return pltpu.make_async_copy(integers.at[span], words.at[span], word_sems.at[source])

    for source in range(sub_count):
        hand_over(source).start()
    for source, (part, at) in enumerate(sources):
        got[source] = part[at * block_rows : (at + 1) * block_rows, :]
    lane = lax.broadcasted_iota(i32, (SUBLANES, LANES), 1)

    def one_source(source, carry):
        first = source * word_rows
        hand_over(source).wait()

        def more(chunk):
            last = jnp.minimum(chunk, chunk_count - 1)
            return (chunk < chunk_count) & (words[first + last, 0] < 8 * strip)

        def two_more(chunk):
            last = jnp.minimum(chunk + 1, chunk_count - 1)
            return (chunk + 1 < chunk_count) & (words[first + last, 0] < 8 * strip)

        def two_chunks(chunk):
            one_chunk(chunk)
            return one_chunk(chunk + 1)

        def one_chunk(chunk):
            blocks = [
                got[
                    source,
                    pl.ds(pl.multiple_of(chunk * group_count + tile * SUBLANES, 8), SUBLANES),
                    :,
                ]
                for tile in range(tiles)
            ]
            for slot in range(LANES):
                word = words[first + chunk, slot]
                target = pl.multiple_of(lax.shift_right_logical(word, 7), SUBLANES)
                turn = word & 127
                for tile in range(tiles):
                    value = pltpu.roll(jnp.where(lane == slot, blocks[tile], 0.0), turn, 1)
                    total = flat[slot % CHAINS]
                    at = pl.ds(target, SUBLANES)
                    total[tile, at, :] = total[tile, at, :] + value
            return chunk + 1

        done = lax.while_loop(two_more, two_chunks, jnp.int32(0))
        lax.while_loop(more, one_chunk, done)
        return carry

    flat = [total.reshape(tiles, -1, LANES) for total in totals]
    lax.fori_loop(0, sub_count, one_source, 0)
    for tile in range(tiles):
        groups = slice(tile * SUBLANES, (tile + 1) * SUBLANES)

        def sweep(sources, target, turn):
            def one_row(step, state):
                row = row_count - 1 - step if turn % 2 else step
                keep = decay[row, tile]
                take = 1.0 - keep
                following = []
                for column in range(column_count):
                    value = sources[0][tile, row, column]
                    for source in sources[1:]:
                        value = value + source[tile, row, column]
                    value = keep * state[column] + take * value
                    target[tile, row, column] = value
                    following.append(value)
                return tuple(following)

            nothing = tuple(jnp.zeros((SUBLANES, LANES), f32) for _ in range(column_count))
            state = lax.fori_loop(0, row_count, one_row, nothing, unroll=4)
            message_rows = 4 * column_count
            for column in range(column_count):
                at = tile * SUBLANES * message_rows + turn * column_count + column
                exits[pl.ds(at, SUBLANES, stride=message_rows), :] = state[column]

        for turn in range(4):
            sources = totals if turn == 0 else totals[turn % 2 : turn % 2 + 1]
            sweep(sources, totals[1 - turn % 2], turn)

        def turn_rows(at, carry):
            rows = pl.ds(pl.multiple_of(at * SUBLANES, SUBLANES), SUBLANES)
            for column in range(column_count):
                swept[column, groups, rows, :] = jnp.swapaxes(totals[0][tile, rows, column], 0, 1)
            return carry

        lax.fori_loop(0, row_count // SUBLANES, turn_rows, 0)
    rows = 4 * column_count
    for out, members in zip(leaving, away):
        for at, k in enumerate(members):
            first = pl.multiple_of((index[0] ^ k) * rows, SUBLANES)
            out[at * rows : (at + 1) * rows, :] = exits[pl.ds(first, rows), :]


def deposit_and_sweep(index, decay, totals, got, sizes):
    sub_count, group_count, row_count, column_count, chunk_count, strip = sizes
    here, away = arriving_layout(sub_count), leaving_layout(sub_count)
    rows = got[0].shape[0] // len(here[0])
    word_rows = rows - chunk_count * group_count
    exit_rows = 4 * column_count
    results = pl.pallas_call(
        functools.partial(deposit_kernel, sizes),
        out_shape=[pltpu.VMEM((column_count, group_count, row_count, LANES), f32)]
        + [pltpu.VMEM((len(members) * exit_rows, LANES), f32) for members in away]
        + [pltpu.VMEM(dump_shape(sizes), f32)] * CHAINS,
        in_specs=[SMEM] + [VMEM] * (1 + len(here) + CHAINS),
        out_specs=[VMEM] * (1 + len(away) + CHAINS),
        scratch_shapes=[
            pltpu.VMEM((sub_count, rows, LANES), f32),
            pltpu.VMEM(((group_count + 1) * exit_rows, LANES), f32),
            pltpu.VMEM((sub_count * word_rows, LANES), i32),
            pltpu.SMEM((sub_count * word_rows, LANES), i32),
            pltpu.SemaphoreType.DMA((sub_count,)),
        ],
        input_output_aliases={
            2 + len(here) + k: 1 + len(away) + k for k in range(CHAINS)
        },
        compiler_params=params(6),
        cost_estimate=cost(10, 10),
    )(index, *pinned(decay, *got, *totals))
    return results[: 1 + len(away)]


def unit_kernel(sizes, index, lat_length, inside, leaving, decay, held):
    sub_count, row_count = sizes
    group = index[0]
    decay[...] = jnp.zeros(decay.shape, f32)
    lengths = lat_length[group // 4, pl.ds(group % 4, 1), :]
    keep = jnp.exp(-1.0 / lengths)
    for sub in range(sub_count):
        part = keep[:, sub * row_count : (sub + 1) * row_count]
        decay[4 * sub : 4 * sub + 4, :row_count] = jnp.broadcast_to(part, (4, row_count))
    decay[...] = jnp.transpose(decay[...], (1, 0))
    held[...] = jnp.zeros(held.shape, f32)
    state_of = lax.broadcasted_iota(i32, (1, LANES), 1) & 3
    for turn in range(4):

        def one_row(step, state, turn=turn):
            row = row_count - 1 - step if turn % 2 else step
            keep = decay[pl.ds(row, 1), :]
            value = keep * state + (1.0 - keep) * held[pl.ds(row, 1), :]
            held[pl.ds(row, 1), :] = value
            return value

        enter = jnp.where(state_of == turn, 1.0, 0.0)
        state = lax.fori_loop(0, row_count, one_row, enter, unroll=8)
        leaving[turn : turn + 1, :] = state
    inside[...] = jnp.transpose(held[...], (1, 0))


def unit_responses(index, lat_length, sub_count, row_count):
    return pl.pallas_call(
        functools.partial(unit_kernel, (sub_count, row_count)),
        in_specs=[SMEM, VMEM],
        out_specs=[VMEM, VMEM],
        out_shape=[
            pltpu.VMEM((LANES, LANES), f32),
            jax.ShapeDtypeStruct((4, LANES), f32),
        ],
        scratch_shapes=[pltpu.VMEM((LANES, LANES), f32)] * 2,
        compiler_params=params(4),
        cost_estimate=cost(10, 10),
    )(index, lat_length)


def circle_weights(length, block_count, near_high, near_low, moment, spread):
    def ramp(shape, axis):
        return lax.broadcasted_iota(i32, shape, axis)

    def twice(x):
        return jnp.concatenate([x, x], axis=1)

    rate = -1.0 / jnp.full((1, LANES), length, f32)
    decay = jnp.exp(rate)
    gain = ((1.0 - decay) / (1.0 + decay)) ** 2
    centre = (1.0 + decay * decay) / (1.0 - decay * decay)
    turn = jnp.exp(rate * float(BLOCK * block_count))
    lag = float(BLOCK * block_count) * turn / (1.0 - turn)
    full_gain = gain / (1.0 - turn)

    shape = (BLOCK, BLOCK)
    gap = jnp.abs(ramp(shape, 0) - ramp(shape, 1)).astype(f32)
    near = twice(gain) * jnp.exp(twice(rate) * gap) * (gap + twice(centre))
    high, low = split(near)
    near_high[0] = high
    near_low[0] = low
    shape = (BLOCK, LANES)
    kind = ramp(shape, 1) & 3
    spot = ramp(shape, 0)
    far = jnp.where(kind < 2, BLOCK - spot, spot).astype(f32)
    sums = jnp.exp(rate * far) * jnp.where((kind & 1) == 1, far, 1.0)
    high, low = split(sums)
    moment[0, :, :LANES] = high
    moment[0, :, LANES:] = low
    shape = (32, BLOCK)
    kind = ramp(shape, 0) & 3
    block = lax.shift_right_logical(ramp(shape, 0), 2)
    spot = ramp(shape, 1)
    reach = jnp.where(kind < 2, spot, BLOCK - spot).astype(f32)
    for at in range(block_count):
        ahead = jnp.where(kind < 2, at - block, block - at) - 1
        steps = jnp.where(ahead < 0, ahead + block_count, ahead)
        full = reach + (steps * BLOCK).astype(f32)
        weight = twice(full_gain) * jnp.exp(twice(rate) * full)
        lead = full + twice(centre + lag)
        value = jnp.where((kind & 1) == 1, weight, weight * lead)
        value = jnp.where(block < block_count, value, 0.0)
        high, low = split(value)
        spread[0, :32, at * BLOCK : (at + 1) * BLOCK] = high
        spread[0, 32:, at * BLOCK : (at + 1) * BLOCK] = low


def weight_kernel(block_count, lon_length, *outs):
    group = pl.program_id(0)
    circle_weights(lon_length[group // 4, group % 4], block_count, *outs)


def weight_shapes(column_total):
    return [(BLOCK, BLOCK)] * 3 + [(64, column_total)]


def prepare(lon_length, column_total, space):
    group_count = lon_length.size
    shapes = weight_shapes(column_total)
    return pl.pallas_call(
        functools.partial(weight_kernel, column_total // BLOCK),
        grid=(group_count,),
        in_specs=[SMEM],
        out_specs=[pl.BlockSpec((1,) + shape, lambda i: (i, 0, 0)) for shape in shapes],
        out_shape=[space((group_count,) + shape, bf16) for shape in shapes],
        compiler_params=params(10),
        cost_estimate=cost(10, 10),
    )(lon_length)


def circle(pieces, near_high, near_low, moment, spread):
    row_count = pieces[0].shape[0]
    whole = jnp.concatenate(pieces, axis=0)
    high, low = split(whole)
    near = dot(high, near_high) + dot(low, near_high) + dot(high, near_low)
    sums = dot(high, moment)
    sums = sums[:, :LANES] + sums[:, LANES:] + dot(low, moment[:, :LANES])
    lane = lax.broadcasted_iota(i32, (row_count, LANES), 1)
    slot = lax.shift_right_logical(lane, 2) & 7
    moments = jnp.zeros((row_count, LANES), f32)
    for at in range(len(pieces)):
        part = sums[at * row_count : (at + 1) * row_count]
        moments = jnp.where(slot == at, part, moments)
    rest = moments - moments.astype(bf16).astype(f32)
    moments = jnp.where((lax.shift_right_logical(lane, 5) & 1) == 1, rest, moments).astype(bf16)
    spread = jnp.concatenate([spread[:32], spread[:32], spread[32:], spread[32:]], axis=0)
    far = dot(moments, spread)
    return [
        near[at * row_count : (at + 1) * row_count] + far[:, at * BLOCK : (at + 1) * BLOCK]
        for at in range(len(pieces))
    ]


def longitude_kernel(swept, near_high, near_low, moment, spread, out):
    column_count = swept.shape[0]
    pieces = [
        jnp.concatenate([swept[2 * at, 0], swept[2 * at + 1, 0]], axis=1)
        for at in range(column_count // 2)
    ]
    pieces = circle(pieces, near_high[0], near_low[0], moment[0], spread[0])
    for at, piece in enumerate(pieces):
        out[0, :, at * BLOCK : (at + 1) * BLOCK] = piece


def pair_kernel(variables, swept, near_high, near_low, moment, spread, table, own, sent, part):
    column_count = swept.shape[0]
    for place, variable in enumerate(variables):
        for level in range(2):
            group = level * 4 + variable
            pieces = [
                jnp.concatenate([swept[2 * at, group], swept[2 * at + 1, group]], axis=1)
                for at in range(column_count // 2)
            ]
            pieces = circle(
                pieces, near_high[group], near_low[group], moment[group], spread[group]
            )
            for target, first in ((sent, 0), (part, 2)):
                weight = table[variable, first + level : first + level + 1, :]
                weight = jnp.concatenate([weight, weight], axis=1)
                for at, piece in enumerate(pieces):
                    spot = slice(at * BLOCK, (at + 1) * BLOCK)
                    value = weight * piece
                    target[place, :, spot] = target[place, :, spot] + value if level else value
            for at, piece in enumerate(pieces):
                own[place, level, :, at * BLOCK : (at + 1) * BLOCK] = piece


def longitude_pair(variables, swept, weights, table):
    column_count, _, row_count, _ = swept.shape
    shape = (row_count, column_count * LANES)
    count = len(variables)
    return pl.pallas_call(
        functools.partial(pair_kernel, variables),
        in_specs=[VMEM] * 6,
        out_specs=[VMEM] * 3,
        out_shape=[
            pltpu.VMEM((count, 2) + shape, f32),
            pltpu.VMEM((count,) + shape, f32),
            pltpu.VMEM((count,) + shape, f32),
        ],
        compiler_params=params(10),
        cost_estimate=cost(10, 10),
    )(*pinned(swept, *weights, table))


def longitude(swept, weights, count, first, stride):
    column_count, _, row_count, _ = swept.shape
    column_total = column_count * LANES

    def of(i):
        return first + stride * i

    in_specs = [
        pl.BlockSpec((column_count, 1, row_count, LANES), lambda i: (0, of(i), 0, 0)),
        pl.BlockSpec((1, BLOCK, BLOCK), lambda i: (of(i), 0, 0)),
        pl.BlockSpec((1, BLOCK, BLOCK), lambda i: (of(i), 0, 0)),
        pl.BlockSpec((1, BLOCK, BLOCK), lambda i: (of(i), 0, 0)),
        pl.BlockSpec((1, 64, column_total), lambda i: (of(i), 0, 0)),
    ]
    out_specs = [pl.BlockSpec((1, row_count, column_total), lambda i: (i, 0, 0))]
    out_shape = [jax.ShapeDtypeStruct((count, row_count, column_total), f32)]
    operands = [swept, *weights]
    return pl.pallas_call(
        longitude_kernel,
        grid=(count,),
        in_specs=in_specs,
        out_specs=out_specs,
        out_shape=out_shape,
        compiler_params=params(14),
        cost_estimate=cost(10, 10),
    )(*operands)


def chain_kernel(sub_count, index, lon_length, leaving, inside, *rest):
    here, away = arriving_layout(sub_count), leaving_layout(sub_count)
    arrived, outs = rest[: len(here)], rest[len(here) :][: len(away)]
    exits, out, held, *weights = rest[len(here) + len(away) :]
    rows = exits.shape[1]
    for part, members in zip(arrived, here):
        for at, k in enumerate(members):
            exits[index[0] ^ k] = part[at * rows : (at + 1) * rows, :]
    column_count = exits.shape[1] // 4
    shape = (column_count, LANES)
    group = index[0]
    circle_weights(lon_length[group // 4, group % 4], column_count // 2, *weights)
    entering = {}
    for turn in range(4):
        order = list(range(sub_count))
        if turn % 2:
            order.reverse()
        state = jnp.zeros(shape, f32)
        for block in order:
            entering[turn, block] = state
            at = (turn * sub_count + block) * column_count
            held[at : at + column_count, :] = state
            state = exits[block, turn * column_count : (turn + 1) * column_count, :]
            for other in range(turn + 1):
                state = state + leaving[turn, block * 4 + other] * entering[other, block]
    pieces = []
    for at in range(column_count // 2):
        pair = [
            held[pl.ds(2 * at + k, 4 * sub_count, stride=column_count), :] for k in range(2)
        ]
        pieces.append(jnp.concatenate(pair, axis=1))
    pieces = circle(pieces, *[weight[0] for weight in weights])
    message_rows = rows + 8
    for at, piece in enumerate(pieces):
        for k in range(2):
            for turn in range(4):
                place = turn * column_count + 2 * at + k
                out[pl.ds(place, sub_count, stride=message_rows), :] = piece[
                    turn * sub_count : (turn + 1) * sub_count, k * LANES : (k + 1) * LANES
                ]
    for block in range(sub_count):
        at = block * message_rows + 4 * column_count
        out[at : at + 4, :] = inside[block * 4 : (block + 1) * 4, :]
        out[at + 4 : (block + 1) * message_rows, :] = jnp.zeros(
            (message_rows - 4 * column_count - 4, LANES), f32
        )
    for target, members in zip(outs, away):
        for place, k in enumerate(members):
            at = pl.multiple_of((index[0] ^ k) * message_rows, SUBLANES)
            to = place * message_rows
            target[to : to + message_rows, :] = out[pl.ds(at, message_rows), :]


def chain_states(sub_count, index, lon_length, exits, leaving, inside):
    here, away = arriving_layout(sub_count), leaving_layout(sub_count)
    rows = exits[0].shape[0] // len(here[0])
    column_total = rows // 4 * LANES
    message_rows = rows + 8
    return pl.pallas_call(
        functools.partial(chain_kernel, sub_count),
        in_specs=[SMEM, SMEM, SMEM, VMEM] + [VMEM] * len(here),
        out_specs=[VMEM] * len(away),
        scratch_shapes=[
            pltpu.VMEM((sub_count, rows, LANES), f32),
            pltpu.VMEM(((sub_count + 1) * message_rows, LANES), f32),
            pltpu.VMEM(((sub_count + 1) * rows, LANES), f32),
        ]
        + [pltpu.VMEM((1,) + shape, bf16) for shape in weight_shapes(column_total)],
        out_shape=[
            pltpu.VMEM((len(members) * message_rows, LANES), f32) for members in away
        ],
        compiler_params=params(16),
        cost_estimate=cost(10, 10),
    )(index, lon_length, leaving, *pinned(inside, *exits))


def gather_kernel(layout, index, *rest):
    *parts, out = rest
    rows = out.shape[0] // sum(len(members) for members in layout)
    for part, members in zip(parts, layout):
        for place, k in enumerate(members):
            at = pl.multiple_of((index[0] ^ k) * rows, SUBLANES)
            out[pl.ds(at, rows), :] = part[place * rows : (place + 1) * rows, :]


def gather_messages(layout, index, parts):
    return pl.pallas_call(
        functools.partial(gather_kernel, layout),
        in_specs=[SMEM] + [VMEM] * len(parts),
        out_specs=VMEM,
        out_shape=pltpu.VMEM((sum(part.shape[0] for part in parts), LANES), f32),
        compiler_params=params(4),
        cost_estimate=cost(10, 10),
    )(index, *pinned(*parts))


def pair_factors(top, low):
    top_take, low_take = 1.0 - top, 1.0 - low
    through = top * low
    sends = (low * top_take, low_take)
    low_out = (low_take * through, low, low_take * low * top_take, low_take * low_take)
    top_out = (
        top * low_out[0] + top_take * top,
        top * low_out[1],
        top * low_out[2] + top_take * top_take,
        top * low_out[3],
    )
    return through, sends, top_out, low_out


def tables_kernel(index, own, across_, beside_, corner_, table, mix, decay):
    band = index[0]
    for at, lengths in enumerate((own, across_, beside_, corner_)):
        for level in range(2):
            for variable in range(4):
                row = at * 8 + level * 4 + variable
                decay[row : row + 1, :] = jnp.full((1, LANES), lengths[level, variable], f32)
    decay[...] = jnp.exp(-1.0 / decay[...])

    def factors(at):
        return pair_factors(decay[at * 8 : at * 8 + 4, :], decay[at * 8 + 4 : at * 8 + 8, :])

    def by_band(*values):
        result = values[0]
        for at in range(1, 4):
            result = jnp.where(band == at, values[at], result)
        return result

    through, sends, top_out, low_out = factors(0)
    across, beside, corner = factors(1), factors(2), factors(3)
    through_n, echo_n = beside[0], beside[2][0]
    third = by_band(across[0], corner[0], across[0], across[0])
    third_echo = by_band(across[2][0], corner[2][0], across[2][0], across[2][0])
    fourth_echo = by_band(corner[2][0], across[2][0], corner[2][0], corner[2][0])
    zeta = third * third * fourth_echo + third_echo
    rows = []
    for i in range(2):
        reply = top_out[2 + i]
        rows.append(by_band(sends[i], reply + through * zeta * sends[i], sends[i], reply))
    for i in range(2):
        rows.append(
            by_band(
                sends[i], sends[i], through * echo_n * sends[i] + top_out[2 + i], sends[i]
            )
        )
    rows.append(through)
    for fin, back, *own in (top_out, low_out):
        for i in range(2):
            rows.append(
                by_band(
                    own[i] + back * (through_n * through_n * zeta + echo_n) * sends[i],
                    own[i] + back * zeta * sends[i],
                    own[i] + back * echo_n * sends[i],
                    own[i],
                )
            )
        none = jnp.zeros_like(fin)
        rows.append(by_band(back, fin + back * zeta * through, back, fin))
        rows.append(by_band(back * through_n, none, none, fin * through_n))
        rows.append(by_band(none, back, fin + back * echo_n * through, none))
    for variable in range(4):
        for at, row in enumerate(rows):
            table[variable, at : at + 1, :] = row[variable : variable + 1]
    row = lax.broadcasted_iota(i32, (SUBLANES, LANES), 0)
    for variable in range(4):
        value = jnp.zeros((SUBLANES, LANES), f32)
        downward, keeps = [], []
        for level in range(8):
            other = (level // 2) ^ band
            place = (other & 1) * 2 + lax.shift_right_logical(other, 1)
            at = place * 8 + (level % 2) * 4 + variable
            keep = jnp.broadcast_to(decay[pl.ds(at, 1), :], (SUBLANES, LANES))
            unit = jnp.where(row == place * 2 + level % 2, 1.0, 0.0)
            value = keep * value + (1.0 - keep) * unit
            downward.append(value)
            keeps.append(keep)
        value = jnp.zeros((SUBLANES, LANES), f32)
        upward = [None] * 8
        for level in reversed(range(8)):
            value = keeps[level] * value + (1.0 - keeps[level]) * downward[level]
            upward[level] = value
        for level in range(2):
            mix[level, variable] = by_band(*[upward[2 * at + level] for at in range(4)])


def tables(index, lengths):
    return pl.pallas_call(
        tables_kernel,
        in_specs=[SMEM] * 5,
        out_specs=[VMEM, VMEM],
        out_shape=[
            jax.ShapeDtypeStruct((4, 16, LANES), f32),
            jax.ShapeDtypeStruct((2, 4, SUBLANES, LANES), f32),
        ],
        scratch_shapes=[pltpu.VMEM((32, LANES), f32)],
        compiler_params=params(4),
        cost_estimate=cost(10, 10),
    )(index, *lengths)


def add_kernel(variables, part, near, table, total):
    for place, variable in enumerate(variables):
        weight = table[variable, 4:5, :]
        for column in range(part.shape[2] // LANES):
            at = slice(column * LANES, (column + 1) * LANES)
            total[place, :, at] = part[place, :, at] + weight * near[place, :, at]


def add_near(variables, part, near, table):
    return pl.pallas_call(
        functools.partial(add_kernel, variables),
        in_specs=[VMEM] * 3,
        out_specs=VMEM,
        out_shape=pltpu.VMEM(part.shape, f32),
        compiler_params=params(4),
        cost_estimate=cost(10, 10),
    )(*pinned(part, near, table))


def dense_kernel(variables, own, near, far, met, table, out):
    for place, variable in enumerate(variables):
        for level in range(2):
            weights = [table[variable, 5 + level * 5 + k : 6 + level * 5 + k, :] for k in range(5)]
            for column in range(near.shape[2] // LANES):
                at = slice(column * LANES, (column + 1) * LANES)
                value = weights[0] * own[place, 0, :, at] + weights[1] * own[place, 1, :, at]
                value = value + weights[2] * near[place, :, at] + weights[3] * far[place, :, at]
                out[place, level, :, at] = value + weights[4] * met[place, :, at]


def dense_part(variables, own, near, far, met, table):
    return pl.pallas_call(
        functools.partial(dense_kernel, variables),
        in_specs=[VMEM] * 5,
        out_specs=VMEM,
        out_shape=pltpu.VMEM(own.shape, f32),
        compiler_params=params(4),
        cost_estimate=cost(10, 10),
    )(*pinned(own, near, far, met, table))


def finish_kernel(mix, *rest):
    *dense, out, added, message, sems = rest
    messages, dense = dense[:4], dense[4:]
    _, _, row_count, column_total = dense[0].shape
    column_count = column_total // LANES
    stride = messages[0].shape[0] // SUBLANES
    copies = []
    for chunk, variables in enumerate(CHUNKS):
        for place, variable in enumerate(variables):
            for at, part in enumerate(messages):
                for level in range(2):
                    source = (level * 4 + variable) * stride
                    target = (2 * at + level) * stride
                    message[target : target + stride, :] = part[source : source + stride, :]
            lanes = []
            for column in range(column_count):
                lanes.append(
                    jnp.concatenate(
                        [
                            message[pl.ds(k * column_count + column, SUBLANES, stride=stride), :]
                            for k in range(4)
                        ],
                        axis=0,
                    )
                )
            high, low = split(jnp.concatenate(lanes, axis=1))
            states = jnp.concatenate([high, high, low, low], axis=0)
            inside = [
                message[pl.ds(4 * column_count + k, SUBLANES, stride=stride), :] for k in range(4)
            ]
            for level in range(2):
                mixed = jnp.concatenate([part * mix[level, variable] for part in inside], axis=0)
                high, low = split(mixed)
                mixed = jnp.concatenate([high, low, high, low], axis=0)
                total = dot(mixed, states, (((0,), (0,)), ((), ())))[:row_count]
                added[variable, level] = total + dense[chunk][place, level]
                copies.append(
                    pltpu.make_async_copy(
                        added.at[variable, level],
                        out.at[level, variable],
                        sems.at[2 * variable + level],
                    )
                )
                copies[-1].start()
    for copy in copies:
        copy.wait()


def finish(mix, messages, dense):
    _, _, row_count, column_total = dense[0].shape
    return pl.pallas_call(
        finish_kernel,
        in_specs=[VMEM] * (1 + len(messages) + len(dense)),
        out_specs=HBM,
        out_shape=pltpu.HBM((2, 4, row_count, column_total), f32),
        scratch_shapes=[
            pltpu.VMEM((4, 2, row_count, column_total), f32),
            pltpu.VMEM((messages[0].shape[0] * 9 // 8, LANES), f32),
            pltpu.SemaphoreType.DMA((8,)),
        ],
        compiler_params=params(12),
        cost_estimate=cost(10, 10),
    )(*pinned(mix, *messages, *dense))


CHUNKS = ((0, 1), (2, 3))
SWAP = [(0, 1), (1, 0), (2, 3), (3, 2)]
CROSS = [(0, 2), (2, 0), (1, 3), (3, 1)]
CORNER = [(0, 3), (3, 0), (1, 2), (2, 1)]
MIDDLE = [(0, 0), (1, 2), (2, 1), (3, 3)]


def four_bands(swept, weights, exits, units, chain, gather, table, mix):
    owns, parts, nears, mets = [], [], [], []

    def filter_some(at, *earlier):
        own, sent, part = longitude_pair(CHUNKS[at], after(swept, *earlier), weights, table)
        owns.append(own)
        parts.append(part)
        nears.append(lax.ppermute(sent, "band", SWAP))
        return part

    def cross_some(at, *earlier):
        part = after(parts[at], *earlier)
        total = add_near(CHUNKS[at], part, nears[at], table)
        mets.append(lax.ppermute(total, "band", MIDDLE))
        return total

    first = filter_some(0)
    response = units(first)

    def before_second_stage(came):
        return (cross_some(0, filter_some(1, came, *response)),)

    exits = exchange(exits, 8, before_second_stage)
    mark = cross_some(1, exits[0])
    messages = exchange(chain([after(exits[0], mark)] + exits[1:], response), 8)
    messages = gather(messages)
    across = lax.ppermute(messages, "band", CROSS)
    beside = lax.ppermute(messages, "band", SWAP)
    dense = []
    for at, variables in enumerate(CHUNKS):
        met = after(mets[at], messages)
        far = lax.ppermute(met, "band", SWAP)
        dense.append(dense_part(variables, owns[at], nears[at], far, met, table))
    corner = lax.ppermute(after(across, *dense), "band", SWAP)
    return finish(mix, (messages, across, beside, corner), dense)


def prefix(part, axis, combine, identity, reverse):
    count = lax.axis_size(axis)
    place = lax.axis_index(axis)
    ahead = count - 1 - place if reverse else place
    gathered = jax.tree.map(lambda a: lax.all_gather(a, axis), part)
    state = jax.tree.map(lambda a, e: jnp.zeros_like(a) + jnp.asarray(e, a.dtype), part, identity)

    def one(turn, state):
        source = count - 1 - turn if reverse else turn
        return combine(
            state, jax.tree.map(lambda a: lax.dynamic_index_in_dim(a, source, 0, False), gathered)
        )

    return lax.fori_loop(0, ahead, one, state)


def combine(earlier, later):
    return (earlier[0] * later[0], later[0] * earlier[1] + later[1])


def level_chain(values, decays, reverse):
    level_count = values.shape[0]
    visit_order = range(level_count - 1, -1, -1) if reverse else range(level_count)
    carry_state = jnp.zeros_like(values[0])
    level_gain = jnp.ones((values.shape[1],), f32)
    outputs = [None] * level_count
    carried = [None] * level_count
    for level_index in visit_order:
        factor = decays[level_index][:, None, None]
        carry_state = factor * carry_state + (1.0 - factor) * values[level_index]
        level_gain = level_gain * decays[level_index]
        outputs[level_index] = carry_state
        carried[level_index] = level_gain
    total_decay = level_gain[:, None, None]
    identity = (jnp.ones_like(total_decay), jnp.zeros_like(carry_state))
    incoming = prefix((total_decay, carry_state), "band", combine, identity, reverse)[1]
    return jnp.stack(
        [
            outputs[level_index] + carried[level_index][:, None, None] * incoming
            for level_index in range(level_count)
        ]
    )


def any_bands(swept, weights, exits, units, chain, gather, vert_length):
    column_count, group_count, row_count, _ = swept.shape
    sub_count = lax.axis_size("sub")
    chained = chain(exchange(exits, sub_count), units())
    messages = gather(exchange(chained, sub_count))
    (values,) = longitude(swept, weights, group_count, 0, 1)
    messages = messages.reshape(group_count, -1, LANES)
    states = messages[:, : 4 * column_count].reshape(group_count, 4, -1)
    inside = messages[:, 4 * column_count : 4 * column_count + 4, :row_count]
    values = values + jnp.einsum("gkr,gkc->grc", inside, states, precision=highest)
    decay = jnp.exp(-1.0 / vert_length)
    values = values.reshape(decay.shape + values.shape[1:])
    return level_chain(level_chain(values, decay, False), decay, True)


def per_device(background, obs_columns, obs_owner, obs_cell, lat_length, lon_length, vert_length):
    level_count, var_count, row_count, lon_count = background.shape
    sub_count = lax.axis_size("sub")
    group_count = level_count * var_count
    strip = row_count * lon_count
    column_count = lon_count // LANES
    capacity = 2 * obs_owner.shape[0] // sub_count
    chunk_count = capacity // LANES
    two_chips = lax.axis_size("band") == 4 and level_count == 2 and sub_count == 8
    index = lax.axis_index("sub").astype(i32).reshape(1)
    band = lax.axis_index("band").astype(i32).reshape(1)

    packed = pack_observations(
        after(index, band),
        obs_columns, obs_owner[:, 0], obs_cell, sub_count, strip, capacity
    )
    vert_lengths = []
    if two_chips:
        vert_length = after(vert_length, *packed)
        vert_lengths = [vert_length] + [
            lax.ppermute(vert_length, "band", pairs) for pairs in (CROSS, SWAP, CORNER)
        ]
    space = pltpu.VMEM if two_chips else pltpu.HBM
    weights = prepare(after(lon_length, *packed), lon_count, space)
    got = exchange(packed, sub_count, lambda came: (*vert_lengths, weights[0]))
    ready = list(weights)
    if two_chips:
        table, mix = tables(after(band, got[0]), vert_lengths)
        ready.append(table)

    sizes = (sub_count, group_count, row_count, column_count, chunk_count, strip)
    decay, *totals = make_ready(
        after(index, got[0]),
        lat_length,
        background.reshape(group_count, row_count, lon_count),
        sizes,
    )
    swept, *exits = deposit_and_sweep(
        index, decay, totals, [after(got[0], *ready)] + got[1:], sizes
    )

    def units(*earlier):
        start = after(index, swept, *earlier)
        return unit_responses(start, lat_length, sub_count, row_count)

    def chain(arrived, response):
        inside, leaving = response
        return chain_states(sub_count, index, lon_length, arrived, leaving, inside)

    def gather(parts):
        return gather_messages(arriving_layout(sub_count), index, parts)

    if two_chips:
        return four_bands(swept, weights, exits, units, chain, gather, table, mix)
    return any_bands(swept, weights, exits, units, chain, gather, vert_length)


def solution(mesh):
    placed = (
        P("band", None, "sub", None),
        P("band", None, "sub"),
        P("sub", None),
        P("sub"),
        P("band", None, None),
        P("band", None),
        P("band", None),
    )
    return jax.shard_map(
        per_device,
        mesh=mesh,
        in_specs=placed,
        out_specs=P("band", None, "sub", None),
        check_vma=False,
    )
```

```python
import functools

import jax
import jax.numpy as jnp
from jax import lax
from jax.experimental import pallas as pl
from jax.experimental.pallas import tpu as pltpu
from jax.sharding import PartitionSpec as P

f32 = jnp.float32
i32 = jnp.int32
bf16 = jnp.bfloat16
highest = lax.Precision.HIGHEST

LANES = 128
SUBLANES = 8
BLOCK = 256
CHAINS = 4

VMEM = pl.BlockSpec(memory_space=pltpu.VMEM)
SMEM = pl.BlockSpec(memory_space=pltpu.SMEM)
HBM = pl.BlockSpec(memory_space=pltpu.HBM)


def params(mib):
    return pltpu.CompilerParams(vmem_limit_bytes=mib << 20)


def pinned(*arrays):
    return [pltpu.with_memory_space_constraint(array, pltpu.VMEM) for array in arrays]


def in_hbm(*arrays):
    return [pltpu.with_memory_space_constraint(array, pltpu.HBM) for array in arrays]


EVEN_ODD = ((0, 2, 4, 6), (1, 3, 5, 7))
BY_PAIRS = ((0, 1), (2, 3), (4, 5), (6, 7))


def leaving_layout(sub_count):
    return EVEN_ODD if sub_count == 8 else tuple((k,) for k in range(sub_count))


def arriving_layout(sub_count):
    return BY_PAIRS if sub_count == 8 else tuple((k,) for k in range(sub_count))


def join_kernel(kept, came, *outs):
    rows = kept.shape[0] // len(outs)
    for at, out in enumerate(outs):
        out[:rows, :] = kept[at * rows : (at + 1) * rows, :]
        out[rows:, :] = came[at * rows : (at + 1) * rows, :]


def join_pairs(kept, came, count):
    rows = 2 * kept.shape[0] // count
    return pl.pallas_call(
        join_kernel,
        in_specs=[VMEM] * 2,
        out_specs=[VMEM] * count,
        out_shape=[pltpu.VMEM((rows, LANES), f32)] * count,
        compiler_params=params(4),
        cost_estimate=cost(10, 10),
    )(*pinned(kept, came))


def after(value, *earlier):
    return lax.optimization_barrier((value,) + earlier)[0]


def exchange(parts, sub_count, meanwhile=None):
    def move(part, k):
        return lax.ppermute(part, "sub", [(at, at ^ k) for at in range(sub_count)])

    if sub_count != 8:
        return [parts[0]] + [move(parts[k], k) for k in range(1, sub_count)]
    kept, sent = parts
    came = move(sent, 1)
    if meanwhile is not None:
        kept = after(kept, *meanwhile(came))
    pairs = join_pairs(kept, came, 4)
    return [pairs[0]] + [move(pairs[k], 2 * k) for k in (1, 2, 3)]


def cost(flops, read):
    return pl.CostEstimate(flops=flops, bytes_accessed=read, transcendentals=0)


def dot(a, b, dims=(((1,), (0,)), ((), ()))):
    return lax.dot_general(a, b, dims, preferred_element_type=f32)


def split(x):
    high = x.astype(bf16)
    return high, (x - high.astype(f32)).astype(bf16)


def pack_kernel(sizes, layout, index, owners, cells, values, *rest):
    outs, (packed, places, tally, sorted_, joined, counts, sem) = rest[:-7], rest[-7:]
    sub_count, group_count, chunk_count, strip = sizes
    block_count = owners.shape[0]
    tiles = group_count // SUBLANES
    lane = lax.broadcasted_iota(i32, (SUBLANES, LANES), 1)
    square = lambda axis: lax.broadcasted_iota(i32, (LANES, LANES), axis)
    owner = owners[...]
    picked = [jnp.where(owner == sub, 1.0, 0.0) for sub in range(sub_count)]
    upto = jnp.where(square(0) <= square(1), 1.0, 0.0).astype(bf16)
    ranks = dot(jnp.concatenate(picked, axis=0).astype(bf16), upto)
    wide = lax.broadcasted_iota(i32, (block_count, LANES), 1)
    place = jnp.zeros((block_count, LANES), f32)
    base = jnp.zeros((block_count, LANES), f32)
    totals = jnp.zeros((block_count, LANES), f32)
    for sub in range(sub_count):
        rank = ranks[sub * block_count : (sub + 1) * block_count]
        total = jnp.broadcast_to(rank[:, LANES - 1 :], rank.shape)
        place = jnp.where(owner == sub, rank - 1.0 + base, place)
        totals = jnp.where(wide == sub, total, totals)
        base = base + total
    places[...] = place.astype(i32)
    tally[...] = totals.astype(i32)
    copy = pltpu.make_async_copy(tally, counts, sem)
    copy.start()
    extra = -(group_count + SUBLANES) % 16
    row = square(0)

    def sort_block(block, carry):
        at = pl.multiple_of(block * LANES, LANES)
        parts = [
            *[values[level, :, pl.ds(at, LANES)] for level in range(values.shape[0])],
            jnp.broadcast_to(cells[pl.ds(block, 1), :], (SUBLANES, LANES)).astype(f32),
        ]
        if extra:
            parts.append(jnp.zeros((extra, LANES), f32))
        whole = jnp.concatenate(parts, axis=0)
        rows = whole.shape[0]
        high, rest = whole.astype(bf16), whole
        rest = rest - high.astype(f32)
        middle = rest.astype(bf16)
        low = (rest - middle.astype(f32)).astype(bf16)
        move = jnp.where(row == places[pl.ds(block, 1), :], 1.0, 0.0).astype(bf16)
        moved = dot(
            jnp.concatenate([high, middle, low], axis=0), move, (((1,), (1,)), ((), ()))
        )
        moved = moved[:rows] + moved[rows : 2 * rows] + moved[2 * rows :]
        for tile in range(tiles + 1):
            sorted_[block, tile] = moved[tile * SUBLANES : (tile + 1) * SUBLANES]
        return carry

    lax.fori_loop(0, block_count, sort_block, 0, unroll=16)
    copy.wait()

    def join_block(block, ends):
        start = jnp.int32(0)
        writes, following = [], []
        for sub in range(sub_count):
            end = ends[sub]
            chunk, offset = lax.shift_right_logical(end, 7), end & 127
            for tile in range(tiles + 1):
                turned = pltpu.roll(sorted_[block, tile], (end - start) & 127, 1)
                kept = jnp.where(lane >= offset, turned, joined[sub, chunk, tile])
                writes.append((sub, chunk, tile, kept, turned))
            start = start + counts[block, sub]
            following.append(end + counts[block, sub])
        for sub, chunk, tile, kept, turned in writes:
            joined[sub, chunk, tile] = kept
            joined[sub, chunk + 1, tile] = turned
        return tuple(following)

    ends = lax.fori_loop(0, block_count, join_block, (jnp.int32(0),) * sub_count, unroll=8)
    word_row = chunk_count * group_count
    word_rows = packed.shape[1] - word_row
    for sub in range(sub_count):
        packed[sub, word_row:, :] = jnp.full((word_rows, LANES), 8.0 * strip, f32)
        for chunk in range(chunk_count):
            for tile in range(tiles):
                at = chunk * group_count + tile * SUBLANES
                packed[sub, at : at + SUBLANES, :] = joined[sub, chunk, tile]
            filled = lane + chunk * LANES < ends[sub]
            cell = jnp.where(filled, joined[sub, chunk, tiles], 0.0).astype(i32)
            word = 8 * (cell - (cell & 127)) + ((cell - lane) & 127)
            word = jnp.where(filled, word, 8 * strip).astype(f32)
            packed[sub, word_row + chunk : word_row + chunk + 1, :] = word[:1]
    rows = packed.shape[1]
    for out, members in zip(outs, layout):
        for at, k in enumerate(members):
            out[at * rows : (at + 1) * rows, :] = packed[index[0] ^ k]


def pack_observations(index, obs_values, owners, cells, sub_count, strip, capacity):
    level_count, var_count, obs_count = obs_values.shape
    group_count = level_count * var_count
    chunk_count = capacity // LANES
    block_count = obs_count // LANES
    rows = chunk_count * group_count + SUBLANES * (-(-chunk_count // SUBLANES))
    tiles = group_count // SUBLANES
    layout = leaving_layout(sub_count)
    return pl.pallas_call(
        functools.partial(pack_kernel, (sub_count, group_count, chunk_count, strip), layout),
        out_shape=[pltpu.VMEM((len(members) * rows, LANES), f32) for members in layout],
        in_specs=[SMEM, VMEM, VMEM, VMEM],
        out_specs=[VMEM] * len(layout),
        scratch_shapes=[
            pltpu.VMEM((sub_count, rows, LANES), f32),
            pltpu.VMEM((block_count, LANES), i32),
            pltpu.VMEM((block_count, LANES), i32),
            pltpu.VMEM((block_count, tiles + 1, SUBLANES, LANES), f32),
            pltpu.VMEM((sub_count, chunk_count + 2, tiles + 1, SUBLANES, LANES), f32),
            pltpu.SMEM((block_count, LANES), i32),
            pltpu.SemaphoreType.DMA,
        ],
        compiler_params=params(6),
        cost_estimate=cost(10, 10),
    )(index, *in_hbm(owners.reshape(block_count, LANES), cells.reshape(block_count, LANES), obs_values))


def ready_kernel(sizes, index, lat_length, field, decay, *rest):
    sub_count, group_count, row_count, column_count, chunk_count, strip = sizes
    totals, (loaded, all_lengths, sem, sems) = rest[:CHAINS], rest[CHAINS:]
    tiles = group_count // SUBLANES

    def load(group):
        return pltpu.make_async_copy(field.at[group], loaded.at[group], sems.at[group])

    fetch = pltpu.make_async_copy(lat_length, all_lengths, sem)
    fetch.start()
    for group in range(group_count):
        load(group).start()

    def clear(row, carry):
        for total in totals[1:]:
            for tile in range(tiles):
                for column in range(column_count):
                    total[tile, row, column] = jnp.zeros((SUBLANES, LANES), f32)
        return carry

    lax.fori_loop(0, row_count, clear, 0)
    fetch.wait()
    shift = index[0] * row_count
    for tile in range(tiles):
        lengths = jnp.concatenate(
            [all_lengths[2 * tile + k] for k in range(SUBLANES // 4)], axis=0
        )
        lengths = pltpu.roll(lengths, jnp.where(shift > 0, lengths.shape[1] - shift, 0), 1)
        keep = jnp.exp(-1.0 / lengths[:, :LANES])
        for row in range(row_count):
            decay[row, tile] = jnp.broadcast_to(keep[:, row : row + 1], (SUBLANES, LANES))
    for group in range(group_count):
        load(group).wait()
    for tile in range(tiles):
        groups = slice(tile * SUBLANES, (tile + 1) * SUBLANES)

        def turn_rows(at, carry):
            rows = pl.ds(pl.multiple_of(at * SUBLANES, SUBLANES), SUBLANES)
            for column in range(column_count):
                lanes = slice(column * LANES, (column + 1) * LANES)
                totals[0][tile, rows, column] = jnp.swapaxes(loaded[groups, rows, lanes], 0, 1)
            return carry

        lax.fori_loop(0, row_count // SUBLANES, turn_rows, 0)


def dump_shape(sizes):
    _, group_count, row_count, column_count, _, _ = sizes
    return (group_count // SUBLANES, row_count + 1, column_count, SUBLANES, LANES)


def make_ready(index, lat_length, field, sizes):
    sub_count, group_count, row_count, column_count, chunk_count, strip = sizes
    tiles = group_count // SUBLANES
    return pl.pallas_call(
        functools.partial(ready_kernel, sizes),
        in_specs=[SMEM, HBM, HBM],
        out_specs=[VMEM] * (1 + CHAINS),
        out_shape=[pltpu.VMEM((row_count, tiles, SUBLANES, LANES), f32)]
        + [pltpu.VMEM(dump_shape(sizes), f32)] * CHAINS,
        scratch_shapes=[
            pltpu.VMEM((group_count, row_count, column_count * LANES), f32),
            pltpu.VMEM(lat_length.shape, f32),
            pltpu.SemaphoreType.DMA,
            pltpu.SemaphoreType.DMA((group_count,)),
        ],
        compiler_params=params(6),
        cost_estimate=cost(10, 10),
    )(index, *in_hbm(lat_length, field))


def deposit_kernel(sizes, index, decay, *rest):
    sub_count, group_count, row_count, column_count, chunk_count, strip = sizes
    here, away = arriving_layout(sub_count), leaving_layout(sub_count)
    arrived, swept = rest[: len(here)], rest[len(here) + CHAINS]
    rest = rest[len(here) + CHAINS + 1 :]
    leaving, totals = rest[: len(away)], rest[len(away) :][:CHAINS]
    got, exits, integers, words, word_sems = rest[len(away) + CHAINS :]
    tiles = group_count // SUBLANES
    word_row = chunk_count * group_count
    block_rows = got.shape[1]
    word_rows = block_rows - word_row
    sources = [(part, at) for part, members in zip(arrived, here) for at in range(len(members))]
    for source, (part, at) in enumerate(sources):
        block = part[at * block_rows : (at + 1) * block_rows, :]
        integers[source * word_rows : (source + 1) * word_rows, :] = block[word_row:].astype(i32)

    def hand_over(source):
        span = pl.ds(source * word_rows, word_rows)
        return pltpu.make_async_copy(integers.at[span], words.at[span], word_sems.at[source])

    for source in range(sub_count):
        hand_over(source).start()
    for source, (part, at) in enumerate(sources):
        got[source] = part[at * block_rows : (at + 1) * block_rows, :]
    lane = lax.broadcasted_iota(i32, (SUBLANES, LANES), 1)

    def one_source(source, carry):
        first = source * word_rows
        hand_over(source).wait()

        def more(chunk):
            last = jnp.minimum(chunk, chunk_count - 1)
            return (chunk < chunk_count) & (words[first + last, 0] < 8 * strip)

        def two_more(chunk):
            last = jnp.minimum(chunk + 1, chunk_count - 1)
            return (chunk + 1 < chunk_count) & (words[first + last, 0] < 8 * strip)

        def two_chunks(chunk):
            one_chunk(chunk)
            return one_chunk(chunk + 1)

        def one_chunk(chunk):
            blocks = [
                got[
                    source,
                    pl.ds(pl.multiple_of(chunk * group_count + tile * SUBLANES, 8), SUBLANES),
                    :,
                ]
                for tile in range(tiles)
            ]
            for slot in range(LANES):
                word = words[first + chunk, slot]
                target = pl.multiple_of(lax.shift_right_logical(word, 7), SUBLANES)
                turn = word & 127
                for tile in range(tiles):
                    value = pltpu.roll(jnp.where(lane == slot, blocks[tile], 0.0), turn, 1)
                    total = flat[slot % CHAINS]
                    at = pl.ds(target, SUBLANES)
                    total[tile, at, :] = total[tile, at, :] + value
            return chunk + 1

        done = lax.while_loop(two_more, two_chunks, jnp.int32(0))
        lax.while_loop(more, one_chunk, done)
        return carry

    flat = [total.reshape(tiles, -1, LANES) for total in totals]
    lax.fori_loop(0, sub_count, one_source, 0)
    for tile in range(tiles):
        groups = slice(tile * SUBLANES, (tile + 1) * SUBLANES)

        def sweep(sources, target, turn):
            def one_row(step, state):
                row = row_count - 1 - step if turn % 2 else step
                keep = decay[row, tile]
                take = 1.0 - keep
                following = []
                for column in range(column_count):
                    value = sources[0][tile, row, column]
                    for source in sources[1:]:
                        value = value + source[tile, row, column]
                    value = keep * state[column] + take * value
                    target[tile, row, column] = value
                    following.append(value)
                return tuple(following)

            nothing = tuple(jnp.zeros((SUBLANES, LANES), f32) for _ in range(column_count))
            state = lax.fori_loop(0, row_count, one_row, nothing, unroll=4)
            message_rows = 4 * column_count
            for column in range(column_count):
                at = tile * SUBLANES * message_rows + turn * column_count + column
                exits[pl.ds(at, SUBLANES, stride=message_rows), :] = state[column]

        for turn in range(4):
            sources = totals if turn == 0 else totals[turn % 2 : turn % 2 + 1]
            sweep(sources, totals[1 - turn % 2], turn)

        def turn_rows(at, carry):
            rows = pl.ds(pl.multiple_of(at * SUBLANES, SUBLANES), SUBLANES)
            for column in range(column_count):
                swept[column, groups, rows, :] = jnp.swapaxes(totals[0][tile, rows, column], 0, 1)
            return carry

        lax.fori_loop(0, row_count // SUBLANES, turn_rows, 0)
    rows = 4 * column_count
    for out, members in zip(leaving, away):
        for at, k in enumerate(members):
            first = pl.multiple_of((index[0] ^ k) * rows, SUBLANES)
            out[at * rows : (at + 1) * rows, :] = exits[pl.ds(first, rows), :]


def deposit_and_sweep(index, decay, totals, got, sizes):
    sub_count, group_count, row_count, column_count, chunk_count, strip = sizes
    here, away = arriving_layout(sub_count), leaving_layout(sub_count)
    rows = got[0].shape[0] // len(here[0])
    word_rows = rows - chunk_count * group_count
    exit_rows = 4 * column_count
    results = pl.pallas_call(
        functools.partial(deposit_kernel, sizes),
        out_shape=[pltpu.VMEM((column_count, group_count, row_count, LANES), f32)]
        + [pltpu.VMEM((len(members) * exit_rows, LANES), f32) for members in away]
        + [pltpu.VMEM(dump_shape(sizes), f32)] * CHAINS,
        in_specs=[SMEM] + [VMEM] * (1 + len(here) + CHAINS),
        out_specs=[VMEM] * (1 + len(away) + CHAINS),
        scratch_shapes=[
            pltpu.VMEM((sub_count, rows, LANES), f32),
            pltpu.VMEM(((group_count + 1) * exit_rows, LANES), f32),
            pltpu.VMEM((sub_count * word_rows, LANES), i32),
            pltpu.SMEM((sub_count * word_rows, LANES), i32),
            pltpu.SemaphoreType.DMA((sub_count,)),
        ],
        input_output_aliases={
            2 + len(here) + k: 1 + len(away) + k for k in range(CHAINS)
        },
        compiler_params=params(6),
        cost_estimate=cost(10, 10),
    )(index, *pinned(decay, *got, *totals))
    return results[: 1 + len(away)]


def unit_kernel(sizes, index, lat_length, inside, leaving, decay, held):
    sub_count, row_count = sizes
    group = index[0]
    decay[...] = jnp.zeros(decay.shape, f32)
    lengths = lat_length[group // 4, pl.ds(group % 4, 1), :]
    keep = jnp.exp(-1.0 / lengths)
    for sub in range(sub_count):
        part = keep[:, sub * row_count : (sub + 1) * row_count]
        decay[4 * sub : 4 * sub + 4, :row_count] = jnp.broadcast_to(part, (4, row_count))
    decay[...] = jnp.transpose(decay[...], (1, 0))
    held[...] = jnp.zeros(held.shape, f32)
    state_of = lax.broadcasted_iota(i32, (1, LANES), 1) & 3
    for turn in range(4):

        def one_row(step, state, turn=turn):
            row = row_count - 1 - step if turn % 2 else step
            keep = decay[pl.ds(row, 1), :]
            value = keep * state + (1.0 - keep) * held[pl.ds(row, 1), :]
            held[pl.ds(row, 1), :] = value
            return value

        enter = jnp.where(state_of == turn, 1.0, 0.0)
        state = lax.fori_loop(0, row_count, one_row, enter, unroll=8)
        leaving[turn : turn + 1, :] = state
    inside[...] = jnp.transpose(held[...], (1, 0))


def unit_responses(index, lat_length, sub_count, row_count):
    return pl.pallas_call(
        functools.partial(unit_kernel, (sub_count, row_count)),
        in_specs=[SMEM, VMEM],
        out_specs=[VMEM, VMEM],
        out_shape=[
            pltpu.VMEM((LANES, LANES), f32),
            jax.ShapeDtypeStruct((4, LANES), f32),
        ],
        scratch_shapes=[pltpu.VMEM((LANES, LANES), f32)] * 2,
        compiler_params=params(4),
        cost_estimate=cost(10, 10),
    )(index, lat_length)


def circle_weights(length, block_count, near_high, near_low, moment, spread):
    def ramp(shape, axis):
        return lax.broadcasted_iota(i32, shape, axis)

    def twice(x):
        return jnp.concatenate([x, x], axis=1)

    rate = -1.0 / jnp.full((1, LANES), length, f32)
    decay = jnp.exp(rate)
    gain = ((1.0 - decay) / (1.0 + decay)) ** 2
    centre = (1.0 + decay * decay) / (1.0 - decay * decay)
    turn = jnp.exp(rate * float(BLOCK * block_count))
    lag = float(BLOCK * block_count) * turn / (1.0 - turn)
    full_gain = gain / (1.0 - turn)

    shape = (BLOCK, BLOCK)
    gap = jnp.abs(ramp(shape, 0) - ramp(shape, 1)).astype(f32)
    near = twice(gain) * jnp.exp(twice(rate) * gap) * (gap + twice(centre))
    high, low = split(near)
    near_high[0] = high
    near_low[0] = low
    shape = (BLOCK, LANES)
    kind = ramp(shape, 1) & 3
    spot = ramp(shape, 0)
    far = jnp.where(kind < 2, BLOCK - spot, spot).astype(f32)
    sums = jnp.exp(rate * far) * jnp.where((kind & 1) == 1, far, 1.0)
    high, low = split(sums)
    moment[0, :, :LANES] = high
    moment[0, :, LANES:] = low
    shape = (32, BLOCK)
    kind = ramp(shape, 0) & 3
    block = lax.shift_right_logical(ramp(shape, 0), 2)
    spot = ramp(shape, 1)
    reach = jnp.where(kind < 2, spot, BLOCK - spot).astype(f32)
    for at in range(block_count):
        ahead = jnp.where(kind < 2, at - block, block - at) - 1
        steps = jnp.where(ahead < 0, ahead + block_count, ahead)
        full = reach + (steps * BLOCK).astype(f32)
        weight = twice(full_gain) * jnp.exp(twice(rate) * full)
        lead = full + twice(centre + lag)
        value = jnp.where((kind & 1) == 1, weight, weight * lead)
        value = jnp.where(block < block_count, value, 0.0)
        high, low = split(value)
        spread[0, :32, at * BLOCK : (at + 1) * BLOCK] = high
        spread[0, 32:, at * BLOCK : (at + 1) * BLOCK] = low


def weight_kernel(block_count, lon_length, *outs):
    group = pl.program_id(0)
    circle_weights(lon_length[group // 4, group % 4], block_count, *outs)


def weight_shapes(column_total):
    return [(BLOCK, BLOCK)] * 3 + [(64, column_total)]


def prepare(lon_length, column_total, space):
    group_count = lon_length.size
    shapes = weight_shapes(column_total)
    return pl.pallas_call(
        functools.partial(weight_kernel, column_total // BLOCK),
        grid=(group_count,),
        in_specs=[SMEM],
        out_specs=[pl.BlockSpec((1,) + shape, lambda i: (i, 0, 0)) for shape in shapes],
        out_shape=[space((group_count,) + shape, bf16) for shape in shapes],
        compiler_params=params(10),
        cost_estimate=cost(10, 10),
    )(lon_length)


def circle(pieces, near_high, near_low, moment, spread):
    row_count = pieces[0].shape[0]
    whole = jnp.concatenate(pieces, axis=0)
    high, low = split(whole)
    near = dot(high, near_high) + dot(low, near_high) + dot(high, near_low)
    sums = dot(high, moment)
    sums = sums[:, :LANES] + sums[:, LANES:] + dot(low, moment[:, :LANES])
    lane = lax.broadcasted_iota(i32, (row_count, LANES), 1)
    slot = lax.shift_right_logical(lane, 2) & 7
    moments = jnp.zeros((row_count, LANES), f32)
    for at in range(len(pieces)):
        part = sums[at * row_count : (at + 1) * row_count]
        moments = jnp.where(slot == at, part, moments)
    rest = moments - moments.astype(bf16).astype(f32)
    moments = jnp.where((lax.shift_right_logical(lane, 5) & 1) == 1, rest, moments).astype(bf16)
    spread = jnp.concatenate([spread[:32], spread[:32], spread[32:], spread[32:]], axis=0)
    far = dot(moments, spread)
    return [
        near[at * row_count : (at + 1) * row_count] + far[:, at * BLOCK : (at + 1) * BLOCK]
        for at in range(len(pieces))
    ]


def longitude_kernel(swept, near_high, near_low, moment, spread, out):
    column_count = swept.shape[0]
    pieces = [
        jnp.concatenate([swept[2 * at, 0], swept[2 * at + 1, 0]], axis=1)
        for at in range(column_count // 2)
    ]
    pieces = circle(pieces, near_high[0], near_low[0], moment[0], spread[0])
    for at, piece in enumerate(pieces):
        out[0, :, at * BLOCK : (at + 1) * BLOCK] = piece


def pair_kernel(variables, swept, near_high, near_low, moment, spread, table, own, sent, part):
    column_count = swept.shape[0]
    for place, variable in enumerate(variables):
        for level in range(2):
            group = level * 4 + variable
            pieces = [
                jnp.concatenate([swept[2 * at, group], swept[2 * at + 1, group]], axis=1)
                for at in range(column_count // 2)
            ]
            pieces = circle(
                pieces, near_high[group], near_low[group], moment[group], spread[group]
            )
            for target, first in ((sent, 0), (part, 2)):
                weight = table[variable, first + level : first + level + 1, :]
                weight = jnp.concatenate([weight, weight], axis=1)
                for at, piece in enumerate(pieces):
                    spot = slice(at * BLOCK, (at + 1) * BLOCK)
                    value = weight * piece
                    target[place, :, spot] = target[place, :, spot] + value if level else value
            for at, piece in enumerate(pieces):
                own[place, level, :, at * BLOCK : (at + 1) * BLOCK] = piece


def longitude_pair(variables, swept, weights, table):
    column_count, _, row_count, _ = swept.shape
    shape = (row_count, column_count * LANES)
    count = len(variables)
    return pl.pallas_call(
        functools.partial(pair_kernel, variables),
        in_specs=[VMEM] * 6,
        out_specs=[VMEM] * 3,
        out_shape=[
            pltpu.VMEM((count, 2) + shape, f32),
            pltpu.VMEM((count,) + shape, f32),
            pltpu.VMEM((count,) + shape, f32),
        ],
        compiler_params=params(10),
        cost_estimate=cost(10, 10),
    )(*pinned(swept, *weights, table))


def longitude(swept, weights, count, first, stride):
    column_count, _, row_count, _ = swept.shape
    column_total = column_count * LANES

    def of(i):
        return first + stride * i

    in_specs = [
        pl.BlockSpec((column_count, 1, row_count, LANES), lambda i: (0, of(i), 0, 0)),
        pl.BlockSpec((1, BLOCK, BLOCK), lambda i: (of(i), 0, 0)),
        pl.BlockSpec((1, BLOCK, BLOCK), lambda i: (of(i), 0, 0)),
        pl.BlockSpec((1, BLOCK, BLOCK), lambda i: (of(i), 0, 0)),
        pl.BlockSpec((1, 64, column_total), lambda i: (of(i), 0, 0)),
    ]
    out_specs = [pl.BlockSpec((1, row_count, column_total), lambda i: (i, 0, 0))]
    out_shape = [jax.ShapeDtypeStruct((count, row_count, column_total), f32)]
    operands = [swept, *weights]
    return pl.pallas_call(
        longitude_kernel,
        grid=(count,),
        in_specs=in_specs,
        out_specs=out_specs,
        out_shape=out_shape,
        compiler_params=params(14),
        cost_estimate=cost(10, 10),
    )(*operands)


def chain_kernel(sub_count, index, lon_length, leaving, inside, *rest):
    here, away = arriving_layout(sub_count), leaving_layout(sub_count)
    arrived, outs = rest[: len(here)], rest[len(here) :][: len(away)]
    exits, out, held, *weights = rest[len(here) + len(away) :]
    rows = exits.shape[1]
    for part, members in zip(arrived, here):
        for at, k in enumerate(members):
            exits[index[0] ^ k] = part[at * rows : (at + 1) * rows, :]
    column_count = exits.shape[1] // 4
    shape = (column_count, LANES)
    group = index[0]
    circle_weights(lon_length[group // 4, group % 4], column_count // 2, *weights)
    entering = {}
    for turn in range(4):
        order = list(range(sub_count))
        if turn % 2:
            order.reverse()
        state = jnp.zeros(shape, f32)
        for block in order:
            entering[turn, block] = state
            at = (turn * sub_count + block) * column_count
            held[at : at + column_count, :] = state
            state = exits[block, turn * column_count : (turn + 1) * column_count, :]
            for other in range(turn + 1):
                state = state + leaving[turn, block * 4 + other] * entering[other, block]
    pieces = []
    for at in range(column_count // 2):
        pair = [
            held[pl.ds(2 * at + k, 4 * sub_count, stride=column_count), :] for k in range(2)
        ]
        pieces.append(jnp.concatenate(pair, axis=1))
    pieces = circle(pieces, *[weight[0] for weight in weights])
    message_rows = rows + 8
    for at, piece in enumerate(pieces):
        for k in range(2):
            for turn in range(4):
                place = turn * column_count + 2 * at + k
                out[pl.ds(place, sub_count, stride=message_rows), :] = piece[
                    turn * sub_count : (turn + 1) * sub_count, k * LANES : (k + 1) * LANES
                ]
    for block in range(sub_count):
        at = block * message_rows + 4 * column_count
        out[at : at + 4, :] = inside[block * 4 : (block + 1) * 4, :]
        out[at + 4 : (block + 1) * message_rows, :] = jnp.zeros(
            (message_rows - 4 * column_count - 4, LANES), f32
        )
    for target, members in zip(outs, away):
        for place, k in enumerate(members):
            at = pl.multiple_of((index[0] ^ k) * message_rows, SUBLANES)
            to = place * message_rows
            target[to : to + message_rows, :] = out[pl.ds(at, message_rows), :]


def chain_states(sub_count, index, lon_length, exits, leaving, inside):
    here, away = arriving_layout(sub_count), leaving_layout(sub_count)
    rows = exits[0].shape[0] // len(here[0])
    column_total = rows // 4 * LANES
    message_rows = rows + 8
    return pl.pallas_call(
        functools.partial(chain_kernel, sub_count),
        in_specs=[SMEM, SMEM, SMEM, VMEM] + [VMEM] * len(here),
        out_specs=[VMEM] * len(away),
        scratch_shapes=[
            pltpu.VMEM((sub_count, rows, LANES), f32),
            pltpu.VMEM(((sub_count + 1) * message_rows, LANES), f32),
            pltpu.VMEM(((sub_count + 1) * rows, LANES), f32),
        ]
        + [pltpu.VMEM((1,) + shape, bf16) for shape in weight_shapes(column_total)],
        out_shape=[
            pltpu.VMEM((len(members) * message_rows, LANES), f32) for members in away
        ],
        compiler_params=params(16),
        cost_estimate=cost(10, 10),
    )(index, lon_length, leaving, *pinned(inside, *exits))


def gather_kernel(layout, index, *rest):
    *parts, out = rest
    rows = out.shape[0] // sum(len(members) for members in layout)
    for part, members in zip(parts, layout):
        for place, k in enumerate(members):
            at = pl.multiple_of((index[0] ^ k) * rows, SUBLANES)
            out[pl.ds(at, rows), :] = part[place * rows : (place + 1) * rows, :]


def gather_messages(layout, index, parts):
    return pl.pallas_call(
        functools.partial(gather_kernel, layout),
        in_specs=[SMEM] + [VMEM] * len(parts),
        out_specs=VMEM,
        out_shape=pltpu.VMEM((sum(part.shape[0] for part in parts), LANES), f32),
        compiler_params=params(4),
        cost_estimate=cost(10, 10),
    )(index, *pinned(*parts))


def pair_factors(top, low):
    top_take, low_take = 1.0 - top, 1.0 - low
    through = top * low
    sends = (low * top_take, low_take)
    low_out = (low_take * through, low, low_take * low * top_take, low_take * low_take)
    top_out = (
        top * low_out[0] + top_take * top,
        top * low_out[1],
        top * low_out[2] + top_take * top_take,
        top * low_out[3],
    )
    return through, sends, top_out, low_out


def tables_kernel(index, own, across_, beside_, corner_, table, mix, decay):
    band = index[0]
    for at, lengths in enumerate((own, across_, beside_, corner_)):
        for level in range(2):
            for variable in range(4):
                row = at * 8 + level * 4 + variable
                decay[row : row + 1, :] = jnp.full((1, LANES), lengths[level, variable], f32)
    decay[...] = jnp.exp(-1.0 / decay[...])

    def factors(at):
        return pair_factors(decay[at * 8 : at * 8 + 4, :], decay[at * 8 + 4 : at * 8 + 8, :])

    def by_band(*values):
        result = values[0]
        for at in range(1, 4):
            result = jnp.where(band == at, values[at], result)
        return result

    through, sends, top_out, low_out = factors(0)
    across, beside, corner = factors(1), factors(2), factors(3)
    through_n, echo_n = beside[0], beside[2][0]
    third = by_band(across[0], corner[0], across[0], across[0])
    third_echo = by_band(across[2][0], corner[2][0], across[2][0], across[2][0])
    fourth_echo = by_band(corner[2][0], across[2][0], corner[2][0], corner[2][0])
    zeta = third * third * fourth_echo + third_echo
    rows = []
    for i in range(2):
        reply = top_out[2 + i]
        rows.append(by_band(sends[i], reply + through * zeta * sends[i], sends[i], reply))
    for i in range(2):
        rows.append(
            by_band(
                sends[i], sends[i], through * echo_n * sends[i] + top_out[2 + i], sends[i]
            )
        )
    rows.append(through)
    for fin, back, *own in (top_out, low_out):
        for i in range(2):
            rows.append(
                by_band(
                    own[i] + back * (through_n * through_n * zeta + echo_n) * sends[i],
                    own[i] + back * zeta * sends[i],
                    own[i] + back * echo_n * sends[i],
                    own[i],
                )
            )
        none = jnp.zeros_like(fin)
        rows.append(by_band(back, fin + back * zeta * through, back, fin))
        rows.append(by_band(back * through_n, none, none, fin * through_n))
        rows.append(by_band(none, back, fin + back * echo_n * through, none))
    for variable in range(4):
        for at, row in enumerate(rows):
            table[variable, at : at + 1, :] = row[variable : variable + 1]
    row = lax.broadcasted_iota(i32, (SUBLANES, LANES), 0)
    for variable in range(4):
        value = jnp.zeros((SUBLANES, LANES), f32)
        downward, keeps = [], []
        for level in range(8):
            other = (level // 2) ^ band
            place = (other & 1) * 2 + lax.shift_right_logical(other, 1)
            at = place * 8 + (level % 2) * 4 + variable
            keep = jnp.broadcast_to(decay[pl.ds(at, 1), :], (SUBLANES, LANES))
            unit = jnp.where(row == place * 2 + level % 2, 1.0, 0.0)
            value = keep * value + (1.0 - keep) * unit
            downward.append(value)
            keeps.append(keep)
        value = jnp.zeros((SUBLANES, LANES), f32)
        upward = [None] * 8
        for level in reversed(range(8)):
            value = keeps[level] * value + (1.0 - keeps[level]) * downward[level]
            upward[level] = value
        for level in range(2):
            mix[level, variable] = by_band(*[upward[2 * at + level] for at in range(4)])


def tables(index, lengths):
    return pl.pallas_call(
        tables_kernel,
        in_specs=[SMEM] * 5,
        out_specs=[VMEM, VMEM],
        out_shape=[
            jax.ShapeDtypeStruct((4, 16, LANES), f32),
            jax.ShapeDtypeStruct((2, 4, SUBLANES, LANES), f32),
        ],
        scratch_shapes=[pltpu.VMEM((32, LANES), f32)],
        compiler_params=params(4),
        cost_estimate=cost(10, 10),
    )(index, *lengths)


def add_kernel(variables, part, near, table, total):
    for place, variable in enumerate(variables):
        weight = table[variable, 4:5, :]
        for column in range(part.shape[2] // LANES):
            at = slice(column * LANES, (column + 1) * LANES)
            total[place, :, at] = part[place, :, at] + weight * near[place, :, at]


def add_near(variables, part, near, table):
    return pl.pallas_call(
        functools.partial(add_kernel, variables),
        in_specs=[VMEM] * 3,
        out_specs=VMEM,
        out_shape=pltpu.VMEM(part.shape, f32),
        compiler_params=params(4),
        cost_estimate=cost(10, 10),
    )(*pinned(part, near, table))


def dense_kernel(variables, own, near, far, met, table, out):
    for place, variable in enumerate(variables):
        for level in range(2):
            weights = [table[variable, 5 + level * 5 + k : 6 + level * 5 + k, :] for k in range(5)]
            for column in range(near.shape[2] // LANES):
                at = slice(column * LANES, (column + 1) * LANES)
                value = weights[0] * own[place, 0, :, at] + weights[1] * own[place, 1, :, at]
                value = value + weights[2] * near[place, :, at] + weights[3] * far[place, :, at]
                out[place, level, :, at] = value + weights[4] * met[place, :, at]


def dense_part(variables, own, near, far, met, table):
    return pl.pallas_call(
        functools.partial(dense_kernel, variables),
        in_specs=[VMEM] * 5,
        out_specs=VMEM,
        out_shape=pltpu.VMEM(own.shape, f32),
        compiler_params=params(4),
        cost_estimate=cost(10, 10),
    )(*pinned(own, near, far, met, table))


def finish_kernel(mix, *rest):
    *dense, out, added, message, sems = rest
    messages, dense = dense[:4], dense[4:]
    _, _, row_count, column_total = dense[0].shape
    column_count = column_total // LANES
    stride = messages[0].shape[0] // SUBLANES
    copies = []
    for chunk, variables in enumerate(CHUNKS):
        for place, variable in enumerate(variables):
            for at, part in enumerate(messages):
                for level in range(2):
                    source = (level * 4 + variable) * stride
                    target = (2 * at + level) * stride
                    message[target : target + stride, :] = part[source : source + stride, :]
            lanes = []
            for column in range(column_count):
                lanes.append(
                    jnp.concatenate(
                        [
                            message[pl.ds(k * column_count + column, SUBLANES, stride=stride), :]
                            for k in range(4)
                        ],
                        axis=0,
                    )
                )
            high, low = split(jnp.concatenate(lanes, axis=1))
            states = jnp.concatenate([high, high, low, low], axis=0)
            inside = [
                message[pl.ds(4 * column_count + k, SUBLANES, stride=stride), :] for k in range(4)
            ]
            for level in range(2):
                mixed = jnp.concatenate([part * mix[level, variable] for part in inside], axis=0)
                high, low = split(mixed)
                mixed = jnp.concatenate([high, low, high, low], axis=0)
                total = dot(mixed, states, (((0,), (0,)), ((), ())))[:row_count]
                added[variable, level] = total + dense[chunk][place, level]
                copies.append(
                    pltpu.make_async_copy(
                        added.at[variable, level],
                        out.at[level, variable],
                        sems.at[2 * variable + level],
                    )
                )
                copies[-1].start()
    for copy in copies:
        copy.wait()


def finish(mix, messages, dense):
    _, _, row_count, column_total = dense[0].shape
    return pl.pallas_call(
        finish_kernel,
        in_specs=[VMEM] * (1 + len(messages) + len(dense)),
        out_specs=HBM,
        out_shape=pltpu.HBM((2, 4, row_count, column_total), f32),
        scratch_shapes=[
            pltpu.VMEM((4, 2, row_count, column_total), f32),
            pltpu.VMEM((messages[0].shape[0] * 9 // 8, LANES), f32),
            pltpu.SemaphoreType.DMA((8,)),
        ],
        compiler_params=params(12),
        cost_estimate=cost(10, 10),
    )(*pinned(mix, *messages, *dense))


CHUNKS = ((0, 1), (2, 3))
SWAP = [(0, 1), (1, 0), (2, 3), (3, 2)]
CROSS = [(0, 2), (2, 0), (1, 3), (3, 1)]
CORNER = [(0, 3), (3, 0), (1, 2), (2, 1)]
MIDDLE = [(0, 0), (1, 2), (2, 1), (3, 3)]


def four_bands(swept, weights, exits, response, chain, gather, table, mix):
    owns, parts, nears, mets = [], [], [], []

    def filter_some(at, *earlier):
        own, sent, part = longitude_pair(CHUNKS[at], after(swept, *earlier), weights, table)
        owns.append(own)
        parts.append(part)
        nears.append(lax.ppermute(sent, "band", SWAP))
        return part

    def cross_some(at, *earlier):
        part = after(parts[at], *earlier)
        total = add_near(CHUNKS[at], part, nears[at], table)
        mets.append(lax.ppermute(total, "band", MIDDLE))
        return total

    filter_some(0)

    def before_second_stage(came):
        return (cross_some(0, filter_some(1, came)),)

    exits = exchange(exits, 8, before_second_stage)
    mark = cross_some(1, exits[0])
    messages = exchange(chain([after(exits[0], mark)] + exits[1:], response), 8)
    messages = gather(messages)
    across = lax.ppermute(messages, "band", CROSS)
    beside = lax.ppermute(messages, "band", SWAP)
    dense = []
    for at, variables in enumerate(CHUNKS):
        met = after(mets[at], messages)
        far = lax.ppermute(met, "band", SWAP)
        dense.append(dense_part(variables, owns[at], nears[at], far, met, table))
    corner = lax.ppermute(after(across, *dense), "band", SWAP)
    return finish(mix, (messages, across, beside, corner), dense)


def prefix(part, axis, combine, identity, reverse):
    count = lax.axis_size(axis)
    place = lax.axis_index(axis)
    ahead = count - 1 - place if reverse else place
    gathered = jax.tree.map(lambda a: lax.all_gather(a, axis), part)
    state = jax.tree.map(lambda a, e: jnp.zeros_like(a) + jnp.asarray(e, a.dtype), part, identity)

    def one(turn, state):
        source = count - 1 - turn if reverse else turn
        return combine(
            state, jax.tree.map(lambda a: lax.dynamic_index_in_dim(a, source, 0, False), gathered)
        )

    return lax.fori_loop(0, ahead, one, state)


def combine(earlier, later):
    return (earlier[0] * later[0], later[0] * earlier[1] + later[1])


def level_chain(values, decays, reverse):
    level_count = values.shape[0]
    visit_order = range(level_count - 1, -1, -1) if reverse else range(level_count)
    carry_state = jnp.zeros_like(values[0])
    level_gain = jnp.ones((values.shape[1],), f32)
    outputs = [None] * level_count
    carried = [None] * level_count
    for level_index in visit_order:
        factor = decays[level_index][:, None, None]
        carry_state = factor * carry_state + (1.0 - factor) * values[level_index]
        level_gain = level_gain * decays[level_index]
        outputs[level_index] = carry_state
        carried[level_index] = level_gain
    total_decay = level_gain[:, None, None]
    identity = (jnp.ones_like(total_decay), jnp.zeros_like(carry_state))
    incoming = prefix((total_decay, carry_state), "band", combine, identity, reverse)[1]
    return jnp.stack(
        [
            outputs[level_index] + carried[level_index][:, None, None] * incoming
            for level_index in range(level_count)
        ]
    )


def any_bands(swept, weights, exits, response, chain, gather, vert_length):
    column_count, group_count, row_count, _ = swept.shape
    sub_count = lax.axis_size("sub")
    chained = chain(exchange(exits, sub_count), response)
    messages = gather(exchange(chained, sub_count))
    (values,) = longitude(swept, weights, group_count, 0, 1)
    messages = messages.reshape(group_count, -1, LANES)
    states = messages[:, : 4 * column_count].reshape(group_count, 4, -1)
    inside = messages[:, 4 * column_count : 4 * column_count + 4, :row_count]
    values = values + jnp.einsum("gkr,gkc->grc", inside, states, precision=highest)
    decay = jnp.exp(-1.0 / vert_length)
    values = values.reshape(decay.shape + values.shape[1:])
    return level_chain(level_chain(values, decay, False), decay, True)


def per_device(background, obs_columns, obs_owner, obs_cell, lat_length, lon_length, vert_length):
    level_count, var_count, row_count, lon_count = background.shape
    sub_count = lax.axis_size("sub")
    group_count = level_count * var_count
    strip = row_count * lon_count
    column_count = lon_count // LANES
    capacity = 2 * obs_owner.shape[0] // sub_count
    chunk_count = capacity // LANES
    two_chips = lax.axis_size("band") == 4 and level_count == 2 and sub_count == 8
    index = lax.axis_index("sub").astype(i32).reshape(1)
    band = lax.axis_index("band").astype(i32).reshape(1)

    packed = pack_observations(
        after(index, band),
        obs_columns, obs_owner[:, 0], obs_cell, sub_count, strip, capacity
    )
    vert_lengths = []
    if two_chips:
        vert_length = after(vert_length, *packed)
        vert_lengths = [vert_length] + [
            lax.ppermute(vert_length, "band", pairs) for pairs in (CROSS, SWAP, CORNER)
        ]
    space = pltpu.VMEM if two_chips else pltpu.HBM
    weights = prepare(after(lon_length, *packed), lon_count, space)
    got = exchange(packed, sub_count, lambda came: (*vert_lengths, weights[0]))
    ready = list(weights)
    if two_chips:
        table, mix = tables(after(band, got[0]), vert_lengths)
        ready.append(table)

    sizes = (sub_count, group_count, row_count, column_count, chunk_count, strip)
    response = unit_responses(after(index, got[0]), lat_length, sub_count, row_count)
    decay, *totals = make_ready(
        after(index, got[0]),
        lat_length,
        background.reshape(group_count, row_count, lon_count),
        sizes,
    )
    swept, *exits = deposit_and_sweep(
        index, decay, totals, [after(got[0], *ready, *response)] + got[1:], sizes
    )

    def chain(arrived, response):
        inside, leaving = response
        return chain_states(sub_count, index, lon_length, arrived, leaving, inside)

    def gather(parts):
        return gather_messages(arriving_layout(sub_count), index, parts)

    if two_chips:
        return four_bands(swept, weights, exits, response, chain, gather, table, mix)
    return any_bands(swept, weights, exits, response, chain, gather, vert_length)


def solution(mesh):
    placed = (
        P("band", None, "sub", None),
        P("band", None, "sub"),
        P("sub", None),
        P("sub"),
        P("band", None, None),
        P("band", None),
        P("band", None),
    )
    return jax.shard_map(
        per_device,
        mesh=mesh,
        in_specs=placed,
        out_specs=P("band", None, "sub", None),
        check_vma=False,
    )
```
